32 devices in a mesh: dp: 8 (over z, y), ffn: 4 (over x, core).
Axes of the slice: x: 2, y: 2, z: 4, core: 2. Of those that a mesh axis runs over, the one named last changes fastest.
Arguments:
- item_owner: int32 [8192, 2], P('dp'), may hold values from 0 to 31, all different within a row; in each aligned block of 1024 rows (0 to 1023, 1024 to 2047, ...) at most 128 rows name the same one
- item_row: int32 [8192, 2], P('dp'), may hold values from 0 to 783
- lengths: int32 [16], P('dp'), may hold values from 1 to 512, as said below
- log_count: int32 [25088], P(('dp', 'ffn')), may hold values from 0 to 4
- item_table: float32 [25088, 256], P(('dp', 'ffn'))
- table_mom: float32 [25088, 256], P(('dp', 'ffn')), may hold values from -0.00024414062 to 0.00024414062
- table_sec: float32 [25088, 256], P(('dp', 'ffn')), may hold values from 1.7028116e-10 to 2.7244986e-09
- qkv_weight: float32 [256, 768], replicated, may hold values from -0.375 to 0.375
- qkv_mom: float32 [256, 768], replicated, may hold values from -0.00024414062 to 0.00024414062
- qkv_sec: float32 [256, 768], replicated, may hold values from 1.7028116e-10 to 2.7244986e-09
- out_weight: float32 [256, 256], replicated, may hold values from -2 to 2
- out_mom: float32 [256, 256], replicated, may hold values from -0.00024414062 to 0.00024414062
- out_sec: float32 [256, 256], replicated, may hold values from 1.7028116e-10 to 2.7244986e-09
- ffn_in: float32 [256, 1024], P(None, 'ffn'), may hold values from -0.375 to 0.375
- ffn_in_mom: float32 [256, 1024], P(None, 'ffn'), may hold values from -0.00024414062 to 0.00024414062
- ffn_in_sec: float32 [256, 1024], P(None, 'ffn'), may hold values from 1.7028116e-10 to 2.7244986e-09
- ffn_back: float32 [1024, 256], P('ffn'), may hold values from -0.1875 to 0.1875
- ffn_back_mom: float32 [1024, 256], P('ffn'), may hold values from -0.00024414062 to 0.00024414062
- ffn_back_sec: float32 [1024, 256], P('ffn'), may hold values from 1.7028116e-10 to 2.7244986e-09
- norm_gains: float32 [3, 256], replicated, may hold values from 0.5 to 1.5
- gains_mom: float32 [3, 256], replicated, may hold values from -0.0009765625 to 0.0009765625
- gains_sec: float32 [3, 256], replicated, may hold values from 2.7244986e-09 to 4.3591978e-08
- positions: float32 [512, 256], replicated, may hold values from -1.5 to 1.5
- positions_mom: float32 [512, 256], replicated, may hold values from -0.00024414062 to 0.00024414062
- positions_sec: float32 [512, 256], replicated, may hold values from 1.7028116e-10 to 2.7244986e-09
Outputs:
- loss_parts: float32 [2], replicated
- stream_rms: float32 [3], replicated
- clip_norm: float32 [1], replicated
- new_table: float32 [25088, 256], P(('dp', 'ffn'))
- new_table_mom: float32 [25088, 256], P(('dp', 'ffn'))
- new_table_sec: float32 [25088, 256], P(('dp', 'ffn'))
- new_qkv: float32 [256, 768], replicated
- new_qkv_mom: float32 [256, 768], replicated
- new_qkv_sec: float32 [256, 768], replicated
- new_out: float32 [256, 256], replicated
- new_out_mom: float32 [256, 256], replicated
- new_out_sec: float32 [256, 256], replicated
- new_ffn_in: float32 [256, 1024], P(None, 'ffn')
- new_ffn_in_mom: float32 [256, 1024], P(None, 'ffn')
- new_ffn_in_sec: float32 [256, 1024], P(None, 'ffn')
- new_ffn_back: float32 [1024, 256], P('ffn')
- new_ffn_back_mom: float32 [1024, 256], P('ffn')
- new_ffn_back_sec: float32 [1024, 256], P('ffn')
- new_gains: float32 [3, 256], replicated
- new_gains_mom: float32 [3, 256], replicated
- new_gains_sec: float32 [3, 256], replicated
- new_positions: float32 [512, 256], replicated
- new_positions_mom: float32 [512, 256], replicated
- new_positions_sec: float32 [512, 256], replicated
The draws below stay inside these ranges and needn't reach their ends.
Inputs may be any that keep to these rules, and one draw needn't show every extreme that they name: `item_owner`: column 0 and column 1 of a slot name different owners. Within the rows of one device no owner is named more than 128 times over both columns, and on some device one owner is named exactly 128 times. An item's owner is device index dp * (devices of ffn) + ffn. `lengths`: A history's valid events are its first slots; some history is full.
All inputs are finite; a program needn't handle non-finite values.
Results may differ from the reference program's by a relative error of at most 0.012.
Values may be sent and summed in bfloat16 or wider, within the bound.
A program may use at most 128 MiB of HBM per device.

```python
import math
import jax
import jax.numpy as jnp
import numpy as np
from jax import lax

D = 256
H = 8
FF = 1024
LEN = 512
ROWS_DEV = 784
SEQ_DEV = 2
STEP = 5
HD = 32
TOK_DEV = 1024
HISTORIES = 16
TOKENS = 8192
VOCAB = 25088
MOST = 128
PARAMS = 7340800
DEVICES = 32


def draw_lengths(key, part):
    key = jax.random.fold_in(key, 11)
    places = jnp.arange(HISTORIES)
    owners = places // SEQ_DEV
    spread = max(HISTORIES // SEQ_DEV - 1, 1)
    base = LEN // 3 + (LEN - LEN // 3) * owners // spread
    jitter = jax.random.randint(key, (HISTORIES,), 0, LEN // 4 + 1)
    result = jnp.maximum(base - jitter, 1)
    return result.at[HISTORIES - 1].set(LEN).astype(jnp.int32)


def draw_item_table(key, part):
    key = jax.random.fold_in(key, 7)
    owners = jnp.arange(VOCAB) // ROWS_DEV
    ratio = owners.astype(jnp.float32) / max(VOCAB // ROWS_DEV - 1, 1)
    scale = (1.0 + 2.0 * ratio) * 0.0625
    noise = jax.random.normal(key, (VOCAB, D), jnp.float32)
    return noise * scale[:, None]


def place_ends(values, key, low, largest):
    place = [jax.random.randint(jax.random.fold_in(key, axis), (), 0, length) for axis, length in enumerate(values.shape)]
    widest = values.shape.index(max(values.shape))
    next_to = place[:widest] + [(place[widest] + 1) % values.shape[widest]] + place[widest + 1:]
    return values.at[tuple(place)].set(low).at[tuple(next_to)].set(largest)


def levels(stream_key, extent, cuts, least, largest):
    level, own = 1.0, jax.random.fold_in(stream_key, 6)
    for position, parts in cuts:
        draws = jnp.exp(jax.random.uniform(jax.random.fold_in(own, position), (parts,), jnp.float32, least / len(cuts), largest / len(cuts)))
        level = level * jnp.repeat(draws, extent[position] // parts).reshape([-1 if axis == position else 1 for axis in range(len(extent))])
    return level


def cumulative_ranks(number_of, lean):
    weights = [(1 << 20) // math.isqrt(rank ** lean) + 1 for rank in range(1, number_of + 1)]
    scale = 1 + sum(weights) // (1 << 30)
    return np.cumsum(np.array([max(1, weight // scale) for weight in weights]))


def ranked(own_key, extent, amount, lean):
    table = cumulative_ranks(amount, lean)
    ticket = jax.random.randint(jax.random.fold_in(own_key, 1), extent, 0, int(table[amount - 1]))
    grade = jnp.searchsorted(jnp.asarray(table, jnp.int32), ticket, side="right")
    return jax.random.permutation(jax.random.fold_in(own_key, 2), amount)[grade].astype(jnp.int32)


def assign_block(rng, own, number, rows, number_of, top, reach, skew):
    ranking = jax.random.permutation(rng, number_of)
    packed, ordinary = portions_of(number_of, rows * top, reach, skew, True), portions_of(number_of, rows * top, reach, skew, False)
    places = jnp.arange(number_of)

    def named(tallies, turn):
        used = int((tallies > 0).sum())
        fixed = max(1, used // 4)
        moved = fixed + (places - fixed + turn * (used - fixed)) % max(1, number_of - fixed)
        return jnp.zeros((number_of,), jnp.int32).at[ranking[jnp.where(places < fixed, places, moved)]].set(jnp.asarray(tallies, jnp.int32))

    tallies = jnp.where(number % 4 == 0, named(packed, number // 4), named(ordinary, number - number // 4 - 1))
    mixed = jax.random.permutation(jax.random.fold_in(own, 3), number_of)
    giver, receiver = mixed[0:number_of // 2 * 2:2], mixed[1:number_of // 2 * 2:2]
    room = jnp.minimum(tallies[giver] - 1, reach - tallies[receiver]) // 2
    room = jnp.where((giver == ranking[0]) | (receiver == ranking[0]) | (tallies[receiver] == 0), 0, jnp.maximum(room, 0))
    moved = jax.random.randint(jax.random.fold_in(own, 4), (number_of // 2,), 0, 1 << 20) % (room + 1)
    tallies = tallies.at[giver].add(-moved).at[receiver].add(moved)
    members = jnp.searchsorted(jnp.cumsum(tallies), jnp.arange(rows * top), side="right").astype(jnp.int32)
    listing = members.reshape(top, rows).T
    listing = listing[jax.random.permutation(jax.random.fold_in(own, 1), rows)]
    turn = jax.random.randint(jax.random.fold_in(own, 2), (rows, 1), 0, top)
    return jnp.take_along_axis(listing, (jnp.arange(top)[None, :] + turn) % top, axis=1)


def portions_of(count, total, bound, skew, full):
    portions = [(1 << 20) // math.isqrt(standing ** skew) + 1 for standing in range(1, count + 1)]
    largest = bound if full else min(bound, max(-(-total // count), total * portions[0] // sum(portions)))
    least = 1 if total - largest >= count - 1 else 0
    counts, spare = [largest] + [least] * (count - 1), total - largest - least * (count - 1)
    while spare > 0:
        movable = [i for i in range(1, count) if counts[i] < largest] or [i for i in range(1, count) if counts[i] < bound]
        pool, remaining = sum([portions[i] for i in movable]), spare
        for i in movable:
            extra = min(bound - counts[i], max(1, remaining * portions[i] // pool), spare)
            counts[i] = counts[i] + extra
            spare = spare - extra
    return np.array(counts)


def bell_draw(own_key, extent, scale, reach, split=(), held_as=jnp.bfloat16):
    level = levels(own_key, extent, split, -0.22, 0.18) if split else 1.0
    values = jax.random.normal(own_key, extent, jnp.float32) * scale * level
    return jnp.minimum(jnp.maximum(values, -reach), reach).astype(held_as)


def setup_inputs(seed: int = 0) -> dict:
    streams_of = jax.random.split(jax.random.key(seed), 26)
    item_owner_keys = jax.random.split(jax.random.fold_in(streams_of[0], 1), TOKENS // TOK_DEV)
    item_owner_turns = jax.random.permutation(jax.random.fold_in(streams_of[0], 3), TOKENS // TOK_DEV)
    item_owner = jax.vmap(lambda own, number: assign_block(jax.random.fold_in(streams_of[0], 2), own, number, TOK_DEV, DEVICES, 2, MOST, 1))(item_owner_keys, item_owner_turns).reshape((TOKENS, 2))
    item_row = place_ends(ranked(streams_of[1], (TOKENS, 2), ROWS_DEV, 2), jax.random.fold_in(streams_of[1], 3), 0, ROWS_DEV - 1).astype(jnp.int32)
    lengths = draw_lengths(jax.random.fold_in(streams_of[25], 71), 0)
    log_count = place_ends(jax.random.randint(streams_of[3], (VOCAB,), 0, 5), jax.random.fold_in(streams_of[3], 1), 0, 4).astype(jnp.int32)
    item_table = draw_item_table(jax.random.fold_in(streams_of[25], 71), 0)
    table_mom = bell_draw(streams_of[5], (VOCAB, D), (0.05 * PARAMS ** -0.5), 0.00024414062, ((0, 32),), jnp.float32)
    table_sec = jnp.clip(jnp.exp(math.log(2.7244986267049853e-09) - 2.7725887 * jax.random.uniform(streams_of[6], (VOCAB, D), jnp.float32) ** levels(streams_of[6], (VOCAB, D), ((0, 32),), -0.2, 0.2)), 1.7028116416906158e-10, 2.7244986267049853e-09)
    qkv_weight = bell_draw(streams_of[7], (D, 3 * D), D ** -0.5, 0.375, (), jnp.float32)
    qkv_mom = bell_draw(streams_of[8], (D, 3 * D), (0.05 * PARAMS ** -0.5), 0.00024414062, (), jnp.float32)
    qkv_sec = jnp.clip(jnp.exp(jax.random.uniform(streams_of[9], (D, 3 * D), jnp.float32, math.log(1.7028116416906158e-10), math.log(2.7244986267049853e-09))), 1.7028116416906158e-10, 2.7244986267049853e-09)
    out_weight = bell_draw(streams_of[10], (D, D), (max(1, 16 * D // LEN)) ** -0.5, 2.0, (), jnp.float32)
    out_mom = bell_draw(streams_of[11], (D, D), (0.05 * PARAMS ** -0.5), 0.00024414062, (), jnp.float32)
    out_sec = jnp.clip(jnp.exp(jax.random.uniform(streams_of[12], (D, D), jnp.float32, math.log(1.7028116416906158e-10), math.log(2.7244986267049853e-09))), 1.7028116416906158e-10, 2.7244986267049853e-09)
    ffn_in = bell_draw(streams_of[13], (D, FF), D ** -0.5, 0.375, ((1, 4),), jnp.float32)
    ffn_in_mom = bell_draw(streams_of[14], (D, FF), (0.05 * PARAMS ** -0.5), 0.00024414062, ((1, 4),), jnp.float32)
    ffn_in_sec = jnp.clip(jnp.exp(math.log(2.7244986267049853e-09) - 2.7725887 * jax.random.uniform(streams_of[15], (D, FF), jnp.float32) ** levels(streams_of[15], (D, FF), ((1, 4),), -0.2, 0.2)), 1.7028116416906158e-10, 2.7244986267049853e-09)
    ffn_back = bell_draw(streams_of[16], (FF, D), FF ** -0.5, 0.1875, ((0, 4),), jnp.float32)
    ffn_back_mom = bell_draw(streams_of[17], (FF, D), (0.05 * PARAMS ** -0.5), 0.00024414062, ((0, 4),), jnp.float32)
    ffn_back_sec = jnp.clip(jnp.exp(math.log(2.7244986267049853e-09) - 2.7725887 * jax.random.uniform(streams_of[18], (FF, D), jnp.float32) ** levels(streams_of[18], (FF, D), ((0, 4),), -0.2, 0.2)), 1.7028116416906158e-10, 2.7244986267049853e-09)
    norm_gains = jnp.clip(1.0 + 0.1 * jax.random.normal(streams_of[19], (3, D), jnp.float32), 0.5, 1.5)
    gains_mom = bell_draw(streams_of[20], (3, D), (0.2 * PARAMS ** -0.5), 0.0009765625, (), jnp.float32)
    gains_sec = jnp.clip(jnp.exp(jax.random.uniform(streams_of[21], (3, D), jnp.float32, math.log(2.7244986267049853e-09), math.log(4.3591978027279765e-08))), 2.7244986267049853e-09, 4.3591978027279765e-08)
    positions = bell_draw(streams_of[22], (LEN, D), 0.1, 1.5, (), jnp.float32)
    positions_mom = bell_draw(streams_of[23], (LEN, D), (0.05 * PARAMS ** -0.5), 0.00024414062, (), jnp.float32)
    positions_sec = jnp.clip(jnp.exp(jax.random.uniform(streams_of[24], (LEN, D), jnp.float32, math.log(1.7028116416906158e-10), math.log(2.7244986267049853e-09))), 1.7028116416906158e-10, 2.7244986267049853e-09)
    return {"item_owner": item_owner, "item_row": item_row, "lengths": lengths, "log_count": log_count, "item_table": item_table, "table_mom": table_mom, "table_sec": table_sec, "qkv_weight": qkv_weight, "qkv_mom": qkv_mom, "qkv_sec": qkv_sec, "out_weight": out_weight, "out_mom": out_mom, "out_sec": out_sec, "ffn_in": ffn_in, "ffn_in_mom": ffn_in_mom, "ffn_in_sec": ffn_in_sec, "ffn_back": ffn_back, "ffn_back_mom": ffn_back_mom, "ffn_back_sec": ffn_back_sec, "norm_gains": norm_gains, "gains_mom": gains_mom, "gains_sec": gains_sec, "positions": positions, "positions_mom": positions_mom, "positions_sec": positions_sec}


EPS = 1e-06
NEG = -1e+30
LEARN = 0.05
GAIN_LEARN = 0.4
BETA_ONE = 0.5
BETA_TWO = 0.5
DECAY = 0.01
ADAM_EPS = 1e-08
CLIP = 0.05
HIGH = lax.Precision.HIGHEST

@jax.custom_vjp
def low(v):
    return lax.optimization_barrier(v.astype(jnp.bfloat16)).astype(jnp.float32)

@jax.custom_vjp
def low_back(v):
    return v

def low_keep(v):
    return (low(v), None)

def low_pass(kept, grad):
    return (grad,)

def back_keep(v):
    return (v, None)

def back_low(kept, grad):
    return (low(grad),)
low.defvjp(low_keep, low_pass)
low_back.defvjp(back_keep, back_low)

def rms_norm(hidden, gain):
    return hidden * lax.rsqrt(lax.optimization_barrier(jnp.mean(hidden * hidden, -1, keepdims=True)) + EPS) * gain

def layer(weights, hidden0, lens):
    qkv_w, out_w, in_w, back_w, gains = weights
    seqs = hidden0.shape[0]
    normed1 = low(rms_norm(hidden0, gains[0]))
    united = low_back(low(jnp.matmul(normed1, low(qkv_w), precision=HIGH)))
    heads = united.reshape(seqs, LEN, 3, H, HD)
    queries = heads[:, :, 0]
    key_rows = heads[:, :, 1]
    values = heads[:, :, 2]
    scores = low_back(jnp.einsum('sqhd,skhd->shqk', queries, key_rows, precision=HIGH) * HD ** (-0.5))
    places = jnp.arange(LEN)
    causal = places[None, :] <= places[:, None]
    allowed = causal[None] & (places[None, None, :] < lens[:, None, None])
    scores = jnp.where(allowed[:, None], scores, NEG)
    probs = jax.nn.softmax(scores, -1)
    mixed = jnp.einsum('shqk,skhd->sqhd', low(probs), values, precision=HIGH).reshape(seqs, LEN, D)
    mixed = low_back(low(mixed))
    attn = low_back(jnp.matmul(mixed, low(out_w), precision=HIGH))
    hidden1 = hidden0 + attn
    normed2 = low(rms_norm(hidden1, gains[1]))
    pre_act = low_back(jnp.matmul(normed2, low(in_w), precision=HIGH))
    activated = low(jax.nn.gelu(pre_act, approximate=True))
    ffn = low_back(jnp.matmul(activated, low(back_w), precision=HIGH))
    hidden2 = hidden1 + ffn
    final = low(rms_norm(hidden2, gains[2]))
    return (final, hidden2, attn, ffn)

def forward(item_owner, item_row, lengths, log_count, table, qkv_w, out_w, in_w, back_w, gains, positions):
    ids = item_owner * ROWS_DEV + item_row
    rows = low_back(low(table[ids]))
    bias = log_count[ids[:, 1]].astype(jnp.float32)
    valid = (jnp.arange(LEN)[None, :] < lengths[:, None]).astype(jnp.float32).reshape(TOKENS)
    hidden0 = rows[:, 0].reshape(HISTORIES, LEN, D) + positions[None]
    groups = HISTORIES // SEQ_DEV
    weights = (qkv_w, out_w, in_w, back_w, gains)

    def group_step(pair):
        return layer(weights, pair[0], pair[1])
    final, hidden2, attn, ffn = lax.map(jax.checkpoint(group_step), (hidden0.reshape(groups, SEQ_DEV, LEN, D), lengths.reshape(groups, SEQ_DEV)))
    final = final.reshape(TOKENS, D)
    hidden2 = hidden2.reshape(TOKENS, D)
    attn = attn.reshape(TOKENS, D)
    ffn = ffn.reshape(TOKENS, D)
    cands = rows[:, 1]
    cand_bias = jnp.where(valid > 0, -bias, NEG)

    def block_total(final_blk):
        logits = low_back(jnp.dot(final_blk, cands.T, precision=HIGH)) + cand_bias[None, :]
        return jax.nn.logsumexp(logits, -1)
    totals = lax.map(jax.checkpoint(block_total), final.reshape(TOKENS // TOK_DEV, TOK_DEV, D)).reshape(TOKENS)
    positive = lax.optimization_barrier(jnp.sum(final * cands, -1)) - bias
    loss_sum = jnp.sum(valid * (totals - positive))
    squares = jnp.stack([jnp.sum(valid * lax.optimization_barrier(jnp.sum(hidden2 * hidden2, -1))), jnp.sum(valid * lax.optimization_barrier(jnp.sum(attn * attn, -1))), jnp.sum(valid * lax.optimization_barrier(jnp.sum(ffn * ffn, -1)))])
    return (loss_sum, (jnp.sum(valid), squares))

def adam(weight, moment, second, grad, factor, learn_rate):
    clipped = grad * factor
    new_mom = BETA_ONE * moment + (1.0 - BETA_ONE) * clipped
    new_sec = BETA_TWO * second + (1.0 - BETA_TWO) * clipped * clipped
    corr_one = 1.0 - BETA_ONE ** STEP
    corr_two = 1.0 - BETA_TWO ** STEP
    new_weight = weight - learn_rate * (new_mom / corr_one / (jnp.sqrt(new_sec / corr_two) + ADAM_EPS) + DECAY * weight)
    return (new_weight, new_mom, new_sec)

def reference(item_owner, item_row, lengths, log_count, item_table, table_mom, table_sec, qkv_weight, qkv_mom, qkv_sec, out_weight, out_mom, out_sec, ffn_in, ffn_in_mom, ffn_in_sec, ffn_back, ffn_back_mom, ffn_back_sec, norm_gains, gains_mom, gains_sec, positions, positions_mom, positions_sec):
    params = (item_table, qkv_weight, out_weight, ffn_in, ffn_back, norm_gains, positions)

    def objective(*weights):
        return forward(item_owner, item_row, lengths, log_count, *weights)
    loss_sum, pull, extras = jax.vjp(objective, *params, has_aux=True)
    count, squares = extras
    grads = pull(jnp.ones((), loss_sum.dtype))
    norm = jnp.sqrt(sum((jnp.sum(grad * grad) for grad in grads)))
    factor = CLIP / jnp.maximum(norm, CLIP)
    table_new = adam(item_table, table_mom, table_sec, grads[0], factor, LEARN)
    qkv_new = adam(qkv_weight, qkv_mom, qkv_sec, grads[1], factor, LEARN)
    out_new = adam(out_weight, out_mom, out_sec, grads[2], factor, LEARN)
    in_new = adam(ffn_in, ffn_in_mom, ffn_in_sec, grads[3], factor, LEARN)
    back_new = adam(ffn_back, ffn_back_mom, ffn_back_sec, grads[4], factor, LEARN)
    gains_new = adam(norm_gains, gains_mom, gains_sec, grads[5], factor, GAIN_LEARN)
    pos_new = adam(positions, positions_mom, positions_sec, grads[6], factor, LEARN)
    loss_parts = jnp.stack([loss_sum, count])
    stream_rms = jnp.sqrt(squares / (count * D))
    return (loss_parts, stream_rms, norm.reshape(1), table_new[0], table_new[1], table_new[2], qkv_new[0], qkv_new[1], qkv_new[2], out_new[0], out_new[1], out_new[2], in_new[0], in_new[1], in_new[2], back_new[0], back_new[1], back_new[2], gains_new[0], gains_new[1], gains_new[2], pos_new[0], pos_new[1], pos_new[2])
```

```python
import functools
import math

import jax
import jax.numpy as jnp
from jax import lax
from jax.experimental import pallas as pl
from jax.experimental.pallas import tpu as pltpu
from jax.sharding import PartitionSpec as P

MESH = pl.DeviceIdType.MESH
LIMIT = 60 * 1024 * 1024


def lowered(value):
    return value.astype(jnp.bfloat16)


def dot(left, right):
    return jnp.dot(left, right, preferred_element_type=jnp.float32)


def against(left, right):
    return lax.dot_general(
        left, right, (((1,), (1,)), ((), ())), preferred_element_type=jnp.float32
    )


def across(left, right):
    return lax.dot_general(
        left, right, (((0,), (0,)), ((), ())), preferred_element_type=jnp.float32
    )


def iota(shape, dim):
    return lax.broadcasted_iota(jnp.int32, shape, dim)


def each(first, last, body):
    if last - first <= 8:
        for k in range(first, last):
            body(k)
    else:

        def step(k, unused):
            body(k)
            return unused

        lax.fori_loop(first, last, step, 0)


class Peers:
    def __init__(self, n_dp):
        self.n_dp = n_dp
        self.d = lax.axis_index("dp")
        self.f = lax.axis_index("ffn")
        near = self.f + 1 - 2 * lax.rem(self.f, 2)
        far = lax.rem(self.f + 2, 4)
        self.member = (self.f, near, far, 3 - self.f)

    def ffn(self, s):
        return (self.d, self.member[s])

    def ahead(self, k):
        return (lax.rem(self.d + k, self.n_dp), self.f)

    def behind(self, k):
        return (lax.rem(self.d + self.n_dp - k, self.n_dp), self.f)

    def greet(self):
        barrier = pltpu.get_barrier_semaphore()
        for s in (1, 2, 3):
            pl.semaphore_signal(barrier, inc=1, device_id=self.ffn(s), device_id_type=MESH)

        def hello(k):
            pl.semaphore_signal(barrier, inc=1, device_id=self.ahead(k), device_id_type=MESH)

        each(1, self.n_dp, hello)
        pl.semaphore_wait(barrier, self.n_dp + 2)


class Wire:
    def __init__(self, send, recv):
        self.send, self.recv = send, recv

    def make(self, src, dst, number, where):
        return pltpu.make_async_remote_copy(
            src_ref=src,
            dst_ref=dst,
            send_sem=self.send.at[number],
            recv_sem=self.recv.at[number],
            device_id=where,
            device_id_type=MESH,
        )


def spread(row, lanes):
    return jnp.broadcast_to(row, (lanes, row.shape[1])).T


def one_hot_rows(row, width):
    column = spread(row, 128)
    lane = iota(column.shape, 1).astype(jnp.float32)
    return jnp.concatenate(
        [
            jnp.where(column == lane + float(128 * b), 1.0, 0.0).astype(jnp.bfloat16)
            for b in range(width // 128)
        ],
        1,
    )


def one_hot_columns(row, height):
    up = iota((height, row.shape[1]), 0).astype(jnp.float32)
    return jnp.where(up == row, 1.0, 0.0)


def lookup_kernel(
    n_dp,
    cap,
    owner_ref,
    row_ref,
    count_ref,
    table_ref,
    in_ref,
    back_ref,
    rows_out,
    bias_out,
    asked_out,
    key_out,
    weights_out,
    hot,
    slot_s,
    table_low,
    req,
    send_rows,
    send_bias,
    found,
    found_bias,
    part,
    part_bias,
    got,
    got_bias,
    ss,
    rs,
):
    here = Peers(n_dp)
    wire = Wire(ss, rs)
    d, f = here.d, here.f
    both = 2 * n_dp
    filled = n_dp * cap
    rows_dev = table_ref.shape[0]
    chunks, span = owner_ref.shape
    quads = chunks // 2
    here.greet()
    weights_out[0, 0] = lowered(in_ref[...])
    weights_out[0, 1] = lowered(back_ref[...])
    w_base = 0
    copies = []
    for s in (1, 2, 3):
        copy = wire.make(weights_out.at[0], weights_out.at[s], w_base + s, here.ffn(s))
        copies.append(copy)
    place = iota((both, span), 0)
    second = (place >= n_dp).astype(jnp.int32)
    ahead = place - second * n_dp + d
    ahead = jnp.where(ahead >= n_dp, ahead - n_dp, ahead)
    named = ahead * 4 + jnp.where(second > 0, here.member[1], f)
    for c in range(chunks):
        hot[c * both : (c + 1) * both, :] = jnp.where(
            owner_ref[c : c + 1, :] == named, 1.0, 0.0
        ).astype(jnp.bfloat16)
    before = jnp.where(iota((span, span), 0) < iota((span, span), 1), 1.0, 0.0)
    ranks = dot(hot[...], before.astype(jnp.bfloat16))
    carry = jnp.zeros((both, 1), jnp.float32)
    place_f = place.astype(jnp.float32)
    asking = jnp.zeros((both, 128), jnp.float32)
    for c in range(chunks):
        ones = hot[c * both : (c + 1) * both, :].astype(jnp.float32)
        slot = jnp.sum(ones * (ranks[c * both : (c + 1) * both, :] + carry), 0, keepdims=True)
        kind = jnp.sum(ones * place_f, 0, keepdims=True)
        present = jnp.sum(ones, 0, keepdims=True)
        carry = carry + jnp.sum(ones, 1, keepdims=True)
        slot_s[c : c + 1, :] = slot
        key_out[c : c + 1, :] = jnp.where(present > 0, kind * cap + slot, -1.0)
        row = row_ref[c : c + 1, :]
        high = (row >> 5).astype(jnp.float32)
        lower = (row & 31).astype(jnp.float32)
        mine = ones[:n_dp]
        spots = lowered(one_hot_columns(slot, 128))
        asking = asking + against(
            lowered(jnp.concatenate([mine * high, mine * lower], 0)), spots
        )
    wanted = (asking[:n_dp] * 32.0 + asking[n_dp:]).astype(jnp.int32)
    for k in range(n_dp):
        req[k, 0:1, :] = wanted[k : k + 1, :]
    q_base = 4

    def ask(k):
        return wire.make(req.at[k], asked_out.at[k], q_base + k, here.ahead(k))

    each(1, n_dp, lambda k: ask(k).start())
    asked_out[0] = req[0]
    for copy in copies:
        copy.start()
    table_low[0:rows_dev, :] = lowered(table_ref[...])
    padded = table_low.shape[0]
    if padded > rows_dev:
        table_low[rows_dev:padded, :] = jnp.zeros((padded - rows_dev, span), jnp.bfloat16)
    counts = lowered(jnp.broadcast_to(count_ref[...], (8, padded)))
    r_base = q_base + n_dp
    b_base = r_base + n_dp

    def at(k):
        return pl.ds(pl.multiple_of(k * cap, cap), cap)

    def reply(k):
        return (
            wire.make(send_rows.at[k], found.at[at(k)], r_base + k, here.behind(k)),
            wire.make(send_bias.at[k], found_bias.at[k], b_base + k, here.behind(k)),
        )

    def fetch(k):
        chosen = one_hot_rows(asked_out[k].astype(jnp.float32), padded)
        return (
            lowered(dot(chosen, table_low[...]))[:cap],
            against(counts, chosen),
        )

    rows, bias = fetch(0)
    found[0:cap, :] = rows
    found_bias[0] = bias

    def serve(k):
        ask(k).wait_recv()
        rows, bias = fetch(k)
        send_rows[k] = rows
        send_bias[k] = bias
        for copy in reply(k):
            copy.start()

    each(1, n_dp, serve)
    e_base = b_base + n_dp
    g_base = e_base + n_dp

    def pass_on(k):
        return (
            wire.make(
                found.at[at(k)],
                found.at[pl.ds(pl.multiple_of(filled + k * cap, cap), cap)],
                e_base + k,
                here.ffn(1),
            ),
            wire.make(found_bias.at[k], found_bias.at[n_dp + k], g_base + k, here.ffn(1)),
        )

    for copy in pass_on(0):
        copy.start()

    def relay(k):
        for copy in reply(k):
            copy.wait_recv()
        for copy in pass_on(k):
            copy.start()

    each(1, n_dp, relay)

    def arrive(k):
        for copy in pass_on(k):
            copy.wait_recv()

    each(0, n_dp, arrive)
    bias_rows = found_bias[:, 0, :].T

    def partial(quarter):
        rows = []
        for column in range(2):
            key = key_out[pl.ds(column * quads + quarter, 1), :]
            chosen = one_hot_rows(key, 2 * filled)
            rows.append(lowered(dot(chosen, found[...])))
        chunk = quads + quarter
        slot = slot_s[pl.ds(chunk, 1), :]
        ones = hot[pl.ds(pl.multiple_of(chunk * both, both), both), :]
        bias = jnp.sum(dot(lowered(bias_rows), ones) * one_hot_columns(slot, 128), 0, keepdims=True)
        return rows, jnp.broadcast_to(bias, (8, span))

    rows, bias = partial(here.member[2])
    x_base = g_base + n_dp
    part[0] = rows[0]
    part[1] = rows[1]
    part_bias[...] = bias
    give = wire.make(part, got, x_base, here.ffn(2))
    give_bias = wire.make(part_bias, got_bias, x_base + 1, here.ffn(2))
    give.start()
    give_bias.start()
    rows, bias = partial(f)
    give.wait_recv()
    give_bias.wait_recv()
    rows_out[0] = rows[0] + got[0]
    other = wire.make(rows_out.at[0], rows_out.at[1], x_base + 2, here.ffn(1))
    other.start()
    rows_out[2] = rows[1] + got[1]
    bias_out[...] = bias + got_bias[...]
    each(1, n_dp, lambda k: ask(k).wait_send())

    def sent(k):
        for copy in reply(k):
            copy.wait_send()

    each(1, n_dp, sent)

    def passed(k):
        for copy in pass_on(k):
            copy.wait_send()

    each(0, n_dp, passed)
    give.wait_send()
    give_bias.wait_send()
    for copy in copies:
        copy.wait()
    other.wait()


def lookup(n_dp, cap, item_owner, item_row, log_count, item_table, ffn_in, ffn_back):
    tokens = item_owner.shape[0]
    rows_dev, width = item_table.shape
    span = tokens // 4
    padded = -(-rows_dev // 128) * 128
    owner = item_owner.T.reshape(8, span)
    row = item_row.T.reshape(8, span)
    count = jnp.pad(log_count.astype(jnp.float32), (0, padded - rows_dev)).reshape(1, padded)
    low, full = jnp.bfloat16, jnp.float32
    vmem = pl.BlockSpec(memory_space=pltpu.VMEM)
    number = 4 + 5 * n_dp + 3
    return pl.pallas_call(
        functools.partial(lookup_kernel, n_dp, cap),
        out_shape=(
            jax.ShapeDtypeStruct((3, span, width), low),
            jax.ShapeDtypeStruct((8, span), full),
            jax.ShapeDtypeStruct((n_dp, 1, 128), jnp.int32),
            jax.ShapeDtypeStruct((8, span), full),
            jax.ShapeDtypeStruct((4, 2, width, width), low),
        ),
        in_specs=[vmem] * 6,
        out_specs=(vmem,) * 5,
        scratch_shapes=[
            pltpu.VMEM((16 * n_dp, span), low),
            pltpu.VMEM((8, span), full),
            pltpu.VMEM((padded, width), low),
            pltpu.VMEM((n_dp, 1, 128), jnp.int32),
            pltpu.VMEM((n_dp, cap, width), low),
            pltpu.VMEM((n_dp, 8, 128), full),
            pltpu.VMEM((2 * n_dp * cap, width), low),
            pltpu.VMEM((2 * n_dp, 8, 128), full),
            pltpu.VMEM((2, span, width), low),
            pltpu.VMEM((8, span), full),
            pltpu.VMEM((2, span, width), low),
            pltpu.VMEM((8, span), full),
            pltpu.SemaphoreType.DMA((number,)),
            pltpu.SemaphoreType.DMA((number,)),
        ],
        compiler_params=pltpu.CompilerParams(
            collective_id=0, has_side_effects=True, vmem_limit_bytes=LIMIT
        ),
        name="lookup",
    )(owner, row, count, item_table, ffn_in, ffn_back)


EPS = 1e-06
NEG = -1e30
HD = 32
ROOT = math.sqrt(2.0 / math.pi)


def factor_of(hidden):
    return lax.rsqrt(jnp.mean(hidden * hidden, -1, keepdims=True) + EPS)


def turned(block):
    return lowered(block.astype(jnp.float32).T)


def rms_back(hidden, gain, upstream):
    factor = factor_of(hidden)
    scaled = upstream * gain
    inner = jnp.mean(scaled * hidden, -1, keepdims=True)
    grad_hidden = factor * scaled - hidden * (factor * factor * factor * inner)
    return grad_hidden, jnp.sum(upstream * hidden * factor, 0, keepdims=True)


def loop(first, last, body):
    def step(k, unused):
        body(k)
        return unused

    lax.fori_loop(first, last, step, 0)


def layer_kernel(
    n_dp,
    rows_ref,
    bias_ref,
    lengths_ref,
    wq_ref,
    wo_ref,
    weights_ref,
    gains_ref,
    positions_ref,
    rowgrad_out,
    gq_out,
    go_out,
    gp_out,
    gf_out,
    sums_out,
    cands,
    cand_bias,
    cand_t,
    cand_col,
    cand_in,
    wq,
    wo,
    h0_s,
    n1_s,
    q_s,
    qt_s,
    k_s,
    v_s,
    kt_s,
    vt_s,
    mask_s,
    p_s,
    p16_s,
    ds16_s,
    stack_s,
    mixt_s,
    h1_s,
    h2_s,
    n2t_s,
    pre_s,
    act_s,
    fin_s,
    fint_s,
    acc_s,
    acc_send,
    acc_got,
    mid_send,
    mid_got,
    tot_s,
    own_s,
    dq_s,
    kv_s,
    kv_send,
    kv_got,
    ss,
    rs,
):
    here = Peers(n_dp)
    wire = Wire(ss, rs)
    f = here.f
    half = lax.rem(f, 2)
    span, width = h0_s.shape
    heads = width // HD
    scale = HD ** (-0.5)
    here.greet()
    length = lengths_ref[f // 2]
    begin = half * span
    lane = iota((1, span), 1)
    valid_lane = jnp.where(lane + begin < length, 1.0, 0.0)
    valid_col = jnp.where(iota((span, 1), 0) + begin < length, 1.0, 0.0)

    cands[0] = rows_ref[2]
    cand_bias[0] = jnp.where(lane + begin < length, -bias_ref[...], NEG)
    c_base, cb_base = 0, n_dp

    def offer(k):
        return (
            wire.make(cands.at[0], cands.at[k], c_base + k, here.ahead(k)),
            wire.make(cand_bias.at[0], cand_bias.at[k], cb_base + k, here.ahead(k)),
        )

    def start_offer(k):
        for copy in offer(k):
            copy.start()

    each(1, n_dp, start_offer)

    wq[...] = lowered(wq_ref[...])
    wo[...] = lowered(wo_ref[...])
    gain1, gain2, gain3 = gains_ref[0:1, :], gains_ref[1:2, :], gains_ref[2:3, :]
    start = pl.multiple_of(begin, span)
    hidden0 = rows_ref[0].astype(jnp.float32) + positions_ref[pl.ds(start, span), :]
    h0_s[...] = hidden0
    normed1 = lowered(hidden0 * factor_of(hidden0) * gain1)
    n1_s[...] = normed1
    q_s[...] = lowered(dot(normed1, wq[:, :width]))
    k_s[0:span, :] = lowered(dot(normed1, wq[:, width : 2 * width]))
    v_s[0:span, :] = lowered(dot(normed1, wq[:, 2 * width :]))
    start = pl.multiple_of(span - begin, span)
    hidden0 = rows_ref[1].astype(jnp.float32) + positions_ref[pl.ds(start, span), :]
    normed1 = lowered(hidden0 * factor_of(hidden0) * gain1)
    k_s[span:, :] = lowered(dot(normed1, wq[:, width : 2 * width]))
    v_s[span:, :] = lowered(dot(normed1, wq[:, 2 * width :]))
    qt_s[...] = turned(q_s[...])
    kt_s[...] = turned(k_s[...])
    vt_s[...] = turned(v_s[...])
    key_at = iota((2 * span, span), 0)
    key_at = jnp.where(key_at < span, key_at + begin, key_at - begin)
    allowed = (key_at <= iota((2 * span, span), 1) + begin) & (key_at < length)
    mask_s[...] = jnp.where(allowed, 0.0, NEG)
    row_head = iota((width, span), 0) // HD
    lane_head = iota((span, width), 1) // HD

    def forward_head(h):
        here_rows = pl.ds(pl.multiple_of(h * HD, HD), HD)
        mine = jnp.where(row_head == h, qt_s[...].astype(jnp.float32), 0.0)
        scores = dot(k_s[...], lowered(mine)) * scale + mask_s[...]
        expo = jnp.exp(scores - jnp.max(scores, 0, keepdims=True))
        probs = expo / jnp.sum(expo, 0, keepdims=True)
        p_s[h] = probs
        low_probs = lowered(probs)
        p16_s[:, pl.ds(pl.multiple_of(h * span, span), span)] = low_probs
        mixt_s[here_rows, :] = lowered(dot(vt_s[here_rows, :], low_probs))

    loop(0, heads, forward_head)
    attn = dot(turned(mixt_s[...]), wo[...])
    hidden1 = h0_s[...] + attn
    h1_s[...] = hidden1
    sum_attn = jnp.sum(valid_col * attn * attn, keepdims=True)
    normed2 = hidden1 * factor_of(hidden1) * gain2
    n2t_s[...] = turned(lowered(normed2))
    normed2 = lowered(normed2)
    for s in range(4):
        pre = dot(normed2, weights_ref[s, 0])
        pre_s[s] = pre
        active = lowered(0.5 * pre * (1.0 + jnp.tanh(ROOT * (pre + 0.044715 * pre * pre * pre))))
        act_s[:, s * span : (s + 1) * span] = active
    branch = dot(act_s[...], jnp.concatenate([weights_ref[s, 1] for s in range(4)], 0))
    hidden2 = h1_s[...] + branch
    h2_s[...] = hidden2
    sum_ffn = jnp.sum(valid_col * branch * branch, keepdims=True)
    sum_hid = jnp.sum(valid_col * hidden2 * hidden2, keepdims=True)
    final = lowered(hidden2 * factor_of(hidden2) * gain3)
    fin_s[0:span, :] = final
    f_base = cb_base + n_dp
    fin = [fin_s.at[pl.ds(s * span, span)] for s in range(4)]
    near = wire.make(fin[0], fin[1], f_base, here.ffn(1))
    far = wire.make(fin[0], fin[2], f_base + 1, here.ffn(2))
    relayed = wire.make(fin[2], fin[3], f_base + 2, here.ffn(1))
    far.start()
    near.start()
    fint_s[:, 0:span] = turned(final)

    def prepare(k):
        cand_t[k] = turned(cands[k])
        cand_col[k] = spread(cand_bias[k, 0:1, :], 128)

    prepare(0)

    def prepare_other(k):
        for copy in offer(k):
            copy.wait_recv()
        prepare(k)

    loop(1, n_dp, prepare_other)
    near.wait_recv()
    fint_s[:, span : 2 * span] = turned(fin_s[span : 2 * span, :])
    acc_s[...] = jnp.zeros_like(acc_s)

    def totals(pair):
        lanes = slice(pair * 2 * span, (pair + 1) * 2 * span)

        def step(b, carry):
            top, total = carry
            column = jnp.concatenate([cand_col[b]] * (2 * span // 128), 1)
            logits = dot(cands[b], fint_s[:, lanes]) + column
            higher = jnp.maximum(top, jnp.max(logits, 0, keepdims=True))
            shrink = jnp.exp(top - higher)
            expo = jnp.exp(logits - higher)
            total = total * shrink + jnp.sum(expo, 0, keepdims=True)
            acc_s[:, lanes] = acc_s[:, lanes] * shrink + dot(cand_t[b], lowered(expo))
            return higher, total

        first = jnp.full((1, 2 * span), NEG, jnp.float32)
        return lax.fori_loop(0, n_dp, step, (first, jnp.zeros((1, 2 * span), jnp.float32)))

    top01, total01 = totals(0)
    far.wait_recv()
    relayed.start()
    fint_s[:, 2 * span : 3 * span] = turned(fin_s[2 * span : 3 * span, :])
    relayed.wait_recv()
    fint_s[:, 3 * span :] = turned(fin_s[3 * span :, :])
    top23, total23 = totals(1)
    stat_row = iota((8, span), 0)

    def packed(top, total):
        return jnp.where(stat_row == 0, top, total)

    acc_send[0] = lowered(acc_s[:, span : 2 * span])
    acc_send[1] = lowered(acc_s[:, 3 * span :])
    mid_send[0] = packed(top01[:, span:], total01[:, span:])
    mid_send[1] = packed(top23[:, span:], total23[:, span:])
    g_base = f_base + 3
    give = wire.make(acc_send.at[pl.ds(0, 2)], acc_got.at[pl.ds(0, 2)], g_base, here.ffn(1))
    give_mid = wire.make(
        mid_send.at[pl.ds(0, 2)], mid_got.at[pl.ds(0, 2)], g_base + 1, here.ffn(1)
    )
    give.start()
    give_mid.start()
    give.wait_recv()
    give_mid.wait_recv()

    def merged(acc, top, total, other, stats):
        other_top, other_total = stats[0:1, :], stats[1:2, :]
        higher = jnp.maximum(top, other_top)
        left, right = jnp.exp(top - higher), jnp.exp(other_top - higher)
        return (
            acc * left + other.astype(jnp.float32) * right,
            higher,
            total * left + other_total * right,
        )

    acc, top, total = merged(
        acc_s[:, 2 * span : 3 * span], top23[:, :span], total23[:, :span], acc_got[1], mid_got[1]
    )
    acc_send[2] = lowered(acc)
    mid_send[2] = packed(top, total)
    give2 = wire.make(acc_send.at[2], acc_got.at[2], g_base + 2, here.ffn(2))
    give2_mid = wire.make(mid_send.at[2], mid_got.at[2], g_base + 3, here.ffn(2))
    give2.start()
    give2_mid.start()
    acc, top, total = merged(
        acc_s[:, :span], top01[:, :span], total01[:, :span], acc_got[0], mid_got[0]
    )
    give2.wait_recv()
    give2_mid.wait_recv()
    acc, top, total = merged(acc, top, total, acc_got[2], mid_got[2])
    log_total = top + jnp.log(total)
    tot_s[0] = jnp.broadcast_to(jnp.where(valid_lane > 0, log_total, -NEG), (8, span))
    t_base = g_base + 4
    tell = [wire.make(tot_s.at[0], tot_s.at[s], t_base + s, here.ffn(s)) for s in (1, 2, 3)]
    for copy in tell:
        copy.start()
    target_t = cand_t[0].astype(jnp.float32)
    positive = (
        jnp.sum(fint_s[:, :span].astype(jnp.float32) * target_t, 0, keepdims=True)
        - bias_ref[0:1, :]
    )
    loss = jnp.sum(valid_lane * (log_total - positive), keepdims=True)
    grad_final = ((acc / total - target_t) * valid_lane).T

    grad_h2, gain_grad3 = rms_back(h2_s[...], gain3, grad_final)
    up = lowered(grad_h2)
    h2_s[...] = grad_h2
    for s in range(4):
        gf_out[s, 1] = across(act_s[:, s * span : (s + 1) * span], up)
        grad_act = against(up, weights_ref[s, 1])
        pre = pre_s[s]
        inner = jnp.tanh(ROOT * (pre + 0.044715 * pre * pre * pre))
        slope = 0.5 * (1.0 + inner) + 0.5 * pre * (1.0 - inner * inner) * (
            ROOT * (1.0 + 3.0 * 0.044715 * pre * pre)
        )
        grad_pre = lowered(grad_act * slope)
        gf_out[s, 0] = dot(n2t_s[...], grad_pre)
        act_s[:, s * span : (s + 1) * span] = grad_pre
    grad_normed2 = against(
        act_s[...], jnp.concatenate([weights_ref[s, 0] for s in range(4)], 1)
    )
    grad_h1_norm, gain_grad2 = rms_back(h1_s[...], gain2, grad_normed2)
    h1_s[...] = h2_s[...] + grad_h1_norm

    for copy in tell:
        copy.wait_recv()
    d_base = t_base + 4

    def hand_back(k):
        return wire.make(cand_t.at[k], cand_in.at[k], d_base + k, here.behind(k))

    def cand_grad(b):
        column = jnp.concatenate([cand_col[b]] * (4 * span // 128), 1)
        level = jnp.concatenate([tot_s[s, 0:1, :] for s in range(4)], 1)
        logits = dot(cands[b], fint_s[...]) + column
        return dot(lowered(jnp.exp(logits - level)), fin_s[...])

    def cand_step(b):
        cand_t[b] = lowered(cand_grad(b))
        hand_back(b).start()

    loop(1, n_dp, cand_step)
    own_s[...] = cand_grad(0)

    grad_h1 = h1_s[...]
    attn_up = lowered(grad_h1)
    go_out[...] = dot(mixt_s[...], attn_up)
    grad_mixed = lowered(against(attn_up, wo[...]))
    grad_mixed_f = grad_mixed.astype(jnp.float32)
    mixt_s[...] = turned(grad_mixed)
    for h in range(heads):
        stack_s[h * span : (h + 1) * span, :] = lowered(
            jnp.where(lane_head == h, grad_mixed_f, 0.0)
        )
    kv_s[...] = dot(p16_s[...], stack_s[...])

    def backward_head(h):
        here_rows = pl.ds(pl.multiple_of(h * HD, HD), HD)
        mine = jnp.where(row_head == h, mixt_s[...].astype(jnp.float32), 0.0)
        grad_probs = dot(v_s[...], lowered(mine))
        probs = p_s[h]
        inner = jnp.sum(probs * grad_probs, 0, keepdims=True)
        grad_scores = lowered(probs * (grad_probs - inner))
        ds16_s[:, pl.ds(pl.multiple_of(h * span, span), span)] = grad_scores
        dq_s[here_rows, :] = dot(kt_s[here_rows, :], grad_scores) * scale

    loop(0, heads, backward_head)
    queries = q_s[...].astype(jnp.float32)
    kv_send[1] = kv_s[span:, :]
    own_v = kv_s[0:span, :]
    for h in range(heads):
        stack_s[h * span : (h + 1) * span, :] = lowered(jnp.where(lane_head == h, queries, 0.0))
    kv_s[...] = dot(ds16_s[...], stack_s[...]) * scale
    kv_send[0] = kv_s[span:, :]
    k_base = d_base + n_dp
    lend = wire.make(kv_send, kv_got, k_base, here.ffn(1))
    lend.start()
    own_k = kv_s[0:span, :]
    grad_q = lowered(dq_s[...].T)
    lend.wait_recv()
    grad_united = jnp.concatenate(
        [grad_q, lowered(own_k + kv_got[0]), lowered(own_v + kv_got[1])], 1
    )
    gq_out[...] = across(n1_s[...], grad_united)
    grad_h0_norm, gain_grad1 = rms_back(h0_s[...], gain1, against(grad_united, wq[...]))
    grad_h0 = h1_s[...] + grad_h0_norm
    gp_out[...] = grad_h0
    rowgrad_out[0] = lowered(grad_h0)
    lane8 = iota((1, width), 1)
    row8 = iota((8, width), 0)
    stats = jnp.where(lane8 == 0, loss, 0.0)
    numbers = (jnp.sum(valid_lane, keepdims=True), sum_hid, sum_attn, sum_ffn)
    for i, number in enumerate(numbers):
        stats = jnp.where(lane8 == i + 1, number, stats)
    sums = jnp.where(row8 == 0, gain_grad1, 0.0)
    sums = jnp.where(row8 == 1, gain_grad2, sums)
    sums = jnp.where(row8 == 2, gain_grad3, sums)
    sums_out[...] = jnp.where(row8 == 3, stats, sums)

    own_s[...] = own_s[...] - valid_col * fin_s[0:span, :].astype(jnp.float32)

    def add_in(k):
        hand_back(k).wait_recv()
        own_s[...] = own_s[...] + cand_in[k].astype(jnp.float32)

    loop(1, n_dp, add_in)
    rowgrad_out[1] = lowered(own_s[...])

    def end(k):
        for copy in offer(k):
            copy.wait_send()
        hand_back(k).wait_send()

    each(1, n_dp, end)
    for copy in (near, far, relayed, give, give_mid, give2, give2_mid, lend, *tell):
        copy.wait_send()


def layer(n_dp, rows, bias, lengths, qkv_weight, out_weight, weights, norm_gains, positions):
    span, width = rows.shape[1:]
    heads = width // HD
    low, full = jnp.bfloat16, jnp.float32
    vmem = pl.BlockSpec(memory_space=pltpu.VMEM)
    smem = pl.BlockSpec(memory_space=pltpu.SMEM)
    square = (span, width)
    number = 4 * n_dp + 16

    def out(shape, kind):
        return jax.ShapeDtypeStruct(shape, kind)

    return pl.pallas_call(
        functools.partial(layer_kernel, n_dp),
        out_shape=(
            out((2,) + square, low),
            out((width, 3 * width), full),
            out((width, width), full),
            out(square, full),
            out((4, 2, width, width), full),
            out((8, width), full),
        ),
        in_specs=[vmem, vmem, smem, vmem, vmem, vmem, vmem, vmem],
        out_specs=(vmem,) * 6,
        scratch_shapes=[
            pltpu.VMEM((n_dp,) + square, low),
            pltpu.VMEM((n_dp, 8, span), full),
            pltpu.VMEM((n_dp, width, span), low),
            pltpu.VMEM((n_dp, span, 128), full),
            pltpu.VMEM((n_dp,) + square, low),
            pltpu.VMEM((width, 3 * width), low),
            pltpu.VMEM((width, width), low),
            pltpu.VMEM(square, full),
            pltpu.VMEM(square, low),
            pltpu.VMEM(square, low),
            pltpu.VMEM((width, span), low),
            pltpu.VMEM((2 * span, width), low),
            pltpu.VMEM((2 * span, width), low),
            pltpu.VMEM((width, 2 * span), low),
            pltpu.VMEM((width, 2 * span), low),
            pltpu.VMEM((2 * span, span), full),
            pltpu.VMEM((heads, 2 * span, span), full),
            pltpu.VMEM((2 * span, heads * span), low),
            pltpu.VMEM((2 * span, heads * span), low),
            pltpu.VMEM((heads * span, width), low),
            pltpu.VMEM((width, span), low),
            pltpu.VMEM(square, full),
            pltpu.VMEM(square, full),
            pltpu.VMEM((width, span), low),
            pltpu.VMEM((4,) + square, full),
            pltpu.VMEM((span, 4 * span), low),
            pltpu.VMEM((4 * span, width), low),
            pltpu.VMEM((width, 4 * span), low),
            pltpu.VMEM((width, 4 * span), full),
            pltpu.VMEM((3, width, span), low),
            pltpu.VMEM((3, width, span), low),
            pltpu.VMEM((4, 8, span), full),
            pltpu.VMEM((4, 8, span), full),
            pltpu.VMEM((4, 8, span), full),
            pltpu.VMEM(square, full),
            pltpu.VMEM((width, span), full),
            pltpu.VMEM((2 * span, width), full),
            pltpu.VMEM((2,) + square, full),
            pltpu.VMEM((2,) + square, full),
            pltpu.SemaphoreType.DMA((number,)),
            pltpu.SemaphoreType.DMA((number,)),
        ],
        compiler_params=pltpu.CompilerParams(
            collective_id=1, has_side_effects=True, vmem_limit_bytes=LIMIT
        ),
        name="layer",
    )(rows, bias, lengths, qkv_weight, out_weight, weights, norm_gains, positions)


LEARN = 0.05
GAIN_LEARN = 0.4
STEP = 5
BETA_ONE = 0.5
BETA_TWO = 0.5
DECAY = 0.01
ADAM_EPS = 1e-08
CLIP = 0.05


def total_of(value):
    return jnp.sum(value, keepdims=True)


def reduce_kernel(
    n_dp,
    cap,
    part,
    rowgrad_ref,
    key_ref,
    asked_ref,
    gq_ref,
    go_ref,
    gp_ref,
    gf_ref,
    sums_ref,
    table_out,
    ffn_out,
    strips_out,
    sums_out,
    rows_s,
    hot_s,
    outgoing,
    incoming,
    near_send,
    near_got,
    far_send,
    far_got,
    own_s,
    piece_send,
    piece_got,
    whole_s,
    small,
    ss,
    rs,
):
    here = Peers(n_dp)
    wire = Wire(ss, rs)
    d, f = here.d, here.f
    half = lax.rem(f, 2)
    span, width = gp_ref.shape
    strip = span // 4
    ffn_rows = 2 * width
    rows_mine = ffn_rows + 6 * strip
    padded = part * n_dp
    block = 2 * span
    if cap < 128:
        incoming[...] = jnp.zeros_like(incoming)
    here.greet()

    def slot(s):
        return rows_s.at[pl.ds(s * block, block)]

    rows_s[0:span, :] = rowgrad_ref[0]
    rows_s[span:block, :] = rowgrad_ref[1]
    base = 0
    far = wire.make(slot(0), slot(2), base, here.ffn(2))
    near = wire.make(slot(0), slot(1), base + 1, here.ffn(1))
    relay = wire.make(slot(2), slot(3), base + 2, here.ffn(1))
    far.start()
    near.start()

    small[0, 0] = sums_ref[...]
    tell = [wire.make(small.at[0, 0], small.at[0, s], base + 2 + s, here.ffn(s)) for s in (1, 2, 3)]
    for copy in tell:
        copy.start()

    halves = (jnp.where(half == 0, 1.0, 0.0), jnp.where(half == 1, 1.0, 0.0))

    def pieces(s):
        first = pl.multiple_of(here.member[s] * strip, strip)
        rows = pl.ds(first, strip)
        yield 0, gf_ref[s, 0]
        yield width, gf_ref[s, 1]
        for j in range(3):
            yield ffn_rows + j * strip, gq_ref[rows, j * width : (j + 1) * width]
        yield ffn_rows + 3 * strip, go_ref[rows, :]
        for u in range(2):
            yield ffn_rows + (4 + u) * strip, gp_ref[rows, :] * halves[u]

    for i, s in enumerate((1, 3)):
        for first, value in pieces(s):
            near_send[i, first : first + value.shape[0], :] = lowered(value)
    base = base + 6
    cross = wire.make(near_send, near_got, base, here.ffn(1))
    cross.start()
    near.wait_recv()
    cross.wait_recv()
    for first, value in pieces(2):
        size = value.shape[0]
        got = near_got[1, first : first + size, :].astype(jnp.float32)
        far_send[first : first + size, :] = lowered(value + got)
    across_chip = wire.make(far_send, far_got, base + 1, here.ffn(2))
    across_chip.start()
    for first, value in pieces(0):
        size = value.shape[0]
        got = near_got[0, first : first + size, :].astype(jnp.float32)
        own_s[first : first + size, :] = value + got
    if padded > rows_mine:
        own_s[rows_mine:padded, :] = jnp.zeros((padded - rows_mine, width), jnp.float32)
    far.wait_recv()
    relay.start()
    relay.wait_recv()

    up = iota((cap, span), 0).astype(jnp.float32)
    r_base = base + 2

    def ship(k):
        return wire.make(
            outgoing.at[k],
            incoming.at[pl.ds(pl.multiple_of(k * 128, 128), cap)],
            r_base + k,
            here.ahead(k),
        )

    def choose(k):
        places = []
        level = up + lax.convert_element_type(k * cap, jnp.float32)
        for s in range(4):
            for column in range(2):
                key = key_ref[pl.ds(column * 4 + here.member[s], 1), :]
                places.append(jnp.where(level == key, 1.0, 0.0).astype(jnp.bfloat16))
        return lowered(dot(jnp.concatenate(places, 1), rows_s[...]))

    def send_rows(k):
        outgoing[k] = choose(k)
        ship(k).start()

    loop(1, n_dp, send_rows)
    incoming[0:cap, :] = choose(0)

    for copy in tell:
        copy.wait_recv()
    small[1, 0] = (small[0, 0] + small[0, 1]) + (small[0, 2] + small[0, 3])
    s_base = r_base + n_dp

    def share(row, k, number):
        return wire.make(
            small.at[row, 0], small.at[row + 1, d], number + k, here.ahead(k)
        )

    each(1, n_dp, lambda k: share(1, k, s_base).start())
    small[2, d] = small[1, 0]

    across_chip.wait_recv()
    own_s[0:rows_mine, :] = own_s[0:rows_mine, :] + far_got[0:rows_mine, :].astype(jnp.float32)
    p_base = s_base + n_dp

    def scatter(k):
        return wire.make(piece_send.at[k], piece_got.at[k], p_base + k, here.ahead(k))

    def part_rows(owner):
        return pl.ds(pl.multiple_of(owner * part, part), part)

    def scatter_step(k):
        owner = lax.rem(d + k, n_dp)
        piece_send[k] = lowered(own_s[part_rows(owner), :])
        scatter(k).start()

    loop(1, n_dp, scatter_step)
    rows_dev = table_out.shape[0]
    for k in range(n_dp):
        hot_s[:, k * 128 : (k + 1) * 128] = lowered(
            one_hot_columns(asked_ref[k].astype(jnp.float32), rows_dev)
        )

    def take_rows(k):
        ship(k).wait_recv()

    each(1, n_dp, take_rows)
    table_grad = dot(hot_s[...], incoming[...])
    table_out[...] = table_grad
    squares = total_of(table_grad * table_grad)
    mine = own_s[part_rows(d), :]
    own_s[0:part, :] = mine

    def add_piece(k):
        scatter(k).wait_recv()
        own_s[0:part, :] = own_s[0:part, :] + piece_got[k].astype(jnp.float32)

    loop(1, n_dp, add_piece)
    summed = own_s[0:part, :]
    squares = squares + total_of(summed * summed)
    whole_s[part_rows(d), :] = lowered(summed)
    a_base = p_base + n_dp

    def gather(k):
        rows = whole_s.at[part_rows(d)]
        return wire.make(rows, rows, a_base + k, here.ahead(k))

    each(1, n_dp, lambda k: gather(k).start())
    n_base = a_base + n_dp
    small[3, 0] = jnp.broadcast_to(squares, small.shape[2:])
    tell_norm = [
        wire.make(small.at[3, 0], small.at[3, s], n_base + s, here.ffn(s)) for s in (1, 2, 3)
    ]
    for copy in tell_norm:
        copy.start()
    each(1, n_dp, lambda k: share(1, k, s_base).wait_recv())
    for copy in tell_norm:
        copy.wait_recv()
    small[4, 0] = (small[3, 0] + small[3, 1]) + (small[3, 2] + small[3, 3])
    m_base = n_base + 4
    each(1, n_dp, lambda k: share(4, k, m_base).start())
    small[5, d] = small[4, 0]

    each(1, n_dp, lambda k: gather(k).wait_recv())
    strip_rows = 6 * strip
    strips_out[f] = whole_s[ffn_rows:rows_mine, :]
    g_base = m_base + n_dp
    mine_at = strips_out.at[f]
    far_at = strips_out.at[here.member[2]]
    far2 = wire.make(mine_at, mine_at, g_base, here.ffn(2))
    near2 = wire.make(mine_at, mine_at, g_base + 1, here.ffn(1))
    relay2 = wire.make(far_at, far_at, g_base + 2, here.ffn(1))
    far2.start()
    near2.start()
    ffn_out[...] = whole_s[0:ffn_rows, :]
    each(1, n_dp, lambda k: share(4, k, m_base).wait_recv())
    totals = small[2, 0]
    for k in range(1, n_dp):
        totals = totals + small[2, k]
    squares = small[5, 0]
    for k in range(1, n_dp):
        squares = squares + small[5, k]
    row8 = iota(totals.shape, 0)
    gains = jnp.where(row8 < 3, totals, 0.0)
    norm = jnp.sqrt(squares + total_of(gains * gains))
    sums_out[...] = jnp.where(row8 == 4, norm, totals)
    far2.wait_recv()
    relay2.start()
    near2.wait_recv()
    relay2.wait_recv()

    def end(k):
        ship(k).wait_send()
        share(1, k, s_base).wait_send()
        scatter(k).wait_send()
        gather(k).wait_send()
        share(4, k, m_base).wait_send()

    each(1, n_dp, end)
    for copy in (far, near, relay, cross, across_chip, far2, near2, relay2, *tell, *tell_norm):
        copy.wait_send()


def reduce_all(n_dp, cap, rows_dev, rowgrad, key, asked, gq, go, gp, gf, sums):
    span, width = gp.shape
    strip_rows = 6 * (span // 4)
    rows_mine = 2 * width + strip_rows
    part = -(-rows_mine // (16 * n_dp)) * 16
    low, full = jnp.bfloat16, jnp.float32
    vmem = pl.BlockSpec(memory_space=pltpu.VMEM)
    number = 7 * n_dp + 20

    def out(shape, kind):
        return jax.ShapeDtypeStruct(shape, kind)

    return pl.pallas_call(
        functools.partial(reduce_kernel, n_dp, cap, part),
        out_shape=(
            out((rows_dev, width), full),
            out((2 * width, width), low),
            out((4, strip_rows, width), low),
            out((8, width), full),
        ),
        in_specs=[vmem] * 8,
        out_specs=(vmem,) * 4,
        scratch_shapes=[
            pltpu.VMEM((8 * span, width), low),
            pltpu.VMEM((rows_dev, n_dp * 128), low),
            pltpu.VMEM((n_dp, cap, width), low),
            pltpu.VMEM((n_dp * 128, width), low),
            pltpu.VMEM((2, rows_mine, width), low),
            pltpu.VMEM((2, rows_mine, width), low),
            pltpu.VMEM((rows_mine, width), low),
            pltpu.VMEM((rows_mine, width), low),
            pltpu.VMEM((part * n_dp, width), full),
            pltpu.VMEM((n_dp, part, width), low),
            pltpu.VMEM((n_dp, part, width), low),
            pltpu.VMEM((part * n_dp, width), low),
            pltpu.VMEM((6, max(n_dp, 4), 8, width), full),
            pltpu.SemaphoreType.DMA((number,)),
            pltpu.SemaphoreType.DMA((number,)),
        ],
        compiler_params=pltpu.CompilerParams(
            collective_id=2, has_side_effects=True, vmem_limit_bytes=LIMIT
        ),
        name="reduce",
    )(rowgrad, key, asked, gq, go, gp, gf, sums)


def update_kernel(
    table_grad,
    ffn_grad,
    strips,
    sums,
    *refs,
):
    ins, outs = refs[:21], refs[21:]
    loss_out, rms_out, norm_out = outs[:3]
    outs = outs[3:]
    norm = sums[4:5, 0:1]
    factor = CLIP / jnp.maximum(norm, CLIP)
    corr_one = 1.0 - BETA_ONE**STEP
    corr_two = 1.0 - BETA_TWO**STEP
    width = sums.shape[1]

    def adam(which, rows, lanes, grad, rate):
        weight, moment, second = (ins[3 * which + i][rows, lanes] for i in range(3))
        clipped = grad.astype(jnp.float32) * factor
        moment = BETA_ONE * moment + (1.0 - BETA_ONE) * clipped
        second = BETA_TWO * second + (1.0 - BETA_TWO) * clipped * clipped
        outs[3 * which][rows, lanes] = weight - rate * (
            moment / corr_one / (jnp.sqrt(second / corr_two) + ADAM_EPS) + DECAY * weight
        )
        outs[3 * which + 1][rows, lanes] = moment
        outs[3 * which + 2][rows, lanes] = second

    every = slice(None)
    rows_dev = table_grad.shape[0]
    for first in range(0, rows_dev, 112):
        rows = slice(first, min(first + 112, rows_dev))
        adam(0, rows, every, table_grad[rows, :], LEARN)
    strip = strips.shape[1] // 6
    for m in range(4):
        rows = slice(m * strip, (m + 1) * strip)
        for j in range(3):
            adam(
                1,
                rows,
                slice(j * width, (j + 1) * width),
                strips[m, j * strip : (j + 1) * strip, :],
                LEARN,
            )
        adam(2, rows, every, strips[m, 3 * strip : 4 * strip, :], LEARN)
        for u in range(2):
            rows = slice((4 * u + m) * strip, (4 * u + m + 1) * strip)
            adam(6, rows, every, strips[m, (4 + u) * strip : (5 + u) * strip, :], LEARN)
    for which in range(2):
        for first in range(0, width, 64):
            rows = slice(first, first + 64)
            start = which * width + first
            adam(3 + which, rows, every, ffn_grad[start : start + 64, :], LEARN)
    adam(5, every, every, sums[0:3, :], GAIN_LEARN)
    stats = sums[3:4, :]
    roots = jnp.sqrt(stats / (stats[:, 1:2] * float(width)))

    def one(row, i):
        return jnp.sum(jnp.where(iota(row.shape, 1) == i, row, 0.0))

    loss_out[0] = one(stats, 0)
    loss_out[1] = one(stats, 1)
    for i in range(3):
        rms_out[i] = one(roots, 2 + i)
    norm_out[0] = one(sums[4:5, :], 0)


def update(table_grad, ffn_grad, strips, sums, states):
    vmem = pl.BlockSpec(memory_space=pltpu.VMEM)
    smem = pl.BlockSpec(memory_space=pltpu.SMEM)
    full = jnp.float32
    return pl.pallas_call(
        update_kernel,
        out_shape=tuple(jax.ShapeDtypeStruct((n,), full) for n in (2, 3, 1))
        + tuple(jax.ShapeDtypeStruct(a.shape, full) for a in states),
        in_specs=[vmem] * (4 + len(states)),
        out_specs=(smem,) * 3 + (vmem,) * len(states),
        compiler_params=pltpu.CompilerParams(vmem_limit_bytes=LIMIT),
        name="update",
    )(table_grad, ffn_grad, strips, sums, *states)


def shards(
    item_owner,
    item_row,
    lengths,
    log_count,
    item_table,
    table_mom,
    table_sec,
    qkv_weight,
    qkv_mom,
    qkv_sec,
    out_weight,
    out_mom,
    out_sec,
    ffn_in,
    ffn_in_mom,
    ffn_in_sec,
    ffn_back,
    ffn_back_mom,
    ffn_back_sec,
    norm_gains,
    gains_mom,
    gains_sec,
    positions,
    positions_mom,
    positions_sec,
):
    n_dp = lax.axis_size("dp")
    tokens = item_owner.shape[0]
    cap = max(2, 4 * tokens // (n_dp * lax.axis_size("ffn")))
    rows, bias, asked, key, weights = lookup(
        n_dp, cap, item_owner, item_row, log_count, item_table, ffn_in, ffn_back
    )
    rowgrad, gq, go, gp, gf, sums = layer(
        n_dp, rows, bias, lengths, qkv_weight, out_weight, weights, norm_gains, positions
    )
    table_grad, ffn_grad, strips, sums = reduce_all(
        n_dp, cap, item_table.shape[0], rowgrad, key, asked, gq, go, gp, gf, sums
    )
    return update(
        table_grad,
        ffn_grad,
        strips,
        sums,
        (
            item_table,
            table_mom,
            table_sec,
            qkv_weight,
            qkv_mom,
            qkv_sec,
            out_weight,
            out_mom,
            out_sec,
            ffn_in,
            ffn_in_mom,
            ffn_in_sec,
            ffn_back,
            ffn_back_mom,
            ffn_back_sec,
            norm_gains,
            gains_mom,
            gains_sec,
            positions,
            positions_mom,
            positions_sec,
        ),
    )


def solution(mesh):
    whole, rows, table = P(), P("dp", None), P(("dp", "ffn"), None)
    wide, tall = P(None, "ffn"), P("ffn", None)
    states = (table,) * 3 + (whole,) * 6 + (wide,) * 3 + (tall,) * 3 + (whole,) * 6
    return jax.shard_map(
        shards,
        mesh=mesh,
        in_specs=(rows, rows, P("dp"), P(("dp", "ffn"))) + states,
        out_specs=(whole,) * 3 + states,
        check_vma=False,
    )
```

```python
import functools
import math
import types

import jax
import jax.numpy as jnp
from jax import lax
from jax.experimental import pallas as pl
from jax.experimental.pallas import tpu as pltpu
from jax.sharding import PartitionSpec as P

MESH = pl.DeviceIdType.MESH
MIB = 1024 * 1024
LOW, FULL = jnp.bfloat16, jnp.float32

EPS = 1e-06
NEG = -1e30
HD = 32
ROOT = math.sqrt(2.0 / math.pi)
LEARN = 0.05
GAIN_LEARN = 0.4
STEP = 5
BETA_ONE = 0.5
BETA_TWO = 0.5
DECAY = 0.01
ADAM_EPS = 1e-08
CLIP = 0.05


def lowered(value):
    return value.astype(LOW)


def raised(value):
    return value.astype(FULL)


def dot(left, right):
    return jnp.dot(left, right, preferred_element_type=FULL)


def against(left, right):
    return lax.dot_general(left, right, (((1,), (1,)), ((), ())), preferred_element_type=FULL)


def across(left, right):
    return lax.dot_general(left, right, (((0,), (0,)), ((), ())), preferred_element_type=FULL)


def iota(shape, dim):
    return lax.broadcasted_iota(jnp.int32, shape, dim)


def loop(first, last, body):
    def step(k, unused):
        body(k)
        return unused

    if last - first == 1:
        body(first)
    elif last > first:
        lax.fori_loop(first, last, step, 0)


def each(first, last, body):
    if last - first <= 8:
        for k in range(first, last):
            body(k)
    else:
        loop(first, last, body)


def at(index, size):
    if isinstance(index, int):
        return pl.ds(index * size, size)
    return pl.ds(pl.multiple_of(index * size, size), size)


def spread(row, lanes):
    return jnp.broadcast_to(row, (lanes, row.shape[1])).T


def turned(block):
    return lowered(raised(block).T)


def total_of(value):
    return jnp.sum(value, keepdims=True)


def one_hot_rows(row, width):
    high = jnp.floor(row * (1.0 / 128.0))
    low = spread(row - high * 128.0, 128)
    base = lowered(jnp.where(low == raised(iota(low.shape, 1)), 1.0, 0.0))
    high = lowered(spread(high, 128))
    zero = jnp.zeros_like(base)
    return jnp.concatenate(
        [jnp.where(high == jnp.asarray(b, LOW), base, zero) for b in range(width // 128)], 1
    )


def one_hot_columns(row, height):
    return jnp.where(raised(iota((height, row.shape[1]), 0)) == row, 1.0, 0.0)


def factor_of(hidden):
    return lax.rsqrt(jnp.mean(hidden * hidden, -1, keepdims=True) + EPS)


def rms_back(hidden, gain, upstream):
    factor = factor_of(hidden)
    scaled = upstream * gain
    inner = jnp.mean(scaled * hidden, -1, keepdims=True)
    grad_hidden = factor * scaled - hidden * (factor * factor * factor * inner)
    return grad_hidden, jnp.sum(upstream * hidden * factor, 0, keepdims=True)


class Peers:
    def __init__(self, n_dp):
        self.n_dp, self.n_z = n_dp, n_dp // 2
        self.d, self.f = lax.axis_index("dp"), lax.axis_index("ffn")
        self.z, self.y = self.d // 2, lax.rem(self.d, 2)
        near = self.f + 1 - 2 * lax.rem(self.f, 2)
        far = lax.rem(self.f + 2, 4)
        self.member = (self.f, near, far, 3 - self.f)

    def ffn(self, s):
        return (self.d, self.member[s])

    def ahead(self, i):
        return self.apart(i // self.n_z, i % self.n_z)

    def behind(self, i):
        return self.apart(i // self.n_z, self.n_z - i % self.n_z)

    def apart(self, ky, kz):
        z = lax.rem(self.z + kz, self.n_z)
        return (z * 2 + self.y + ky - 2 * self.y * ky, self.f)

    def side(self):
        return (self.d + 1 - 2 * self.y, self.f)

    def up(self, k):
        return (lax.rem(self.z + k, self.n_z) * 2 + self.y, self.f)

    def down(self, k):
        return (lax.rem(self.z + self.n_z - k, self.n_z) * 2 + self.y, self.f)

    def greet(self):
        barrier = pltpu.get_barrier_semaphore()

        def hello(where):
            pl.semaphore_signal(barrier, inc=1, device_id=where, device_id_type=MESH)

        for s in (1, 2, 3):
            hello(self.ffn(s))
        each(1, self.n_dp, lambda k: hello(self.ahead(k)))

    def met(self):
        pl.semaphore_wait(pltpu.get_barrier_semaphore(), self.n_dp + 2)


class Wire:
    def __init__(self, send, recv):
        self.send, self.recv, self.used = send, recv, 0

    def take(self, number):
        self.used += number
        return self.used - number

    def make(self, src, dst, number, where):
        return pltpu.make_async_remote_copy(
            src_ref=src,
            dst_ref=dst,
            send_sem=self.send.at[number],
            recv_sem=self.recv.at[number],
            device_id=where,
            device_id_type=MESH,
        )


class Group:
    def __init__(self, *copies):
        self.copies = copies

    def start(self):
        for copy in self.copies:
            copy.start()

    def wait_recv(self):
        for copy in self.copies:
            copy.wait_recv()

    def wait_send(self):
        for copy in self.copies:
            copy.wait_send()


INPUTS = [
    "owner",
    "row",
    "lengths",
    "count",
    "table",
    "wq",
    "wo",
    "w_in",
    "w_back",
    "gains",
    "positions",
]
OUTPUTS = ["table_grad", "ffn_grad", "strips", "sums"]


def plan(n_dp, cap, rows_dev, span, width, heads):
    n_z = n_dp // 2
    filled = n_dp * cap
    padded = -(-rows_dev // 128) * 128
    square = (span, width)
    ffn_part, strip_part = parts(n_dp, span, width)
    return {
        "table_s": (rows_dev, width, FULL),
        "wq_s": (width, 3 * width, FULL),
        "wo_s": (width, width, FULL),
        "positions_s": (2 * span, width, FULL),
        "weights": (4, 2, width, width, LOW),
        "hot": (32 * n_dp, span, LOW),
        "slot_s": (8, span, FULL),
        "kind_s": (8, span, FULL),
        "table_low": (padded, width, LOW),
        "req": (n_dp, 1, 128, jnp.int32),
        "asked": (n_dp, 1, 128, jnp.int32),
        "send_rows": (n_dp, cap, width, LOW),
        "send_bias": (n_dp, 1, 128, FULL),
        "found": (4 * filled, width, LOW),
        "found_bias": (4 * n_dp, 1, 128, FULL),
        "bias_s": (8, span, FULL),
        "cands": (n_dp * span, width, LOW),
        "cand_bias": (n_dp, 8, span, FULL),
        "cand_t": (width, (n_dp if kept(n_dp) else 1) * span, LOW),
        "cand_col": ((n_dp if kept(n_dp) else 1) * span, 128, FULL),
        "logit_s": (6 * span if kept(n_dp) else 2 * span, span, FULL),
        "stat_s": (4, 8, span, FULL),
        "wq16": (width, 3 * width, LOW),
        "wo16": (width, width, LOW),
        "h0_s": square + (FULL,),
        "n1_s": square + (LOW,),
        "q_s": square + (LOW,),
        "qt_s": (width, span, LOW),
        "k_s": (2 * span, width, LOW),
        "v_s": (2 * span, width, LOW),
        "kt_s": (width, 2 * span, LOW),
        "vt_s": (width, 2 * span, LOW),
        "mask_s": (2 * span, span, FULL),
        "p_s": (heads, 2 * span, span, FULL),
        "p16_s": (2 * span, heads * span, LOW),
        "stack_s": (heads * span, width, LOW),
        "mixt_s": (width, span, LOW),
        "h1_s": square + (FULL,),
        "h2_s": square + (FULL,),
        "n2t_s": (width, span, LOW),
        "pre_s": (4 * span, width, FULL),
        "act_s": (span, 4 * span, LOW),
        "fin_s": (4 * span, width, LOW),
        "fint_s": (width, 4 * span, LOW),
        "acc_s": (width, 4 * span, FULL),
        "acc_send": (3, width, span, LOW),
        "acc_got": (3, width, span, LOW),
        "mid_send": (3, 8, span, FULL),
        "mid_got": (3, 8, span, FULL),
        "tot_s": (4, 8, span, FULL),
        "cand_send": (n_z, span, width, LOW),
        "side_got": (n_z, span, width, LOW),
        "line_got": (n_z, span, width, LOW),
        "own_s": square + (FULL,),
        "dq_s": (width, span, FULL),
        "kv_s": (2 * span, width, FULL),
        "kv_got": (2 * span, width, FULL),
        "gf_s": (4, 2, width, width, FULL),
        "fnear_send": (2, 2 * width, width, LOW),
        "fnear_got": (2, 2 * width, width, LOW),
        "ffar_send": (2 * width, width, LOW),
        "ffar_got": (2 * width, width, LOW),
        "snear_send": (2, 6 * span // 4, width, LOW),
        "snear_got": (2, 6 * span // 4, width, LOW),
        "sfar_send": (6 * span // 4, width, LOW),
        "sfar_got": (6 * span // 4, width, LOW),
        "strip_s": (n_dp * strip_part, width, FULL),
        "fside_send": (n_z * ffn_part, width, LOW),
        "fside_got": (n_z * ffn_part, width, LOW),
        "fline_send": (n_z, ffn_part, width, LOW),
        "fline_got": (n_z, ffn_part, width, LOW),
        "sside_send": (n_z * strip_part, width, LOW),
        "sside_got": (n_z * strip_part, width, LOW),
        "sline_send": (n_z, strip_part, width, LOW),
        "sline_got": (n_z, strip_part, width, LOW),
        "whole_f": (n_dp * ffn_part, width, LOW),
        "whole_t": (n_dp * strip_part, width, LOW),
        "incoming": (filled, width, LOW),
        "padded_in": (8 * 128 if cap < 128 else 16, width, LOW),
        "owned": (rows_dev, min(n_dp, 8) * 128, LOW),
        "small": (5, 4, 8, width, FULL),
        "small_dp": (2, n_dp, 8, width, FULL),
    }


def kept(n_dp):
    return n_dp <= 8


def parts(n_dp, span, width):
    return (
        -(-2 * width // (16 * n_dp)) * 16,
        -(-6 * span // (64 * n_dp)) * 16,
    )


def step_kernel(n_dp, cap, names, *refs):
    r = types.SimpleNamespace(**dict(zip(names, refs)))
    here = Peers(n_dp)
    wire = Wire(r.send_sems, r.recv_sems)
    d, f, n_z = here.d, here.f, here.n_z
    me, near, far, cross = here.member
    span, width = r.h0_s.shape
    heads = width // HD
    scale = HD ** (-0.5)
    half = lax.rem(f, 2)
    begin = half * span
    filled = n_dp * cap
    kinds = 4 * n_dp
    rows_dev = r.table_s.shape[0]
    padded = r.table_low.shape[0]
    ended = []

    here.greet()
    loads = [
        pltpu.make_async_copy(src, dst, r.load_sems.at[i])
        for i, (src, dst) in enumerate(
            (
                (r.table, r.table_s),
                (r.wq, r.wq_s),
                (r.wo, r.wo_s),
                (r.positions, r.positions_s),
            )
        )
    ]
    for load in loads:
        load.start()

    place = iota((kinds, span), 0)
    slot_of = jnp.zeros((kinds, span), jnp.int32)
    for s in (1, 2, 3):
        slot_of = slot_of + (place >= s * n_dp).astype(jnp.int32)
    steps = place - slot_of * n_dp
    other_y = (steps >= n_z).astype(jnp.int32)
    steps = steps - other_y * n_z + here.z
    steps = jnp.where(steps >= n_z, steps - n_z, steps)
    ahead = steps * 2 + here.y + other_y * (1 - 2 * here.y)
    named = ahead * 4 + jnp.where(
        slot_of == 0, me, jnp.where(slot_of == 1, near, jnp.where(slot_of == 2, far, cross))
    )

    def chunk_of(ref, c):
        return ref[c // 4 : c // 4 + 1, (c % 4) * span : (c % 4 + 1) * span]

    for c in range(8):
        r.hot[c * kinds : (c + 1) * kinds, :] = lowered(
            jnp.where(chunk_of(r.owner, c) == named, 1.0, 0.0)
        )
    before = lowered(jnp.where(iota((span, span), 0) < iota((span, span), 1), 1.0, 0.0))
    carry = jnp.zeros((kinds, 1), FULL)
    place_f = raised(place)
    asking = jnp.zeros((2 * n_dp, 128), FULL)
    for c in range(8):
        ones = raised(r.hot[c * kinds : (c + 1) * kinds, :])
        ranks = dot(r.hot[c * kinds : (c + 1) * kinds, :], before)
        slot = jnp.sum(ones * (ranks + carry), 0, keepdims=True)
        carry = carry + jnp.sum(ones, 1, keepdims=True)
        r.slot_s[c : c + 1, :] = slot
        r.kind_s[c : c + 1, :] = jnp.sum(ones * place_f, 0, keepdims=True)
        row = chunk_of(r.row, c)
        mine = ones[:n_dp]
        sought = jnp.concatenate([mine * raised(row >> 5), mine * raised(row & 31)], 0)
        asking = asking + against(lowered(sought), lowered(one_hot_columns(slot, 128)))
    wanted = (asking[:n_dp] * 32.0 + asking[n_dp:]).astype(jnp.int32)
    for k in range(n_dp):
        r.req[k, 0:1, :] = wanted[k : k + 1, :]
    r.asked[0] = r.req[0]
    q_base = wire.take(n_dp)

    def ask(k):
        return wire.make(r.req.at[k], r.asked.at[k], q_base + k, here.ahead(k))

    here.met()
    each(1, n_dp, lambda k: ask(k).start())

    r.weights[0, 0] = lowered(r.w_in[...])
    r.weights[0, 1] = lowered(r.w_back[...])
    w_base = wire.take(3)
    w_near = wire.make(r.weights.at[0], r.weights.at[1], w_base, here.ffn(1))
    w_far = wire.make(r.weights.at[0], r.weights.at[2], w_base + 1, here.ffn(2))
    w_relay = wire.make(r.weights.at[2], r.weights.at[3], w_base + 2, here.ffn(1))
    w_far.start()
    w_near.start()
    ended += [w_far, w_near, w_relay]

    loads[0].wait()
    r.table_low[0:rows_dev, :] = lowered(r.table_s[...])
    if padded > rows_dev:
        r.table_low[rows_dev:padded, :] = jnp.zeros((padded - rows_dev, width), LOW)
    counts = lowered(jnp.broadcast_to(raised(r.count[...].reshape(1, rows_dev)), (8, rows_dev)))
    if padded > rows_dev:
        counts = jnp.concatenate([counts, jnp.zeros((8, padded - rows_dev), LOW)], 1)
    r_base, b_base = wire.take(n_dp), wire.take(n_dp)

    def reply(k):
        return Group(
            wire.make(r.send_rows.at[k], r.found.at[at(k, cap)], r_base + k, here.behind(k)),
            wire.make(r.send_bias.at[k], r.found_bias.at[k], b_base + k, here.behind(k)),
        )

    def fetch(k):
        chosen = one_hot_rows(raised(r.asked[k]), padded)
        return lowered(dot(chosen, r.table_low[...]))[:cap], against(counts, chosen)[0:1, :]

    def serve(k):
        ask(k).wait_recv()
        rows, bias = fetch(k)
        r.send_rows[k] = rows
        r.send_bias[k] = bias
        reply(k).start()

    loop(1, n_dp, serve)
    rows, bias = fetch(0)
    r.found[0:cap, :] = rows
    r.found_bias[0] = bias
    passes = [(wire.take(n_dp), wire.take(n_dp)) for i in range(3)]

    def pass_on(k, source, target, number, who):
        first, second = passes[number]
        return Group(
            wire.make(
                r.found.at[at(source * n_dp + k, cap)],
                r.found.at[at(target * n_dp + k, cap)],
                first + k,
                here.ffn(who),
            ),
            wire.make(
                r.found_bias.at[source * n_dp + k],
                r.found_bias.at[target * n_dp + k],
                second + k,
                here.ffn(who),
            ),
        )

    def to_far(k):
        return pass_on(k, 0, 2, 0, 2)

    def to_near(k):
        return pass_on(k, 0, 1, 1, 1)

    def relay(k):
        return pass_on(k, 2, 3, 2, 1)

    def forward(k):
        to_far(k).start()
        to_near(k).start()

    def relay_on(k):
        to_far(k).wait_recv()
        relay(k).start()

    forward(0)
    lag = min(3, n_dp - 1)

    def take_on(k):
        reply(k).wait_recv()
        forward(k)

    each(1, lag, take_on)

    def take_both(k):
        take_on(k)
        relay_on(k - lag)

    each(lag, n_dp, take_both)
    w_far.wait_recv()
    w_relay.start()
    each(n_dp - lag, n_dp, relay_on)
    loads[1].wait()
    loads[2].wait()
    r.wq16[...] = lowered(r.wq_s[...])
    r.wo16[...] = lowered(r.wo_s[...])

    def take_near(k):
        to_near(k).wait_recv()
        relay(k).wait_recv()

    each(0, n_dp, take_near)

    def chosen_rows(column, quarter):
        chunk = pl.ds(column * 4 + quarter, 1)
        key = r.kind_s[chunk, :] * float(cap) + r.slot_s[chunk, :]
        return dot(one_hot_rows(key, 4 * filled), r.found[...])

    r.cands[0:span, :] = lowered(chosen_rows(1, f))
    bias_rows = lowered(r.found_bias[:, 0, :].T)
    lane = iota((1, span), 1)
    length = r.lengths[f // 2]
    valid_lane = jnp.where(lane + begin < length, 1.0, 0.0)
    valid_col = jnp.where(iota((span, 1), 0) + begin < length, 1.0, 0.0)
    chunk = 4 + f
    marks = one_hot_columns(r.slot_s[pl.ds(chunk, 1), :], 128)
    bias = jnp.sum(dot(bias_rows, r.hot[at(chunk, kinds), :]) * marks, 0, keepdims=True)
    r.bias_s[...] = jnp.broadcast_to(bias, (8, span))
    r.cand_bias[0] = jnp.broadcast_to(jnp.where(lane + begin < length, -bias, NEG), (8, span))
    z_base, y_base = wire.take(2 * n_z), wire.take(2 * n_z)

    def slot(k, ky):
        if isinstance(k, int) and k == 0:
            return ky
        return 1 + k + ky * (n_z - 1)

    def offer_line(k):
        i = slot(k, 0)
        return Group(
            wire.make(r.cands.at[at(0, span)], r.cands.at[at(i, span)], z_base + k, here.up(k)),
            wire.make(r.cand_bias.at[0], r.cand_bias.at[i], z_base + n_z + k, here.up(k)),
        )

    def offer_side(k):
        i, j = slot(k, 0), slot(k, 1)
        return Group(
            wire.make(r.cands.at[at(i, span)], r.cands.at[at(j, span)], y_base + k, here.side()),
            wire.make(r.cand_bias.at[i], r.cand_bias.at[j], y_base + n_z + k, here.side()),
        )

    def nearest(j):
        return jnp.where(here.z == 0, n_z - j, j)

    each(1, n_z, lambda k: offer_line(k).start())
    offer_side(0).start()

    def hand_on(j):
        k = nearest(j)
        offer_line(k).wait_recv()
        offer_side(k).start()

    loads[3].wait()
    gain1, gain2, gain3 = r.gains[0:1, :], r.gains[1:2, :], r.gains[2:3, :]
    hidden0 = raised(lowered(chosen_rows(0, f))) + r.positions_s[at(half, span), :]
    r.h0_s[...] = hidden0
    normed1 = lowered(hidden0 * factor_of(hidden0) * gain1)
    r.n1_s[...] = normed1
    r.q_s[...] = lowered(dot(normed1, r.wq16[:, :width]))
    r.k_s[0:span, :] = lowered(dot(normed1, r.wq16[:, width : 2 * width]))
    r.v_s[0:span, :] = lowered(dot(normed1, r.wq16[:, 2 * width :]))
    hidden0 = raised(lowered(chosen_rows(0, near))) + r.positions_s[at(1 - half, span), :]
    normed1 = lowered(hidden0 * factor_of(hidden0) * gain1)
    r.k_s[span:, :] = lowered(dot(normed1, r.wq16[:, width : 2 * width]))
    r.v_s[span:, :] = lowered(dot(normed1, r.wq16[:, 2 * width :]))
    r.qt_s[...] = turned(r.q_s[...])
    r.kt_s[...] = turned(r.k_s[...])
    r.vt_s[...] = turned(r.v_s[...])
    key_at = iota((2 * span, span), 0)
    key_at = jnp.where(key_at < span, key_at + begin, key_at - begin)
    allowed = (key_at <= iota((2 * span, span), 1) + begin) & (key_at < length)
    r.mask_s[...] = jnp.where(allowed, 0.0, NEG)
    row_head = iota((width, span), 0) // HD
    lane_head = iota((span, width), 1) // HD

    def forward_head(h):
        rows = at(h, HD)
        mine = jnp.where(row_head == h, raised(r.qt_s[...]), 0.0)
        scores = dot(r.k_s[...], lowered(mine)) * scale + r.mask_s[...]
        expo = jnp.exp(scores - jnp.max(scores, 0, keepdims=True))
        probs = expo / jnp.sum(expo, 0, keepdims=True)
        r.p_s[h] = probs
        low_probs = lowered(probs)
        r.p16_s[:, at(h, span)] = low_probs
        r.mixt_s[rows, :] = lowered(dot(r.vt_s[rows, :], low_probs))

    loop(0, heads, forward_head)
    hand_on(1)
    attn = dot(turned(r.mixt_s[...]), r.wo16[...])
    hidden1 = r.h0_s[...] + attn
    r.h1_s[...] = hidden1
    sum_attn = total_of(valid_col * attn * attn)
    normed2 = lowered(hidden1 * factor_of(hidden1) * gain2)
    r.n2t_s[...] = turned(normed2)
    w_near.wait_recv()
    w_relay.wait_recv()
    for s in range(4):
        pre = dot(normed2, r.weights[s, 0])
        r.pre_s[s * span : (s + 1) * span, :] = pre
        inner = jnp.tanh(ROOT * (pre + 0.044715 * pre * pre * pre))
        r.act_s[:, s * span : (s + 1) * span] = lowered(0.5 * pre * (1.0 + inner))
    branch = dot(r.act_s[...], jnp.concatenate([r.weights[s, 1] for s in range(4)], 0))
    hidden2 = r.h1_s[...] + branch
    r.h2_s[...] = hidden2
    sum_ffn = total_of(valid_col * branch * branch)
    sum_hid = total_of(valid_col * hidden2 * hidden2)
    final = lowered(hidden2 * factor_of(hidden2) * gain3)
    r.fin_s[0:span, :] = final
    f_base = wire.take(3)
    fin = [r.fin_s.at[at(s, span)] for s in range(4)]
    fin_near = wire.make(fin[0], fin[1], f_base, here.ffn(1))
    fin_far = wire.make(fin[0], fin[2], f_base + 1, here.ffn(2))
    fin_relay = wire.make(fin[2], fin[3], f_base + 2, here.ffn(1))
    fin_far.start()
    fin_near.start()
    ended += [fin_far, fin_near, fin_relay]

    def turn_fin(s):
        r.fint_s[:, s * span : (s + 1) * span] = turned(r.fin_s[s * span : (s + 1) * span, :])

    turn_fin(0)

    def prepare(i):
        if kept(n_dp):
            r.cand_t[:, at(i, span)] = turned(r.cands[at(i, span), :])
            r.cand_col[at(i, span), :] = spread(r.cand_bias[i, 0:1, :], 128)

    def columns(i, number):
        if kept(n_dp):
            return r.cand_col[slots(i, number), :]
        rows = [spread(r.cand_bias[i + j, 0:1, :], 128) for j in range(number)]
        return jnp.concatenate(rows, 0)

    def slots(i, number):
        if isinstance(i, int):
            return pl.ds(i * span, number * span)
        return pl.ds(pl.multiple_of(i * span, span), number * span)

    prepare(0)
    offer_side(0).wait_recv()
    prepare(1)
    r.acc_s[...] = jnp.zeros_like(r.acc_s)
    for s in range(4):
        r.stat_s[s, 0:1, :] = jnp.full((1, span), NEG, FULL)
        r.stat_s[s, 1:2, :] = jnp.zeros((1, span), FULL)

    def count_in(s, i, number):
        lanes = slice(s * span, (s + 1) * span)
        rows = slots(i, number)
        first = s % 2 * 3 * span if kept(n_dp) else 0
        held = slice(first, first + number * span)
        logits = dot(r.cands[rows, :], r.fint_s[:, lanes])
        r.logit_s[held, :] = logits + jnp.concatenate([columns(i, number)] * (span // 128), 1)
        top = r.stat_s[s, 0:1, :]
        higher = jnp.maximum(top, jnp.max(r.logit_s[held, :], 0, keepdims=True))
        shrink = jnp.exp(top - higher)
        expo = jnp.exp(r.logit_s[held, :] - higher)
        r.stat_s[s, 0:1, :] = higher
        r.stat_s[s, 1:2, :] = r.stat_s[s, 1:2, :] * shrink + jnp.sum(expo, 0, keepdims=True)
        if kept(n_dp):
            part = dot(r.cand_t[:, rows], lowered(expo))
        else:
            part = across(r.cands[rows, :], lowered(expo))
        r.acc_s[:, lanes] = r.acc_s[:, lanes] * shrink + part

    def count(s, group):
        first = (0, 2, n_z + 1)[group]
        number = (2, n_z - 1, n_z - 1)[group]
        if number <= 3:
            if number:
                count_in(s, first, number)
        else:
            loop(first, first + number, lambda i: count_in(s, i, 1))

    count(0, 0)
    fin_near.wait_recv()
    turn_fin(1)
    count(1, 0)
    each(2, n_z, hand_on)
    fin_far.wait_recv()
    fin_relay.start()
    turn_fin(2)
    count(2, 0)
    loop(2, n_z + 1, prepare)
    count(2, 1)
    fin_relay.wait_recv()
    turn_fin(3)
    count(3, 0)
    count(3, 1)
    count(0, 1)
    count(1, 1)

    def prepare_side(k):
        offer_side(k).wait_recv()
        prepare(slot(k, 1))

    loop(1, n_z, prepare_side)

    a_base = wire.take(6)

    def give(i, who):
        return Group(
            wire.make(r.acc_send.at[i], r.acc_got.at[i], a_base + 2 * i, here.ffn(who)),
            wire.make(r.mid_send.at[i], r.mid_got.at[i], a_base + 2 * i + 1, here.ffn(who)),
        )

    gives = [give(0, 1), give(1, 1), give(2, 2)]
    ended += gives

    def fill(i, s):
        r.acc_send[i] = lowered(r.acc_s[:, s * span : (s + 1) * span])
        r.mid_send[i] = r.stat_s[s]
        gives[i].start()

    def merge(s, i):
        gives[i].wait_recv()
        lanes = slice(s * span, (s + 1) * span)
        top, other = r.stat_s[s, 0:1, :], r.mid_got[i, 0:1, :]
        higher = jnp.maximum(top, other)
        left, right = jnp.exp(top - higher), jnp.exp(other - higher)
        r.acc_s[:, lanes] = r.acc_s[:, lanes] * left + raised(r.acc_got[i]) * right
        r.stat_s[s, 0:1, :] = higher
        r.stat_s[s, 1:2, :] = r.stat_s[s, 1:2, :] * left + r.mid_got[i, 1:2, :] * right

    count(3, 2)
    fill(0, 3)
    count(2, 2)
    merge(2, 0)
    fill(2, 2)
    count(1, 2)
    fill(1, 1)
    count(0, 2)
    merge(0, 1)
    merge(0, 2)
    total = r.stat_s[0, 1:2, :]
    log_total = r.stat_s[0, 0:1, :] + jnp.log(total)
    r.tot_s[0] = jnp.broadcast_to(jnp.where(valid_lane > 0, log_total, -NEG), (8, span))
    def end_pass(k):
        to_far(k).wait_send()
        to_near(k).wait_send()
        relay(k).wait_send()

    each(0, n_dp, end_pass)

    t_base = wire.take(4)
    tell = Group(
        *[wire.make(r.tot_s.at[0], r.tot_s.at[s], t_base + s, here.ffn(s)) for s in (1, 2, 3)]
    )
    tell.start()
    ended.append(tell)
    if not kept(n_dp):
        r.cand_t[...] = turned(r.cands[0:span, :])
    target_t = raised(r.cand_t[:, 0:span])
    positive = (
        jnp.sum(raised(r.fint_s[:, :span]) * target_t, 0, keepdims=True) - r.bias_s[0:1, :]
    )
    loss = total_of(valid_lane * (log_total - positive))
    grad_final = ((r.acc_s[:, 0:span] / total - target_t) * valid_lane).T

    grad_h2, gain_grad3 = rms_back(r.h2_s[...], gain3, grad_final)
    up = lowered(grad_h2)
    r.h2_s[...] = grad_h2
    for s in (1, 3, 2, 0):
        lanes = slice(s * span, (s + 1) * span)
        r.gf_s[s, 1] = across(r.act_s[:, lanes], up)
        grad_act = against(up, r.weights[s, 1])
        pre = r.pre_s[s * span : (s + 1) * span, :]
        inner = jnp.tanh(ROOT * (pre + 0.044715 * pre * pre * pre))
        slope = 0.5 * (1.0 + inner) + 0.5 * pre * (1.0 - inner * inner) * (
            ROOT * (1.0 + 3.0 * 0.044715 * pre * pre)
        )
        grad_pre = lowered(grad_act * slope)
        r.gf_s[s, 0] = dot(r.n2t_s[...], grad_pre)
        r.act_s[:, lanes] = grad_pre
    for i, s in enumerate((1, 3)):
        for j in range(2):
            r.fnear_send[i, j * width : (j + 1) * width, :] = lowered(r.gf_s[s, j])
    e_base = wire.take(4)
    f_near = wire.make(r.fnear_send, r.fnear_got, e_base, here.ffn(1))
    f_far = wire.make(r.ffar_send, r.ffar_got, e_base + 1, here.ffn(2))
    s_near = wire.make(r.snear_send, r.snear_got, e_base + 2, here.ffn(1))
    s_far = wire.make(r.sfar_send, r.sfar_got, e_base + 3, here.ffn(2))
    ended += [f_near, f_far, s_near, s_far]
    f_near.start()

    tell.wait_recv()
    side_base, line_base = wire.take(n_z), wire.take(n_z)

    def cand_side(k):
        return wire.make(r.cand_send.at[k], r.side_got.at[k], side_base + k, here.side())

    def cand_line(k):
        return wire.make(r.cand_send.at[k], r.line_got.at[k], line_base + k, here.down(k))

    def cand_grad(i):
        column = jnp.concatenate([columns(i, 1)] * (4 * span // 128), 1)
        level = jnp.concatenate([r.tot_s[s, 0:1, :] for s in range(4)], 1)
        logits = dot(r.cands[at(i, span), :], r.fint_s[...]) + column
        return dot(lowered(jnp.exp(logits - level)), r.fin_s[...])

    def slot_at(k, ky):
        return jnp.where(k == 0, ky, 1 + k + ky * (n_z - 1))

    def side_step(k):
        r.cand_send[k] = lowered(cand_grad(slot_at(k, 1)))
        cand_side(k).start()

    def line_step(k):
        grad = cand_grad(slot_at(k, 0))
        cand_side(k).wait_send()
        cand_side(k).wait_recv()
        r.cand_send[k] = lowered(grad + raised(r.side_got[k]))
        cand_line(k).start()

    middle = n_z // 2
    side_step(middle)

    def side_rest(k):
        side_step(lax.rem(k + middle, n_z))

    loop(1, n_z, side_rest)

    grad_normed2 = against(
        r.act_s[...], jnp.concatenate([r.weights[s, 0] for s in range(4)], 1)
    )
    grad_h1_norm, gain_grad2 = rms_back(r.h1_s[...], gain2, grad_normed2)
    grad_h1 = r.h2_s[...] + grad_h1_norm
    r.h1_s[...] = grad_h1
    f_near.wait_recv()
    for j in range(2):
        rows = slice(j * width, (j + 1) * width)
        r.ffar_send[rows, :] = lowered(r.gf_s[2, j] + raised(r.fnear_got[1, rows, :]))
    f_far.start()

    attn_up = lowered(grad_h1)
    r.acc_s[:, 3 * width :] = dot(r.mixt_s[...], attn_up)
    grad_mixed = lowered(against(attn_up, r.wo16[...]))
    grad_mixed_f = raised(grad_mixed)
    r.mixt_s[...] = turned(grad_mixed)
    for h in range(heads):
        r.stack_s[h * span : (h + 1) * span, :] = lowered(
            jnp.where(lane_head == h, grad_mixed_f, 0.0)
        )
    r.kv_s[...] = dot(r.p16_s[...], r.stack_s[...])
    r.logit_s[span : 2 * span, :] = r.kv_s[span:, :]
    r.own_s[...] = r.kv_s[0:span, :]

    def backward_head(h):
        rows = at(h, HD)
        mine = jnp.where(row_head == h, raised(r.mixt_s[...]), 0.0)
        grad_probs = dot(r.v_s[...], lowered(mine))
        probs = r.p_s[h]
        inner = jnp.sum(probs * grad_probs, 0, keepdims=True)
        grad_scores = lowered(probs * (grad_probs - inner))
        r.p16_s[:, at(h, span)] = grad_scores
        r.dq_s[rows, :] = dot(r.kt_s[rows, :], grad_scores) * scale

    loop(0, heads // 2, backward_head)
    if middle:
        line_step(middle)
    loop(heads // 2, heads, backward_head)
    queries = raised(r.q_s[...])
    for h in range(heads):
        r.stack_s[h * span : (h + 1) * span, :] = lowered(jnp.where(lane_head == h, queries, 0.0))
    r.kv_s[...] = dot(r.p16_s[...], r.stack_s[...]) * scale
    r.logit_s[0:span, :] = r.kv_s[span:, :]
    k_base = wire.take(1)
    lend = wire.make(r.logit_s.at[at(0, 2 * span)], r.kv_got, k_base, here.ffn(1))
    ended.append(lend)
    lend.start()
    ffn_part, strip_part = parts(n_dp, span, width)
    f_far.wait_recv()
    for j in range(2):
        rows = slice(j * width, (j + 1) * width)
        r.pre_s[rows, :] = (
            r.gf_s[0, j] + raised(r.fnear_got[0, rows, :]) + raised(r.ffar_got[rows, :])
        )
    if n_dp * ffn_part > 2 * width:
        r.pre_s[2 * width : n_dp * ffn_part, :] = jnp.zeros(
            (n_dp * ffn_part - 2 * width, width), FULL
        )
    m_base = wire.take(2 + 2 * n_z)

    def sum_dp(source, size, side_send, side_got, line_send, line_got, base):
        def rows_of(k, y):
            return at(y * n_z + lax.rem(here.z + k, n_z), size)

        across_y = wire.make(side_send, side_got, base, here.side())

        def along(k):
            return wire.make(line_send.at[k], line_got.at[k], base + 1 + k, here.up(k))

        def begin_side():
            def fill_side(k):
                side_send[at(k, size), :] = lowered(source[rows_of(k, 1 - here.y), :])

            loop(0, n_z, fill_side)
            across_y.start()

        def begin_line():
            across_y.wait_recv()

            def fill_line(k):
                line_send[k] = lowered(
                    source[rows_of(k, here.y), :] + raised(side_got[at(k, size), :])
                )
                along(k).start()

            loop(1, n_z, fill_line)

        def finish():
            value = source[rows_of(0, here.y), :] + raised(side_got[0:size, :])
            for k in range(1, n_z):
                along(k).wait_recv()
                value = value + raised(line_got[k])
            return value

        def end():
            across_y.wait_send()
            each(1, n_z, lambda k: along(k).wait_send())

        return begin_side, begin_line, finish, end

    ffn_side, ffn_line, ffn_finish, ffn_end = sum_dp(
        r.pre_s,
        ffn_part,
        r.fside_send,
        r.fside_got,
        r.fline_send,
        r.fline_got,
        m_base,
    )
    strip_side, strip_line, strip_finish, strip_end = sum_dp(
        r.strip_s,
        strip_part,
        r.sside_send,
        r.sside_got,
        r.sline_send,
        r.sline_got,
        m_base + 1 + n_z,
    )
    ffn_side()


    loop(1, middle, line_step)
    loop(middle + 1, n_z, line_step)
    grad_q = lowered(r.dq_s[...].T)
    lend.wait_recv()
    grad_united = jnp.concatenate(
        [
            grad_q,
            lowered(r.kv_s[0:span, :] + r.kv_got[0:span, :]),
            lowered(r.own_s[...] + r.kv_got[span:, :]),
        ],
        1,
    )
    grad_h0_norm, gain_grad1 = rms_back(r.h0_s[...], gain1, against(grad_united, r.wq16[...]))
    grad_h0 = r.h1_s[...] + grad_h0_norm
    r.h0_s[...] = grad_h0

    r.acc_s[:, : 3 * width] = across(r.n1_s[...], grad_united)

    strip = span // 4
    strip_rows = 6 * strip
    halves = (jnp.where(half == 0, 1.0, 0.0), jnp.where(half == 1, 1.0, 0.0))

    def pieces(s):
        rows = pl.ds(pl.multiple_of(here.member[s] * strip, strip), strip)
        for j in range(3):
            yield j * strip, r.acc_s[rows, j * width : (j + 1) * width]
        yield 3 * strip, r.acc_s[rows, 3 * width :]
        for u in range(2):
            yield (4 + u) * strip, r.h0_s[rows, :] * halves[u]

    for i, s in enumerate((1, 3)):
        for first, value in pieces(s):
            r.snear_send[i, first : first + strip, :] = lowered(value)
    s_near.start()

    o_base = wire.take(6)

    def chunk(s, column):
        return r.found.at[at(2 * s + column, span)]

    def row_copies(column):
        return (
            wire.make(chunk(0, column), chunk(2, column), o_base + 3 * column, here.ffn(2)),
            wire.make(chunk(0, column), chunk(1, column), o_base + 3 * column + 1, here.ffn(1)),
            wire.make(chunk(2, column), chunk(3, column), o_base + 3 * column + 2, here.ffn(1)),
        )

    in_far, in_near, in_relay = row_copies(0)
    out_far, out_near, out_relay = row_copies(1)
    ended += [in_far, in_near, in_relay, out_far, out_near, out_relay]
    r.found[0:span, :] = lowered(grad_h0)
    in_far.start()
    in_near.start()

    lane8 = iota((1, width), 1)
    row8 = iota((8, width), 0)
    stats = jnp.where(lane8 == 0, loss, 0.0)
    for i, number in enumerate((total_of(valid_lane), sum_hid, sum_attn, sum_ffn)):
        stats = jnp.where(lane8 == i + 1, number, stats)
    small = jnp.where(row8 == 0, gain_grad1, 0.0)
    small = jnp.where(row8 == 1, gain_grad2, small)
    small = jnp.where(row8 == 2, gain_grad3, small)
    r.small[0, 0] = jnp.where(row8 == 3, stats, small)
    l_base = wire.take(4)

    def to_members(row, base):
        return Group(
            *[
                wire.make(r.small.at[row, 0], r.small.at[row, s], base + s, here.ffn(s))
                for s in (1, 2, 3)
            ]
        )

    tell_small = to_members(0, l_base)
    tell_small.start()
    ended.append(tell_small)

    grad = cand_grad(0)
    s_near.wait_recv()
    for first, value in pieces(2):
        got = raised(r.snear_got[1, first : first + strip, :])
        r.sfar_send[first : first + strip, :] = lowered(value + got)
    s_far.start()
    ffn_line()
    cand_side(0).wait_send()
    cand_side(0).wait_recv()
    r.own_s[...] = (
        grad + raised(r.side_got[0]) - valid_col * raised(r.fin_s[0:span, :])
    )

    def add_line(k):
        cand_line(k).wait_recv()
        r.own_s[...] = r.own_s[...] + raised(r.line_got[k])

    loop(1, n_z, add_line)
    r.found[span : 2 * span, :] = lowered(r.own_s[...])
    out_far.start()
    out_near.start()

    in_far.wait_recv()
    in_relay.start()

    s_far.wait_recv()
    for first, value in pieces(0):
        rows = slice(first, first + strip)
        r.strip_s[rows, :] = (
            value + raised(r.snear_got[0, rows, :]) + raised(r.sfar_got[rows, :])
        )
    if n_dp * strip_part > strip_rows:
        r.strip_s[strip_rows:, :] = jnp.zeros((n_dp * strip_part - strip_rows, width), FULL)
    strip_side()

    order = here.y * n_z + here.z
    v_base = wire.take(2 * n_z + 2)

    def gather_dp(ref, size, base):
        own_part = ref.at[at(order, size)]
        own_column = ref.at[at(here.y, n_z * size)]

        def line(k):
            return wire.make(own_part, own_part, base + k, here.up(k))

        return line, wire.make(own_column, own_column, base + n_z, here.side())

    ffn_all, ffn_all_side = gather_dp(r.whole_f, ffn_part, v_base)
    strip_all, strip_all_side = gather_dp(r.whole_t, strip_part, v_base + n_z + 1)
    ended += [ffn_all_side, strip_all_side]
    mine = ffn_finish()
    squares = total_of(mine * mine)
    r.whole_f[at(order, ffn_part), :] = lowered(mine)
    each(1, n_z, lambda k: ffn_all(k).start())

    for s in range(4):
        for column in range(2):
            chunk_row = pl.ds(column * 4 + here.member[s], 1)
            r.p16_s[0:cap, (2 * s + column) * span : (2 * s + column + 1) * span] = lowered(
                one_hot_columns(r.slot_s[chunk_row, :], cap)
            )
    where_to = jnp.concatenate(
        [
            r.kind_s[pl.ds(column * 4 + here.member[s], 1), :]
            for s in range(4)
            for column in range(2)
        ],
        1,
    )
    where_to = lowered(jnp.broadcast_to(where_to, (16, 8 * span)))

    tell_small.wait_recv()
    r.small[1, 0] = (r.small[0, 0] + r.small[0, 1]) + (r.small[0, 2] + r.small[0, 3])
    h_base = wire.take(2 * n_dp)

    def share(row, k, number):
        return wire.make(
            r.small.at[row, 0], r.small_dp.at[row // 4, d], number + k, here.ahead(k)
        )

    each(1, n_dp, lambda k: share(1, k, h_base).start())
    r.small_dp[0, d] = r.small[1, 0]

    out_far.wait_recv()
    out_relay.start()

    strip_line()
    each(1, n_z, lambda k: ffn_all(k).wait_recv())
    ffn_all_side.start()

    in_near.wait_recv()
    in_relay.wait_recv()
    out_near.wait_recv()
    out_relay.wait_recv()

    g_base = wire.take(n_dp)

    def outgoing(k):
        return pl.ds(pl.multiple_of(8 * span + k * cap, cap), cap)

    def ship(k):
        return wire.make(
            r.found.at[outgoing(k)], r.incoming.at[at(k, cap)], g_base + k, here.ahead(k)
        )

    zero16 = jnp.zeros((16, 8 * span), LOW)

    def choose(k):
        wanted = where_to == lowered(jnp.full((16, 8 * span), k, FULL))
        picked = jnp.concatenate(
            [
                jnp.where(wanted, r.p16_s[i * 16 : (i + 1) * 16, :], zero16)
                for i in range(cap // 16)
            ],
            0,
        )
        return lowered(dot(picked, r.found[0 : 8 * span, :]))

    def fill_rows(k):
        r.found[outgoing(k), :] = choose(k)

    fill_rows(n_z)
    ship(n_z).start()
    loop(1, n_z, fill_rows)
    loop(n_z + 1, n_dp, fill_rows)

    mine = strip_finish()
    squares = squares + total_of(mine * mine)
    r.whole_t[at(order, strip_part), :] = lowered(mine)
    each(1, n_z, lambda k: strip_all(k).start())
    each(1, n_z, lambda k: ship(k).start())
    each(n_z + 1, n_dp, lambda k: ship(k).start())
    r.incoming[0:cap, :] = choose(0)

    several = min(n_dp, 8)

    def own_marks(g):
        for k in range(several):
            r.owned[:, k * 128 : (k + 1) * 128] = lowered(
                one_hot_columns(raised(r.asked[g * several + k]), rows_dev)
            )

    if n_dp == several:
        own_marks(0)

    each(1, n_z, lambda k: strip_all(k).wait_recv())
    strip_all_side.start()

    ffn_all_side.wait_recv()
    r.ffn_grad[...] = r.whole_f[0 : 2 * width, :]

    strip_all_side.wait_recv()
    r.strips[f] = r.whole_t[0:strip_rows, :]
    c_base = wire.take(3)
    mine_at, far_at = r.strips.at[f], r.strips.at[far]
    strip_far = wire.make(mine_at, mine_at, c_base, here.ffn(2))
    strip_near = wire.make(mine_at, mine_at, c_base + 1, here.ffn(1))
    strip_relay = wire.make(far_at, far_at, c_base + 2, here.ffn(1))
    ended += [strip_far, strip_near, strip_relay]
    strip_far.start()
    strip_near.start()

    each(1, n_dp, lambda k: ship(k).wait_recv())

    if n_dp == several:
        r.table_grad[...] = dot(r.owned[...], r.incoming[...])
    else:
        r.table_grad[...] = jnp.zeros((rows_dev, width), FULL)
        r.padded_in[...] = jnp.zeros_like(r.padded_in)

        def add_rows(g):
            own_marks(g)
            for k in range(several):
                r.padded_in[k * 128 : k * 128 + cap, :] = r.incoming[
                    at(g * several + k, cap), :
                ]
            r.table_grad[...] = r.table_grad[...] + dot(r.owned[...], r.padded_in[...])

        loop(0, n_dp // several, add_rows)
    table_grad = r.table_grad[...]
    squares = squares + total_of(table_grad * table_grad)

    r.small[3, 0] = jnp.broadcast_to(squares, (8, width))
    tell_norm = to_members(3, wire.take(4))
    tell_norm.start()
    ended.append(tell_norm)
    each(1, n_dp, lambda k: share(1, k, h_base).wait_recv())
    tell_norm.wait_recv()
    r.small[4, 0] = (r.small[3, 0] + r.small[3, 1]) + (r.small[3, 2] + r.small[3, 3])

    each(1, n_dp, lambda k: share(4, k, h_base + n_dp).start())
    r.small_dp[1, d] = r.small[4, 0]
    strip_far.wait_recv()
    strip_relay.start()
    each(1, n_dp, lambda k: share(4, k, h_base + n_dp).wait_recv())
    totals, squares = r.small_dp[0, 0], r.small_dp[1, 0]
    for k in range(1, n_dp):
        totals = totals + r.small_dp[0, k]
        squares = squares + r.small_dp[1, k]
    gains = jnp.where(row8 < 3, totals, 0.0)
    norm = jnp.sqrt(squares + total_of(gains * gains))
    r.sums[...] = jnp.where(row8 == 4, norm, totals)

    def end_dp(k):
        ask(k).wait_send()
        reply(k).wait_send()
        ship(k).wait_send()
        share(1, k, h_base).wait_send()
        share(4, k, h_base + n_dp).wait_send()

    each(1, n_dp, end_dp)

    def end_side(k):
        offer_side(k).wait_send()

    each(0, n_z, end_side)

    def end_line(k):
        offer_line(k).wait_send()
        cand_line(k).wait_send()
        ffn_all(k).wait_send()
        strip_all(k).wait_send()

    each(1, n_z, end_line)
    ffn_end()
    strip_end()
    strip_near.wait_recv()
    strip_relay.wait_recv()
    for copy in ended:
        copy.wait_send()


def step(n_dp, cap, owner, row, lengths, count, table, wq, wo, w_in, w_back, gains, positions):
    rows_dev, width = table.shape
    span = owner.shape[1] // 4
    heads = width // HD
    shapes = plan(n_dp, cap, rows_dev, span, width, heads)
    names = INPUTS + OUTPUTS + list(shapes) + ["load_sems", "send_sems", "recv_sems"]
    vmem = pl.BlockSpec(memory_space=pltpu.VMEM)
    smem = pl.BlockSpec(memory_space=pltpu.SMEM)
    rest = pl.BlockSpec(memory_space=pl.ANY)
    number = 20 * n_dp + 80

    def out(kind, *shape):
        return jax.ShapeDtypeStruct(shape, kind)

    return pl.pallas_call(
        functools.partial(step_kernel, n_dp, cap, names),
        out_shape=(
            out(FULL, rows_dev, width),
            out(LOW, 2 * width, width),
            out(LOW, 4, 6 * span // 4, width),
            out(FULL, 8, width),
        ),
        in_specs=[vmem, vmem, smem, vmem, rest, rest, rest, vmem, vmem, vmem, rest],
        out_specs=(vmem,) * 4,
        scratch_shapes=[pltpu.VMEM(shape[:-1], shape[-1]) for shape in shapes.values()]
        + [
            pltpu.SemaphoreType.DMA((4,)),
            pltpu.SemaphoreType.DMA((number,)),
            pltpu.SemaphoreType.DMA((number,)),
        ],
        compiler_params=pltpu.CompilerParams(
            collective_id=0,
            has_side_effects=True,
            vmem_limit_bytes=63 * MIB,
        ),
        name="step",
    )(owner, row, lengths, count, table, wq, wo, w_in, w_back, gains, positions)


STATES = 21
GAINS = 5


def jobs(rows_dev, width):
    quarter = -(-rows_dev // 32) * 8
    result = []
    for first in range(0, rows_dev, quarter):
        result.append((0, first, min(quarter, rows_dev - first)))
    return result + [(3, 0, width), (4, 0, width), (1, 0, width), (6, 0, 2 * width), (2, 0, width)]


def update_kernel(rows_dev, table_grad, ffn_grad, strips, sums, *refs):
    ins, refs = refs[:STATES], refs[STATES:]
    loss_out, rms_out, norm_out = refs[:3]
    outs, refs = refs[3 : 3 + STATES], refs[3 + STATES :]
    held, made, refs = refs[:18], refs[18:36], refs[36:]
    table_s, ffn_s, strips_s, grad_sems, in_sems, out_sems = refs
    width = sums.shape[1]
    work = jobs(rows_dev, width)

    def kept_at(which, i):
        return 3 * (which if which < GAINS else which - 1) + i

    def moves(number):
        which, first, rows = work[number]
        part = pl.ds(first, rows)
        here = [kept_at(which, i) for i in range(3)]
        return (
            [
                pltpu.make_async_copy(
                    ins[3 * which + i].at[part],
                    held[here[i]].at[part],
                    in_sems.at[number, i],
                )
                for i in range(3)
            ],
            [
                pltpu.make_async_copy(
                    made[here[i]].at[part],
                    outs[3 * which + i].at[part],
                    out_sems.at[number, i],
                )
                for i in range(3)
            ],
        )

    grads = [
        pltpu.make_async_copy(table_grad, table_s, grad_sems.at[0]),
        pltpu.make_async_copy(ffn_grad, ffn_s, grad_sems.at[1]),
        pltpu.make_async_copy(strips, strips_s, grad_sems.at[2]),
    ]
    grads[0].start()
    for number in range(len(work)):
        for copy in moves(number)[0]:
            copy.start()
        if number == 1:
            grads[1].start()
            grads[2].start()
    norm = sums[4:5, 0:1]
    factor = CLIP / jnp.maximum(norm, CLIP)
    corr_one = 1.0 - BETA_ONE**STEP
    corr_two = 1.0 - BETA_TWO**STEP

    def adam(which, rows, lanes, grad, rate):
        if which == GAINS:
            source, target = ins[3 * which : 3 * which + 3], outs[3 * which : 3 * which + 3]
        else:
            first = kept_at(which, 0)
            source, target = held[first : first + 3], made[first : first + 3]
        weight, moment, second = (ref[rows, lanes] for ref in source)
        clipped = raised(grad) * factor
        moment = BETA_ONE * moment + (1.0 - BETA_ONE) * clipped
        second = BETA_TWO * second + (1.0 - BETA_TWO) * clipped * clipped
        target[0][rows, lanes] = weight - rate * (
            moment / corr_one / (jnp.sqrt(second / corr_two) + ADAM_EPS) + DECAY * weight
        )
        target[1][rows, lanes] = moment
        target[2][rows, lanes] = second

    every = slice(None)
    strip = strips_s.shape[1] // 6
    waited = set()

    def need(i):
        if i not in waited:
            waited.add(i)
            grads[i].wait()

    for number, (which, first, rows) in enumerate(work):
        copies_in, copies_out = moves(number)
        need(0 if which == 0 else 1 if which in (3, 4) else 2)
        for copy in copies_in:
            copy.wait()
        if which == 0:
            part = slice(first, first + rows)
            adam(0, part, every, table_s[part, :], LEARN)
        elif which in (3, 4):
            start = (which - 3) * width
            adam(which, every, every, ffn_s[start : start + width, :], LEARN)
        for m in range(4):
            at_rows = slice(m * strip, (m + 1) * strip)
            if which == 1:
                for j in range(3):
                    lanes = slice(j * width, (j + 1) * width)
                    grad = strips_s[m, j * strip : (j + 1) * strip, :]
                    adam(1, at_rows, lanes, grad, LEARN)
            elif which == 2:
                adam(2, at_rows, every, strips_s[m, 3 * strip : 4 * strip, :], LEARN)
            elif which == 6:
                for u in range(2):
                    at_rows = slice((4 * u + m) * strip, (4 * u + m + 1) * strip)
                    grad = strips_s[m, (4 + u) * strip : (5 + u) * strip, :]
                    adam(6, at_rows, every, grad, LEARN)
        for copy in copies_out:
            copy.start()
    adam(GAINS, every, every, sums[0:3, :], GAIN_LEARN)
    stats = sums[3:4, :]
    roots = jnp.sqrt(stats / (stats[:, 1:2] * float(width)))

    def one(row, i):
        return jnp.sum(jnp.where(iota(row.shape, 1) == i, row, 0.0))

    loss_out[0] = one(stats, 0)
    loss_out[1] = one(stats, 1)
    for i in range(3):
        rms_out[i] = one(roots, 2 + i)
    norm_out[0] = one(sums[4:5, :], 0)
    for number in range(len(work)):
        for copy in moves(number)[1]:
            copy.wait()


def update(table_grad, ffn_grad, strips, sums, states):
    vmem = pl.BlockSpec(memory_space=pltpu.VMEM)
    smem = pl.BlockSpec(memory_space=pltpu.SMEM)
    rest = pl.BlockSpec(memory_space=pl.ANY)
    places = [vmem if i // 3 == GAINS else rest for i in range(STATES)]
    room = [pltpu.VMEM(a.shape, FULL) for i, a in enumerate(states) if i // 3 != GAINS]
    rows_dev, width = table_grad.shape
    number = len(jobs(rows_dev, width))
    return pl.pallas_call(
        functools.partial(update_kernel, rows_dev),
        out_shape=tuple(jax.ShapeDtypeStruct((n,), FULL) for n in (2, 3, 1))
        + tuple(jax.ShapeDtypeStruct(a.shape, FULL) for a in states),
        in_specs=[rest] * 3 + [vmem] + places,
        out_specs=[smem] * 3 + places,
        scratch_shapes=room
        + room
        + [pltpu.VMEM(a.shape, a.dtype) for a in (table_grad, ffn_grad, strips)]
        + [
            pltpu.SemaphoreType.DMA((3,)),
            pltpu.SemaphoreType.DMA((number, 3)),
            pltpu.SemaphoreType.DMA((number, 3)),
        ],
        compiler_params=pltpu.CompilerParams(vmem_limit_bytes=63 * MIB),
        name="update",
    )(table_grad, ffn_grad, strips, sums, *states)


def shards(
    item_owner,
    item_row,
    lengths,
    log_count,
    item_table,
    table_mom,
    table_sec,
    qkv_weight,
    qkv_mom,
    qkv_sec,
    out_weight,
    out_mom,
    out_sec,
    ffn_in,
    ffn_in_mom,
    ffn_in_sec,
    ffn_back,
    ffn_back_mom,
    ffn_back_sec,
    norm_gains,
    gains_mom,
    gains_sec,
    positions,
    positions_mom,
    positions_sec,
):
    n_dp = lax.axis_size("dp")
    tokens = item_owner.shape[0]
    cap = max(2, 4 * tokens // (n_dp * lax.axis_size("ffn")))
    table_grad, ffn_grad, strips, sums = step(
        n_dp,
        cap,
        item_owner.T,
        item_row.T,
        lengths,
        log_count,
        item_table,
        qkv_weight,
        out_weight,
        ffn_in,
        ffn_back,
        norm_gains,
        positions,
    )
    return update(
        table_grad,
        ffn_grad,
        strips,
        sums,
        (
            item_table,
            table_mom,
            table_sec,
            qkv_weight,
            qkv_mom,
            qkv_sec,
            out_weight,
            out_mom,
            out_sec,
            ffn_in,
            ffn_in_mom,
            ffn_in_sec,
            ffn_back,
            ffn_back_mom,
            ffn_back_sec,
            norm_gains,
            gains_mom,
            gains_sec,
            positions,
            positions_mom,
            positions_sec,
        ),
    )


def solution(mesh):
    whole, rows, table = P(), P("dp", None), P(("dp", "ffn"), None)
    wide, tall = P(None, "ffn"), P("ffn", None)
    states = (table,) * 3 + (whole,) * 6 + (wide,) * 3 + (tall,) * 3 + (whole,) * 6
    return jax.shard_map(
        shards,
        mesh=mesh,
        in_specs=(rows, rows, P("dp"), P(("dp", "ffn"))) + states,
        out_specs=(whole,) * 3 + states,
        check_vma=False,
    )
```

```python
import functools
import math
import types

import jax
import jax.numpy as jnp
from jax import lax
from jax.experimental import pallas as pl
from jax.experimental.pallas import tpu as pltpu
from jax.sharding import PartitionSpec as P

MESH = pl.DeviceIdType.MESH
MIB = 1024 * 1024
LOW, FULL = jnp.bfloat16, jnp.float32

EPS = 1e-06
NEG = -1e30
HD = 32
ROOT = math.sqrt(2.0 / math.pi)
LEARN = 0.05
GAIN_LEARN = 0.4
STEP = 5
BETA_ONE = 0.5
BETA_TWO = 0.5
DECAY = 0.01
ADAM_EPS = 1e-08
CLIP = 0.05


def lowered(value):
    return value.astype(LOW)


def raised(value):
    return value.astype(FULL)


def dot(left, right):
    return jnp.dot(left, right, preferred_element_type=FULL)


def against(left, right):
    return lax.dot_general(left, right, (((1,), (1,)), ((), ())), preferred_element_type=FULL)


def across(left, right):
    return lax.dot_general(left, right, (((0,), (0,)), ((), ())), preferred_element_type=FULL)


def iota(shape, dim):
    return lax.broadcasted_iota(jnp.int32, shape, dim)


def loop(first, last, body):
    def step(k, unused):
        body(k)
        return unused

    if last - first == 1:
        body(first)
    elif last > first:
        lax.fori_loop(first, last, step, 0)


def each(first, last, body):
    if last - first <= 8:
        for k in range(first, last):
            body(k)
    else:
        loop(first, last, body)


def at(index, size):
    if isinstance(index, int):
        return pl.ds(index * size, size)
    return pl.ds(pl.multiple_of(index * size, size), size)


def spread(row, lanes):
    return jnp.broadcast_to(row, (lanes, row.shape[1])).T


def turned(block):
    return lowered(raised(block).T)


def total_of(value):
    return jnp.sum(value, keepdims=True)


def one_hot_rows(row, width):
    high = jnp.floor(row * (1.0 / 128.0))
    low = spread(row - high * 128.0, 128)
    base = lowered(jnp.where(low == raised(iota(low.shape, 1)), 1.0, 0.0))
    high = lowered(spread(high, 128))
    zero = jnp.zeros_like(base)
    return jnp.concatenate(
        [jnp.where(high == jnp.asarray(b, LOW), base, zero) for b in range(width // 128)], 1
    )


def one_hot_columns(row, height):
    return jnp.where(raised(iota((height, row.shape[1]), 0)) == row, 1.0, 0.0)


def factor_of(hidden):
    return lax.rsqrt(jnp.mean(hidden * hidden, -1, keepdims=True) + EPS)


def rms_back(hidden, gain, upstream):
    factor = factor_of(hidden)
    scaled = upstream * gain
    inner = jnp.mean(scaled * hidden, -1, keepdims=True)
    grad_hidden = factor * scaled - hidden * (factor * factor * factor * inner)
    return grad_hidden, jnp.sum(upstream * hidden * factor, 0, keepdims=True)


class Peers:
    def __init__(self, n_dp):
        self.n_dp, self.n_z = n_dp, n_dp // 2
        self.d, self.f = lax.axis_index("dp"), lax.axis_index("ffn")
        self.z, self.y = self.d // 2, lax.rem(self.d, 2)
        near = self.f + 1 - 2 * lax.rem(self.f, 2)
        far = lax.rem(self.f + 2, 4)
        self.member = (self.f, near, far, 3 - self.f)

    def ffn(self, s):
        return (self.d, self.member[s])

    def ahead(self, i):
        return self.apart(i // self.n_z, i % self.n_z)

    def behind(self, i):
        return self.apart(i // self.n_z, self.n_z - i % self.n_z)

    def apart(self, ky, kz):
        z = lax.rem(self.z + kz, self.n_z)
        return (z * 2 + self.y + ky - 2 * self.y * ky, self.f)

    def side(self):
        return (self.d + 1 - 2 * self.y, self.f)

    def up(self, k):
        return (lax.rem(self.z + k, self.n_z) * 2 + self.y, self.f)

    def down(self, k):
        return (lax.rem(self.z + self.n_z - k, self.n_z) * 2 + self.y, self.f)

    def greet(self):
        barrier = pltpu.get_barrier_semaphore()

        def hello(where):
            pl.semaphore_signal(barrier, inc=1, device_id=where, device_id_type=MESH)

        for s in (1, 2, 3):
            hello(self.ffn(s))
        each(1, self.n_dp, lambda k: hello(self.ahead(k)))

    def met(self):
        pl.semaphore_wait(pltpu.get_barrier_semaphore(), self.n_dp + 2)


class Number:
    def __init__(self, leave, arrive, shared=False):
        self.leave, self.arrive, self.shared = leave, arrive, shared

    def __add__(self, k):
        return Number(self.leave if self.shared else self.leave + k, self.arrive + k, self.shared)


class Wire:
    def __init__(self, send, recv):
        self.send, self.recv = send, recv
        self.left, self.arrived, self.most = 0, 0, 0

    def take(self, number, arrivals=None, shared=False):
        result = Number(self.left, self.arrived, shared)
        self.left += 1 if shared else number
        self.arrived += number if arrivals is None else arrivals
        self.most = max(self.most, self.left)
        return result

    def renew(self):
        self.left = 0

    def make(self, src, dst, number, where, landing=None):
        return pltpu.make_async_remote_copy(
            src_ref=src,
            dst_ref=dst,
            send_sem=self.send.at[number.leave],
            recv_sem=self.recv.at[(landing or number).arrive],
            device_id=where,
            device_id_type=MESH,
        )


class Joined:
    def __init__(self, copies, all_of_them):
        self.copies, self.all = copies, all_of_them

    def start(self):
        for copy in self.copies:
            copy.start()

    def wait_recv(self):
        self.all.wait_recv()

    def wait_send(self):
        self.all.wait_send()


class Group:
    def __init__(self, *copies):
        self.copies = copies

    def start(self):
        for copy in self.copies:
            copy.start()

    def wait_recv(self):
        for copy in self.copies:
            copy.wait_recv()

    def wait_send(self):
        for copy in self.copies:
            copy.wait_send()


INPUTS = [
    "owner",
    "row",
    "lengths",
    "count",
    "table",
    "wq",
    "wo",
    "w_in",
    "w_back",
    "gains",
    "positions",
]
OUTPUTS = ["table_out", "ffn_out", "strips_out", "sums"]


def plan(n_dp, cap, rows_dev, span, width, heads):
    n_z = n_dp // 2
    filled = n_dp * cap
    padded = -(-rows_dev // 128) * 128
    square = (span, width)
    ffn_part, strip_part = parts(n_dp, span, width)
    return {
        "table_s": (rows_dev, width, FULL),
        "wq_s": (width, 3 * width, FULL),
        "wo_s": (width, width, FULL),
        "positions_s": (2 * span, width, FULL),
        "w_s": (2, width, width, FULL),
        "weights": (4, 2, width, width, LOW),
        "hot": (32 * n_dp, span, LOW),
        "slot_s": (8, span, FULL),
        "kind_s": (8, span, FULL),
        "table_low": (padded, width, LOW),
        "req": (n_dp, 1, 128, jnp.int32),
        "asked": (n_dp, 1, 128, jnp.int32),
        "send_rows": (n_dp, cap, width, LOW),
        "send_bias": (n_dp, 1, 128, FULL),
        "found": (4 * filled, width, LOW),
        "found_bias": (4 * n_dp, 1, 128, FULL),
        "bias_s": (8, span, FULL),
        "cands": (n_dp * span, width, LOW),
        "cand_bias": (n_dp, 8, span, FULL),
        "cand_t": (width, (n_dp if kept(n_dp) else 1) * span, LOW),
        "cand_col": ((n_dp if kept(n_dp) else 1) * span, 128, FULL),
        "logit_s": (6 * span if kept(n_dp) else 2 * span, span, FULL),
        "stat_s": (4, 8, span, FULL),
        "scale_s": (8, 4 * span, FULL),
        "expo_s": (n_dp * span if kept(n_dp) else 16, 4 * span, LOW),
        "wq16": (width, 3 * width, LOW),
        "wo16": (width, width, LOW),
        "h0_s": square + (FULL,),
        "n1_s": square + (LOW,),
        "q_s": square + (LOW,),
        "qt_s": (width, span, LOW),
        "k_s": (2 * span, width, LOW),
        "v_s": (2 * span, width, LOW),
        "kt_s": (width, 2 * span, LOW),
        "vt_s": (width, 2 * span, LOW),
        "mask_s": (2 * span, span, FULL),
        "p_s": (heads, 2 * span, span, FULL),
        "p16_s": (2 * span, heads * span, LOW),
        "stack_s": (heads * span, width, LOW),
        "mixt_s": (width, span, LOW),
        "h1_s": square + (FULL,),
        "h2_s": square + (FULL,),
        "n2t_s": (width, span, LOW),
        "pre_s": (4 * span, width, FULL),
        "act_s": (span, 4 * span, LOW),
        "fin_s": (4 * span, width, LOW),
        "fint_s": (width, 4 * span, LOW),
        "acc_s": (width, 4 * span, FULL),
        "acc_send": (3, width, span, LOW),
        "acc_got": (3, width, span, LOW),
        "mid_send": (3, 8, span, FULL),
        "mid_got": (3, 8, span, FULL),
        "tot_s": (4, 8, span, FULL),
        "cand_send": (n_z, span, width, LOW),
        "side_got": (n_z, span, width, LOW),
        "line_got": (n_z, span, width, LOW),
        "own_s": square + (FULL,),
        "dq_s": (width, span, FULL),
        "kv_s": (2 * span, width, FULL),
        "kv_got": (2 * span, width, FULL),
        "gf_s": (4, 2, width, width, FULL),
        "fnear_send": (2, 2 * width, width, LOW),
        "fnear_got": (2, 2 * width, width, LOW),
        "ffar_send": (2 * width, width, LOW),
        "ffar_got": (2 * width, width, LOW),
        "enear_send": (2, span // 2, width, LOW),
        "enear_got": (2, span // 2, width, LOW),
        "efar_send": (span // 2, width, LOW),
        "efar_got": (span // 2, width, LOW),
        "snear_send": (2, span, width, LOW),
        "snear_got": (2, span, width, LOW),
        "sfar_send": (span, width, LOW),
        "sfar_got": (span, width, LOW),
        "gv_s": square + (LOW,),
        "strip_s": (n_dp * strip_part, width, FULL),
        "fside_send": (n_z * ffn_part, width, LOW),
        "fside_got": (n_z * ffn_part, width, LOW),
        "fline_send": (n_z, ffn_part, width, LOW),
        "fline_got": (n_z, ffn_part, width, LOW),
        "sside_send": (n_z * strip_part, width, LOW),
        "sside_got": (n_z * strip_part, width, LOW),
        "sline_send": (n_z, strip_part, width, LOW),
        "sline_got": (n_z, strip_part, width, LOW),
        "whole_f": (n_dp * ffn_part, width, LOW),
        "whole_t": (n_dp * strip_part, width, LOW),
        "incoming": (filled, width, LOW),
        "place_s": (3 * span if kept(n_dp) else 16, 4 * filled if kept(n_dp) else 128, LOW),
        "placed_s": (3 * span if kept(n_dp) else 16, width, LOW),
        "pick_s": (filled if kept(n_dp) else 16, 8 * span, LOW),
        "padded_in": (8 * 128 if cap < 128 else 16, width, LOW),
        "owned": (rows_dev, min(n_dp, 8) * 128, LOW),
        "table_grad": (rows_dev, width, FULL),
        "strips": (4, 6 * span // 4, width, LOW),
        "small": (5, 4, 8, width, FULL),
        "small_dp": (2, n_dp, 8, width, FULL),
    }


def kept(n_dp):
    return n_dp <= 8


def parts(n_dp, span, width):
    return (
        -(-(2 * width + span // 2) // (16 * n_dp)) * 16,
        -(-span // (16 * n_dp)) * 16,
    )


def step_kernel(n_dp, cap, names, *refs):
    r = types.SimpleNamespace(**dict(zip(names, refs)))
    here = Peers(n_dp)
    wire = Wire(r.send_sems, r.recv_sems)
    d, f, n_z = here.d, here.f, here.n_z
    me, near, far, cross = here.member
    span, width = r.h0_s.shape
    heads = width // HD
    scale = HD ** (-0.5)
    half = lax.rem(f, 2)
    begin = half * span
    filled = n_dp * cap
    kinds = 4 * n_dp
    rows_dev = r.table_s.shape[0]
    padded = r.table_low.shape[0]
    ended = []

    here.greet()
    loads = [
        pltpu.make_async_copy(src, dst, r.load_sems.at[i])
        for i, (src, dst) in enumerate(
            (
                (r.table, r.table_s),
                (r.wq, r.wq_s),
                (r.wo, r.wo_s),
                (r.positions, r.positions_s),
                (r.w_in, r.w_s.at[0]),
                (r.w_back, r.w_s.at[1]),
            )
        )
    ]
    for i in (4, 5, 0, 1, 2, 3):
        loads[i].start()

    place = iota((kinds, span), 0)
    slot_of = jnp.zeros((kinds, span), jnp.int32)
    for s in (1, 2, 3):
        slot_of = slot_of + (place >= s * n_dp).astype(jnp.int32)
    steps = place - slot_of * n_dp
    other_y = (steps >= n_z).astype(jnp.int32)
    steps = steps - other_y * n_z + here.z
    steps = jnp.where(steps >= n_z, steps - n_z, steps)
    ahead = steps * 2 + here.y + other_y * (1 - 2 * here.y)
    named = ahead * 4 + jnp.where(
        slot_of == 0, me, jnp.where(slot_of == 1, near, jnp.where(slot_of == 2, far, cross))
    )

    def chunk_of(ref, c):
        return ref[c // 4 : c // 4 + 1, (c % 4) * span : (c % 4 + 1) * span]

    for c in range(8):
        r.hot[c * kinds : (c + 1) * kinds, :] = lowered(
            jnp.where(chunk_of(r.owner, c) == named, 1.0, 0.0)
        )
    before = lowered(jnp.where(iota((span, span), 0) < iota((span, span), 1), 1.0, 0.0))
    carry = jnp.zeros((kinds, 1), FULL)
    place_f = raised(place)
    asking = jnp.zeros((2 * n_dp, 128), FULL)
    for c in range(8):
        ones = raised(r.hot[c * kinds : (c + 1) * kinds, :])
        ranks = dot(r.hot[c * kinds : (c + 1) * kinds, :], before)
        slot = jnp.sum(ones * (ranks + carry), 0, keepdims=True)
        carry = carry + jnp.sum(ones, 1, keepdims=True)
        r.slot_s[c : c + 1, :] = slot
        r.kind_s[c : c + 1, :] = jnp.sum(ones * place_f, 0, keepdims=True)
        row = chunk_of(r.row, c)
        mine = ones[:n_dp]
        sought = jnp.concatenate([mine * raised(row >> 5), mine * raised(row & 31)], 0)
        asking = asking + against(lowered(sought), lowered(one_hot_columns(slot, 128)))
    wanted = (asking[:n_dp] * 32.0 + asking[n_dp:]).astype(jnp.int32)
    for k in range(n_dp):
        r.req[k, 0:1, :] = wanted[k : k + 1, :]
    r.asked[0] = r.req[0]
    q_base = wire.take(n_dp, shared=True)

    def ask(k):
        return wire.make(r.req.at[k], r.asked.at[k], q_base + k, here.ahead(k))

    here.met()
    each(1, n_dp, lambda k: ask(k).start())

    loads[4].wait()
    loads[5].wait()
    r.weights[0] = lowered(r.w_s[...])
    w_base = wire.take(3)
    w_near = wire.make(r.weights.at[0], r.weights.at[1], w_base, here.ffn(1))
    w_far = wire.make(r.weights.at[0], r.weights.at[2], w_base + 1, here.ffn(2))
    w_relay = wire.make(r.weights.at[2], r.weights.at[3], w_base + 2, here.ffn(1))
    w_far.start()
    w_near.start()

    def build_marks():
        for s in range(4):
            for column in range(2):
                chunk_row = pl.ds(column * 4 + here.member[s], 1)
                r.p16_s[0:cap, (2 * s + column) * span : (2 * s + column + 1) * span] = lowered(
                    one_hot_columns(r.slot_s[chunk_row, :], cap)
                )
        where_to = jnp.concatenate(
            [
                r.kind_s[pl.ds(column * 4 + here.member[s], 1), :]
                for s in range(4)
                for column in range(2)
            ],
            1,
        )
        where_to = lowered(jnp.broadcast_to(where_to, (16, 8 * span)))
        return where_to

    zero16 = jnp.zeros((16, 8 * span), LOW)

    def picks(where_to, k):
        wanted = where_to == lowered(jnp.full((16, 8 * span), k, FULL))
        return jnp.concatenate(
            [
                jnp.where(wanted, r.p16_s[i * 16 : (i + 1) * 16, :], zero16)
                for i in range(cap // 16)
            ],
            0,
        )

    def key_of(column, quarter):
        chunk = pl.ds(column * 4 + quarter, 1)
        return r.kind_s[chunk, :] * float(cap) + r.slot_s[chunk, :]

    if kept(n_dp):
        marks_to = build_marks()

        def keep_picks(k):
            r.pick_s[at(k, cap), :] = picks(marks_to, k)

        loop(0, n_dp, keep_picks)
        for i, (column, quarter) in enumerate(((1, f), (0, f), (0, near))):
            r.place_s[at(i, span), :] = one_hot_rows(key_of(column, quarter), 4 * filled)

    loads[0].wait()
    r.table_low[0:rows_dev, :] = lowered(r.table_s[...])
    if padded > rows_dev:
        r.table_low[rows_dev:padded, :] = jnp.zeros((padded - rows_dev, width), LOW)
    counts = lowered(jnp.broadcast_to(raised(r.count[...].reshape(1, rows_dev)), (8, rows_dev)))
    if padded > rows_dev:
        counts = jnp.concatenate([counts, jnp.zeros((8, padded - rows_dev), LOW)], 1)
    r_base, b_base = wire.take(n_dp, shared=True), wire.take(1)
    others = pl.ds(1, n_dp - 1)

    def reply(k):
        return wire.make(r.send_rows.at[k], r.found.at[at(k, cap)], r_base + k, here.behind(k))

    def reply_bias(k):
        return wire.make(r.send_bias.at[k], r.found_bias.at[k], b_base, here.behind(k))

    def all_replies():
        rest = r.found.at[pl.ds(cap, filled - cap)]
        return wire.make(r.send_rows.at[others], rest, r_base, here.side())

    def all_biases():
        return wire.make(r.send_bias.at[others], r.found_bias.at[others], b_base, here.side())

    def fetch(k):
        chosen = one_hot_rows(raised(r.asked[k]), padded)
        return lowered(dot(chosen, r.table_low[...]))[:cap], against(counts, chosen)[0:1, :]

    def serve(k):
        ask(k).wait_recv()
        rows, bias = fetch(k)
        r.send_rows[k] = rows
        r.send_bias[k] = bias
        reply(k).start()
        reply_bias(k).start()

    loop(1, n_dp, serve)
    rows, bias = fetch(0)
    r.found[0:cap, :] = rows
    r.found_bias[0] = bias
    cuts = [(k, 1) for k in range(n_dp)]
    passes = [wire.take(len(cuts), shared=True) for i in range(3)]
    bias_passes = [wire.take(1) for i in range(3)]

    def pass_on(i, source, target, number, who):
        sem = bias_passes[number] if i == len(cuts) else passes[number] + i
        if i == len(cuts):
            src, dst = (r.found_bias.at[at(slot, n_dp)] for slot in (source, target))
        else:
            first, several = cuts[i]
            src, dst = (
                r.found.at[pl.ds((slot * n_dp + first) * cap, several * cap)]
                for slot in (source, target)
            )
        return wire.make(src, dst, sem, here.ffn(who))

    def all_passes(source, number):
        rows = r.found.at[at(source, filled)]
        return wire.make(rows, rows, passes[number], here.side())

    def to_far(i):
        return pass_on(i, 0, 2, 0, 2)

    def to_near(i):
        return pass_on(i, 0, 1, 1, 1)

    def relay(i):
        return pass_on(i, 2, 3, 2, 1)

    def take_on(i):
        first, several = cuts[i]
        for k in range(max(first, 1), first + several):
            reply(k).wait_recv()
        to_far(i).start()
        to_near(i).start()

    def relay_on(i):
        to_far(i).wait_recv()
        relay(i).start()

    for i in range(len(cuts)):
        take_on(i)
        if i > 1:
            relay_on(i - 2)
    all_biases().wait_recv()
    to_far(len(cuts)).start()
    to_near(len(cuts)).start()
    w_far.wait_recv()
    w_relay.start()
    for i in range(len(cuts) - 2, len(cuts) + 1):
        relay_on(i)
    loads[1].wait()
    loads[2].wait()
    r.wq16[...] = lowered(r.wq_s[...])
    r.wo16[...] = lowered(r.wo_s[...])
    for i in range(len(cuts)):
        to_near(i).wait_recv()
        relay(i).wait_recv()

    if kept(n_dp):
        r.placed_s[...] = lowered(dot(r.place_s[...], r.found[...]))

    def chosen_rows(i):
        if kept(n_dp):
            return r.placed_s[at(i, span), :]
        column, quarter = ((1, f), (0, f), (0, near))[i]
        return lowered(dot(one_hot_rows(key_of(column, quarter), 4 * filled), r.found[...]))

    r.cands[0:span, :] = chosen_rows(0)
    to_near(len(cuts)).wait_recv()
    relay(len(cuts)).wait_recv()
    bias_rows = lowered(r.found_bias[:, 0, :].T)
    lane = iota((1, span), 1)
    length = r.lengths[f // 2]
    valid_lane = jnp.where(lane + begin < length, 1.0, 0.0)
    valid_col = jnp.where(iota((span, 1), 0) + begin < length, 1.0, 0.0)
    chunk = 4 + f
    marks = one_hot_columns(r.slot_s[pl.ds(chunk, 1), :], 128)
    bias = jnp.sum(dot(bias_rows, r.hot[at(chunk, kinds), :]) * marks, 0, keepdims=True)
    r.bias_s[...] = jnp.broadcast_to(bias, (8, span))
    r.cand_bias[0] = jnp.broadcast_to(jnp.where(lane + begin < length, -bias, NEG), (8, span))
    z_base, y_base = wire.take(0, 2 * n_z), wire.take(2 * n_z)
    u_base = wire.take(4 * n_z, 0)
    has_up, has_down = here.z + 1 < n_z, here.z > 0

    def slot(k, ky):
        if isinstance(k, int) and k == 0:
            return ky
        return 1 + k + ky * (n_z - 1)

    def offer_line(source, target, number, where):
        i, j = slot(source, 0), slot(target, 0)
        return Group(
            wire.make(
                r.cands.at[at(i, span)], r.cands.at[at(j, span)], number, where, z_base + target
            ),
            wire.make(
                r.cand_bias.at[i],
                r.cand_bias.at[j],
                number + 2 * n_z,
                where,
                z_base + n_z + target,
            ),
        )

    def send_up(a):
        return offer_line(a, a + 1, u_base + a, here.up(1))

    def send_down(b):
        source = b if isinstance(b, int) and b == 0 else n_z - b
        return offer_line(source, n_z - 1 - b, u_base + n_z + b, here.down(1))

    def offer_side(k):
        i, j = slot(k, 0), slot(k, 1)
        return Group(
            wire.make(r.cands.at[at(i, span)], r.cands.at[at(j, span)], y_base + k, here.side()),
            wire.make(r.cand_bias.at[i], r.cand_bias.at[j], y_base + n_z + k, here.side()),
        )

    offer_side(0).start()
    pl.when(has_up)(lambda: send_up(0).start())
    pl.when(has_down)(lambda: send_down(0).start())

    def hand_on(j):
        @pl.when(here.z >= j)
        def from_below():
            offer_line(0, j, u_base, here.up(1)).wait_recv()
            pl.when(has_up)(lambda: send_up(j).start())
            offer_side(j).start()

        @pl.when(here.z + j < n_z)
        def from_above():
            offer_line(0, n_z - j, u_base, here.up(1)).wait_recv()
            pl.when(has_down)(lambda: send_down(j).start())
            offer_side(n_z - j).start()

    loads[3].wait()
    gain1, gain2, gain3 = r.gains[0:1, :], r.gains[1:2, :], r.gains[2:3, :]
    hidden0 = raised(chosen_rows(1)) + r.positions_s[at(half, span), :]
    r.h0_s[...] = hidden0
    normed1 = lowered(hidden0 * factor_of(hidden0) * gain1)
    r.n1_s[...] = normed1
    r.q_s[...] = lowered(dot(normed1, r.wq16[:, :width]))
    r.k_s[0:span, :] = lowered(dot(normed1, r.wq16[:, width : 2 * width]))
    r.v_s[0:span, :] = lowered(dot(normed1, r.wq16[:, 2 * width :]))
    hidden0 = raised(chosen_rows(2)) + r.positions_s[at(1 - half, span), :]
    normed1 = lowered(hidden0 * factor_of(hidden0) * gain1)
    r.k_s[span:, :] = lowered(dot(normed1, r.wq16[:, width : 2 * width]))
    r.v_s[span:, :] = lowered(dot(normed1, r.wq16[:, 2 * width :]))
    r.qt_s[...] = turned(r.q_s[...])
    r.kt_s[...] = turned(r.k_s[...])
    r.vt_s[...] = turned(r.v_s[...])
    key_at = iota((2 * span, span), 0)
    key_at = jnp.where(key_at < span, key_at + begin, key_at - begin)
    allowed = (key_at <= iota((2 * span, span), 1) + begin) & (key_at < length)
    r.mask_s[...] = jnp.where(allowed, 0.0, NEG)
    row_head = iota((width, span), 0) // HD
    lane_head = iota((span, width), 1) // HD

    def forward_head(h):
        rows = at(h, HD)
        mine = jnp.where(row_head == h, raised(r.qt_s[...]), 0.0)
        scores = dot(r.k_s[...], lowered(mine)) * scale + r.mask_s[...]
        expo = jnp.exp(scores - jnp.max(scores, 0, keepdims=True))
        probs = expo / jnp.sum(expo, 0, keepdims=True)
        r.p_s[h] = probs
        low_probs = lowered(probs)
        r.p16_s[:, at(h, span)] = low_probs
        r.mixt_s[rows, :] = lowered(dot(r.vt_s[rows, :], low_probs))

    loop(0, heads * 3 // 4, forward_head)
    hand_on(1)
    loop(heads * 3 // 4, heads, forward_head)
    attn = dot(turned(r.mixt_s[...]), r.wo16[...])
    hidden1 = r.h0_s[...] + attn
    r.h1_s[...] = hidden1
    sum_attn = total_of(valid_col * attn * attn)
    normed2 = lowered(hidden1 * factor_of(hidden1) * gain2)
    r.n2t_s[...] = turned(normed2)
    w_near.wait_recv()
    w_relay.wait_recv()
    for s in range(4):
        pre = dot(normed2, r.weights[s, 0])
        r.pre_s[s * span : (s + 1) * span, :] = pre
        inner = jnp.tanh(ROOT * (pre + 0.044715 * pre * pre * pre))
        r.act_s[:, s * span : (s + 1) * span] = lowered(0.5 * pre * (1.0 + inner))
    branch = dot(r.act_s[...], jnp.concatenate([r.weights[s, 1] for s in range(4)], 0))
    hidden2 = r.h1_s[...] + branch
    r.h2_s[...] = hidden2
    sum_ffn = total_of(valid_col * branch * branch)
    sum_hid = total_of(valid_col * hidden2 * hidden2)
    final = lowered(hidden2 * factor_of(hidden2) * gain3)
    r.fin_s[0:span, :] = final
    f_base = wire.take(3)
    fin = [r.fin_s.at[at(s, span)] for s in range(4)]
    fin_near = wire.make(fin[0], fin[1], f_base, here.ffn(1))
    fin_far = wire.make(fin[0], fin[2], f_base + 1, here.ffn(2))
    fin_relay = wire.make(fin[2], fin[3], f_base + 2, here.ffn(1))
    fin_far.start()
    fin_near.start()
    ended += [fin_far, fin_near, fin_relay]

    def turn_fin(s):
        r.fint_s[:, s * span : (s + 1) * span] = turned(r.fin_s[s * span : (s + 1) * span, :])

    turn_fin(0)
    if n_z > 2:
        hand_on(2)

    def prepare(i):
        if kept(n_dp):
            r.cand_t[:, at(i, span)] = turned(r.cands[at(i, span), :])
            r.cand_col[at(i, span), :] = spread(r.cand_bias[i, 0:1, :], 128)

    def columns(i, number):
        if kept(n_dp):
            return r.cand_col[slots(i, number), :]
        rows = [spread(r.cand_bias[i + j, 0:1, :], 128) for j in range(number)]
        return jnp.concatenate(rows, 0)

    def slots(i, number):
        if isinstance(i, int):
            return pl.ds(i * span, number * span)
        return pl.ds(pl.multiple_of(i * span, span), number * span)

    prepare(0)
    offer_side(0).wait_recv()
    prepare(1)
    r.acc_s[...] = jnp.zeros_like(r.acc_s)
    for s in range(4):
        r.stat_s[s, 0:1, :] = jnp.full((1, span), NEG, FULL)
        r.stat_s[s, 1:2, :] = jnp.zeros((1, span), FULL)

    def count_in(s, i, number, group):
        lanes = slice(s * span, (s + 1) * span)
        rows = slots(i, number)
        first = s % 2 * 3 * span if kept(n_dp) else 0
        held = slice(first, first + number * span)
        logits = dot(r.cands[rows, :], r.fint_s[:, lanes])
        r.logit_s[held, :] = logits + jnp.concatenate([columns(i, number)] * (span // 128), 1)
        top = r.stat_s[s, 0:1, :]
        higher = jnp.maximum(top, jnp.max(r.logit_s[held, :], 0, keepdims=True))
        shrink = jnp.exp(top - higher)
        expo = jnp.exp(r.logit_s[held, :] - higher)
        r.stat_s[s, 0:1, :] = higher
        r.stat_s[s, 1:2, :] = r.stat_s[s, 1:2, :] * shrink + jnp.sum(expo, 0, keepdims=True)
        if kept(n_dp):
            low_expo = lowered(expo)
            r.expo_s[rows, lanes] = low_expo
            r.stat_s[s, 2 + group : 3 + group, :] = higher
            part = dot(r.cand_t[:, rows], low_expo)
        else:
            part = across(r.cands[rows, :], lowered(expo))
        r.acc_s[:, lanes] = r.acc_s[:, lanes] * shrink + part

    def count(s, group):
        first = (0, 2, n_z + 1)[group]
        number = (2, n_z - 1, n_z - 1)[group]
        if number <= 3:
            if number:
                count_in(s, first, number, group)
        else:
            loop(first, first + number, lambda i: count_in(s, i, 1, group))

    count(0, 0)
    fin_near.wait_recv()
    turn_fin(1)
    count(1, 0)
    fin_far.wait_recv()
    fin_relay.start()
    turn_fin(2)
    count(2, 0)
    fin_relay.wait_recv()
    turn_fin(3)
    count(3, 0)
    loop(3, n_z, hand_on)
    loop(2, n_z + 1, prepare)
    count(3, 1)
    count(2, 1)
    count(0, 1)
    count(1, 1)

    def prepare_side(k):
        offer_side(k).wait_recv()
        prepare(slot(k, 1))

    loop(1, n_z, prepare_side)

    a_base = wire.take(6)

    def give(i, who):
        return Group(
            wire.make(r.acc_send.at[i], r.acc_got.at[i], a_base + 2 * i, here.ffn(who)),
            wire.make(r.mid_send.at[i], r.mid_got.at[i], a_base + 2 * i + 1, here.ffn(who)),
        )

    gives = [give(0, 1), give(1, 1), give(2, 2)]
    ended += gives

    def fill(i, s):
        r.acc_send[i] = lowered(r.acc_s[:, s * span : (s + 1) * span])
        r.mid_send[i] = r.stat_s[s]
        gives[i].start()

    def merge(s, i):
        gives[i].wait_recv()
        lanes = slice(s * span, (s + 1) * span)
        top, other = r.stat_s[s, 0:1, :], r.mid_got[i, 0:1, :]
        higher = jnp.maximum(top, other)
        left, right = jnp.exp(top - higher), jnp.exp(other - higher)
        r.acc_s[:, lanes] = r.acc_s[:, lanes] * left + raised(r.acc_got[i]) * right
        r.stat_s[s, 0:1, :] = higher
        r.stat_s[s, 1:2, :] = r.stat_s[s, 1:2, :] * left + r.mid_got[i, 1:2, :] * right

    count(3, 2)
    fill(0, 3)
    count(2, 2)
    merge(2, 0)
    fill(2, 2)
    count(1, 2)
    fill(1, 1)
    count(0, 2)
    merge(0, 1)
    merge(0, 2)
    total = r.stat_s[0, 1:2, :]
    log_total = r.stat_s[0, 0:1, :] + jnp.log(total)
    r.tot_s[0] = jnp.broadcast_to(jnp.where(valid_lane > 0, log_total, -NEG), (8, span))
    for copy in (
        all_passes(0, 0),
        all_passes(0, 1),
        all_passes(2, 2),
        to_far(len(cuts)),
        to_near(len(cuts)),
        relay(len(cuts)),
    ):
        copy.wait_send()

    t_base = wire.take(1)

    def to_members(ref, number):
        three = ref.at[pl.ds(1, 3)]
        return Joined(
            [wire.make(ref.at[0], ref.at[s], number, here.ffn(s)) for s in (1, 2, 3)],
            wire.make(three, three, number, here.side()),
        )

    tell = to_members(r.tot_s, t_base)
    tell.start()
    ended.append(tell)
    if not kept(n_dp):
        r.cand_t[...] = turned(r.cands[0:span, :])
    target_t = raised(r.cand_t[:, 0:span])
    positive = (
        jnp.sum(raised(r.fint_s[:, :span]) * target_t, 0, keepdims=True) - r.bias_s[0:1, :]
    )
    loss = total_of(valid_lane * (log_total - positive))
    grad_final = ((r.acc_s[:, 0:span] / total - target_t) * valid_lane).T

    grad_h2, gain_grad3 = rms_back(r.h2_s[...], gain3, grad_final)
    up = lowered(grad_h2)
    r.h2_s[...] = grad_h2
    for s in (1, 3, 2, 0):
        lanes = slice(s * span, (s + 1) * span)
        r.gf_s[s, 1] = across(r.act_s[:, lanes], up)
        grad_act = against(up, r.weights[s, 1])
        pre = r.pre_s[s * span : (s + 1) * span, :]
        inner = jnp.tanh(ROOT * (pre + 0.044715 * pre * pre * pre))
        slope = 0.5 * (1.0 + inner) + 0.5 * pre * (1.0 - inner * inner) * (
            ROOT * (1.0 + 3.0 * 0.044715 * pre * pre)
        )
        grad_pre = lowered(grad_act * slope)
        r.gf_s[s, 0] = dot(r.n2t_s[...], grad_pre)
        r.act_s[:, lanes] = grad_pre
    for i, s in enumerate((1, 3)):
        for j in range(2):
            r.fnear_send[i, j * width : (j + 1) * width, :] = lowered(r.gf_s[s, j])
    all_asks = wire.make(r.req.at[others], r.req.at[others], q_base, here.side())
    for copy in (all_asks, all_replies(), all_biases(), w_far, w_near, w_relay):
        copy.wait_send()
    def end_offers(j):
        pl.when(has_up & (here.z >= j))(lambda: send_up(j).wait_send())
        pl.when(has_down & (here.z + j < n_z))(lambda: send_down(j).wait_send())

    each(0, n_z, end_offers)
    each(0, n_z, lambda k: offer_side(k).wait_send())
    for copy in ended:
        copy.wait_send()
    ended.clear()
    wire.renew()
    e_base = wire.take(6)
    f_near = wire.make(r.fnear_send, r.fnear_got, e_base, here.ffn(1))
    f_far = wire.make(r.ffar_send, r.ffar_got, e_base + 1, here.ffn(2))
    s_near = wire.make(r.snear_send, r.snear_got, e_base + 2, here.ffn(1))
    s_far = wire.make(r.sfar_send, r.sfar_got, e_base + 3, here.ffn(2))
    e_near = wire.make(r.enear_send, r.enear_got, e_base + 4, here.ffn(1))
    e_far = wire.make(r.efar_send, r.efar_got, e_base + 5, here.ffn(2))
    ended += [f_near, f_far, s_near, s_far, e_near, e_far]
    f_near.start()

    tell.wait_recv()
    if kept(n_dp):
        for s in range(4):
            for group in range(3):
                level = r.stat_s[s, 2 + group : 3 + group, :] - r.tot_s[s, 0:1, :]
                r.scale_s[group : group + 1, s * span : (s + 1) * span] = jnp.exp(level)
    side_base, line_base = wire.take(n_z), wire.take(n_z)

    def cand_side(k):
        return wire.make(r.cand_send.at[k], r.side_got.at[k], side_base + k, here.side())

    def cand_line(k):
        return wire.make(r.cand_send.at[k], r.line_got.at[k], line_base + k, here.down(k))

    def cand_grad(i):
        if kept(n_dp):
            group = jnp.where(i < 2, 0, jnp.where(i <= n_z, 1, 2))
            share_of = r.scale_s[pl.ds(group, 1), :]
            weights = raised(r.expo_s[at(i, span), :]) * share_of
            return dot(lowered(weights), r.fin_s[...])
        column = jnp.concatenate([columns(i, 1)] * (4 * span // 128), 1)
        level = jnp.concatenate([r.tot_s[s, 0:1, :] for s in range(4)], 1)
        logits = dot(r.cands[at(i, span), :], r.fint_s[...]) + column
        return dot(lowered(jnp.exp(logits - level)), r.fin_s[...])

    def slot_at(k, ky):
        return jnp.where(k == 0, ky, 1 + k + ky * (n_z - 1))

    def side_step(k):
        r.cand_send[k] = lowered(cand_grad(slot_at(k, 1)))
        cand_side(k).start()

    def line_step(k):
        grad = cand_grad(slot_at(k, 0))
        cand_side(k).wait_send()
        cand_side(k).wait_recv()
        r.cand_send[k] = lowered(grad + raised(r.side_got[k]))
        cand_line(k).start()

    middle = n_z // 2
    side_step(middle)
    loop(1, middle, side_step)
    loop(middle + 1, n_z, side_step)
    if middle:
        side_step(0)

    grad_normed2 = against(
        r.act_s[...], jnp.concatenate([r.weights[s, 0] for s in range(4)], 1)
    )
    grad_h1_norm, gain_grad2 = rms_back(r.h1_s[...], gain2, grad_normed2)
    grad_h1 = r.h2_s[...] + grad_h1_norm
    r.h1_s[...] = grad_h1
    f_near.wait_recv()
    for j in range(2):
        rows = slice(j * width, (j + 1) * width)
        r.ffar_send[rows, :] = lowered(r.gf_s[2, j] + raised(r.fnear_got[1, rows, :]))
    f_far.start()

    attn_up = lowered(grad_h1)
    r.acc_s[:, 3 * width :] = dot(r.mixt_s[...], attn_up)
    grad_mixed = lowered(against(attn_up, r.wo16[...]))
    grad_mixed_f = raised(grad_mixed)
    r.mixt_s[...] = turned(grad_mixed)
    for h in range(heads):
        r.stack_s[h * span : (h + 1) * span, :] = lowered(
            jnp.where(lane_head == h, grad_mixed_f, 0.0)
        )
    r.kv_s[...] = dot(r.p16_s[...], r.stack_s[...])
    r.logit_s[span : 2 * span, :] = r.kv_s[span:, :]
    r.own_s[...] = r.kv_s[0:span, :]
    k_base = wire.take(2)

    def lend(i):
        rows = at(i, span)
        return wire.make(r.logit_s.at[rows], r.kv_got.at[rows], k_base + i, here.ffn(1))

    lend_k, lend_v = lend(0), lend(1)
    ended += [lend_k, lend_v]
    lend_v.start()

    def backward_head(h):
        rows = at(h, HD)
        mine = jnp.where(row_head == h, raised(r.mixt_s[...]), 0.0)
        grad_probs = dot(r.v_s[...], lowered(mine))
        probs = r.p_s[h]
        inner = jnp.sum(probs * grad_probs, 0, keepdims=True)
        grad_scores = lowered(probs * (grad_probs - inner))
        r.p16_s[:, at(h, span)] = grad_scores
        r.dq_s[rows, :] = dot(r.kt_s[rows, :], grad_scores) * scale

    loop(0, heads // 2, backward_head)
    if middle:
        line_step(middle)
    strip = span // 4
    halves = (jnp.where(half == 0, 1.0, 0.0), jnp.where(half == 1, 1.0, 0.0))

    def strip_at(s):
        return pl.ds(pl.multiple_of(here.member[s] * strip, strip), strip)

    def early_pieces(s):
        yield 0, r.acc_s[strip_at(s), 3 * width :]
        yield strip, r.acc_s[strip_at(s), 2 * width : 3 * width]

    def pieces(s):
        for j in range(2):
            yield j * strip, r.acc_s[strip_at(s), j * width : (j + 1) * width]
        for u in range(2):
            yield (2 + u) * strip, r.h0_s[strip_at(s), :] * halves[u]

    lend_v.wait_recv()
    r.gv_s[...] = lowered(r.own_s[...] + r.kv_got[span:, :])
    r.acc_s[:, 2 * width : 3 * width] = across(r.n1_s[...], r.gv_s[...])
    for i, s in enumerate((1, 3)):
        for first, value in early_pieces(s):
            r.enear_send[i, first : first + strip, :] = lowered(value)
    e_near.start()
    loop(heads // 2, heads, backward_head)
    loop(1, middle, line_step)
    e_near.wait_recv()
    for first, value in early_pieces(2):
        got = raised(r.enear_got[1, first : first + strip, :])
        r.efar_send[first : first + strip, :] = lowered(value + got)
    e_far.start()
    queries = raised(r.q_s[...])
    for h in range(heads):
        r.stack_s[h * span : (h + 1) * span, :] = lowered(jnp.where(lane_head == h, queries, 0.0))
    r.kv_s[...] = dot(r.p16_s[...], r.stack_s[...]) * scale
    r.logit_s[0:span, :] = r.kv_s[span:, :]
    lend_k.start()
    loop(middle + 1, n_z, line_step)
    r.h2_s[...] = cand_grad(0)
    ffn_part, strip_part = parts(n_dp, span, width)
    f_far.wait_recv()
    for j in range(2):
        rows = slice(j * width, (j + 1) * width)
        r.pre_s[rows, :] = (
            r.gf_s[0, j] + raised(r.fnear_got[0, rows, :]) + raised(r.ffar_got[rows, :])
        )
    e_far.wait_recv()
    early_rows = 2 * width + 2 * strip
    for first, value in early_pieces(0):
        rows = slice(first, first + strip)
        r.pre_s[2 * width + first : 2 * width + first + strip, :] = (
            value + raised(r.enear_got[0, rows, :]) + raised(r.efar_got[rows, :])
        )
    if n_dp * ffn_part > early_rows:
        r.pre_s[early_rows : n_dp * ffn_part, :] = jnp.zeros(
            (n_dp * ffn_part - early_rows, width), FULL
        )
    m_base = wire.take(2 + 2 * n_z)

    def sum_dp(source, size, side_send, side_got, line_send, line_got, base):
        def rows_of(k, y):
            return at(y * n_z + lax.rem(here.z + k, n_z), size)

        across_y = wire.make(side_send, side_got, base, here.side())

        def along(k):
            return wire.make(line_send.at[k], line_got.at[k], base + 1 + k, here.up(k))

        def begin_side():
            def fill_side(k):
                side_send[at(k, size), :] = lowered(source[rows_of(k, 1 - here.y), :])

            loop(0, n_z, fill_side)
            across_y.start()

        def begin_line():
            across_y.wait_recv()

            def fill_line(k):
                line_send[k] = lowered(
                    source[rows_of(k, here.y), :] + raised(side_got[at(k, size), :])
                )
                along(k).start()

            loop(1, n_z, fill_line)

        def finish():
            value = source[rows_of(0, here.y), :] + raised(side_got[0:size, :])
            for k in range(1, n_z):
                along(k).wait_recv()
                value = value + raised(line_got[k])
            return value

        def end():
            across_y.wait_send()
            each(1, n_z, lambda k: along(k).wait_send())

        return begin_side, begin_line, finish, end

    ffn_side, ffn_line, ffn_finish, ffn_end = sum_dp(
        r.pre_s,
        ffn_part,
        r.fside_send,
        r.fside_got,
        r.fline_send,
        r.fline_got,
        m_base,
    )
    strip_side, strip_line, strip_finish, strip_end = sum_dp(
        r.strip_s,
        strip_part,
        r.sside_send,
        r.sside_got,
        r.sline_send,
        r.sline_got,
        m_base + 1 + n_z,
    )
    ffn_side()


    grad_q = lowered(r.dq_s[...].T)
    lend_k.wait_recv()
    grad_qk = jnp.concatenate(
        [grad_q, lowered(r.kv_s[0:span, :] + r.kv_got[0:span, :])],
        1,
    )
    grad_united = jnp.concatenate([grad_qk, r.gv_s[...]], 1)
    grad_h0_norm, gain_grad1 = rms_back(r.h0_s[...], gain1, against(grad_united, r.wq16[...]))
    grad_h0 = r.h1_s[...] + grad_h0_norm
    r.h0_s[...] = grad_h0

    r.acc_s[:, : 2 * width] = across(r.n1_s[...], grad_qk)

    for i, s in enumerate((1, 3)):
        for first, value in pieces(s):
            r.snear_send[i, first : first + strip, :] = lowered(value)
    s_near.start()

    o_base = wire.take(6)

    def chunk(s, column):
        return r.found.at[at(2 * s + column, span)]

    def row_copies(column):
        return (
            wire.make(chunk(0, column), chunk(2, column), o_base + 3 * column, here.ffn(2)),
            wire.make(chunk(0, column), chunk(1, column), o_base + 3 * column + 1, here.ffn(1)),
            wire.make(chunk(2, column), chunk(3, column), o_base + 3 * column + 2, here.ffn(1)),
        )

    in_far, in_near, in_relay = row_copies(0)
    out_far, out_near, out_relay = row_copies(1)
    ended += [in_far, in_near, in_relay, out_far, out_near, out_relay]
    r.found[0:span, :] = lowered(grad_h0)
    in_far.start()
    in_near.start()

    lane8 = iota((1, width), 1)
    row8 = iota((8, width), 0)
    stats = jnp.where(lane8 == 0, loss, 0.0)
    for i, number in enumerate((total_of(valid_lane), sum_hid, sum_attn, sum_ffn)):
        stats = jnp.where(lane8 == i + 1, number, stats)
    small = jnp.where(row8 == 0, gain_grad1, 0.0)
    small = jnp.where(row8 == 1, gain_grad2, small)
    small = jnp.where(row8 == 2, gain_grad3, small)
    r.small[0, 0] = jnp.where(row8 == 3, stats, small)
    l_base = wire.take(1)

    tell_small = to_members(r.small.at[0], l_base)
    tell_small.start()
    ended.append(tell_small)

    s_near.wait_recv()
    for first, value in pieces(2):
        got = raised(r.snear_got[1, first : first + strip, :])
        r.sfar_send[first : first + strip, :] = lowered(value + got)
    s_far.start()
    cand_side(0).wait_send()
    cand_side(0).wait_recv()
    r.own_s[...] = (
        r.h2_s[...] + raised(r.side_got[0]) - valid_col * raised(r.fin_s[0:span, :])
    )

    def add_line(k):
        cand_line(k).wait_recv()
        r.own_s[...] = r.own_s[...] + raised(r.line_got[k])

    loop(1, n_z, add_line)
    r.found[span : 2 * span, :] = lowered(r.own_s[...])
    out_far.start()
    out_near.start()

    ffn_line()

    in_far.wait_recv()
    in_relay.start()

    s_far.wait_recv()
    for first, value in pieces(0):
        rows = slice(first, first + strip)
        r.strip_s[rows, :] = (
            value + raised(r.snear_got[0, rows, :]) + raised(r.sfar_got[rows, :])
        )
    late_rows = 4 * strip
    if n_dp * strip_part > late_rows:
        r.strip_s[late_rows:, :] = jnp.zeros((n_dp * strip_part - late_rows, width), FULL)
    strip_side()

    order = here.y * n_z + here.z
    v_base = wire.take(4)

    def gather_dp(ref, size, base):
        own_part = ref.at[at(order, size)]
        own_column = ref.at[at(here.y, n_z * size)]

        def line(k):
            return wire.make(own_part, own_part, base, here.up(k))

        others = ref.at[pl.ds(0, (n_z - 1) * size)]
        lines = Joined(
            [line(k) for k in range(1, n_z)], wire.make(others, others, base, here.side())
        )
        return lines, wire.make(own_column, own_column, base + 1, here.side())

    ffn_all, ffn_all_side = gather_dp(r.whole_f, ffn_part, v_base)
    strip_all, strip_all_side = gather_dp(r.whole_t, strip_part, v_base + 2)
    ended += [ffn_all, strip_all, ffn_all_side, strip_all_side]
    mine = ffn_finish()
    squares = total_of(mine * mine)
    r.whole_f[at(order, ffn_part), :] = lowered(mine)
    ffn_all.start()
    tell_small.wait_recv()
    r.small[1, 0] = (r.small[0, 0] + r.small[0, 1]) + (r.small[0, 2] + r.small[0, 3])
    h_base = wire.take(2)

    def share(row, k, number):
        return wire.make(r.small.at[row, 0], r.small_dp.at[row // 4, d], number, here.ahead(k))

    def all_shares(row, number):
        others = r.small_dp.at[row // 4, pl.ds(0, n_dp - 1)]
        return wire.make(others, others, number, here.side())

    each(1, n_dp, lambda k: share(1, k, h_base).start())
    r.small_dp[0, d] = r.small[1, 0]

    out_far.wait_recv()
    out_relay.start()

    strip_line()

    in_near.wait_recv()
    in_relay.wait_recv()
    out_near.wait_recv()
    out_relay.wait_recv()

    g_base = wire.take(1)

    def outgoing(k):
        return pl.ds(pl.multiple_of(8 * span + k * cap, cap), cap)

    def ship(k):
        return wire.make(
            r.found.at[outgoing(k)], r.incoming.at[at(k, cap)], g_base, here.ahead(k)
        )

    def all_rows():
        rows = pl.ds(8 * span + cap, (n_dp - 1) * cap)
        landed = r.incoming.at[pl.ds(cap, (n_dp - 1) * cap)]
        return wire.make(r.found.at[rows], landed, g_base, here.side())

    places = pl.ds(8 * span, filled)
    if kept(n_dp):
        r.found[places, :] = lowered(dot(r.pick_s[...], r.found[0 : 8 * span, :]))
    else:
        marks_to = build_marks()

        def choose(k):
            chosen = picks(marks_to, k)
            r.found[outgoing(k), :] = lowered(dot(chosen, r.found[0 : 8 * span, :]))

        loop(0, n_dp, choose)
    ship(n_z).start()
    r.incoming[0:cap, :] = r.found[outgoing(0), :]

    mine = strip_finish()
    squares = squares + total_of(mine * mine)
    r.whole_t[at(order, strip_part), :] = lowered(mine)
    strip_all.start()
    each(1, n_z, lambda k: ship(k).start())
    each(n_z + 1, n_dp, lambda k: ship(k).start())

    several = min(n_dp, 8)

    def own_marks(g):
        for k in range(several):
            r.owned[:, k * 128 : (k + 1) * 128] = lowered(
                one_hot_columns(raised(r.asked[g * several + k]), rows_dev)
            )

    if n_dp == several:
        own_marks(0)

    ffn_all.wait_recv()
    ffn_all_side.start()

    strip_all.wait_recv()
    strip_all_side.start()

    strip_all_side.wait_recv()
    c_base = wire.take(6)

    def spread_strips(first, rows, base):
        part = pl.ds(first, rows)
        mine_at, far_at = r.strips.at[f, part], r.strips.at[far, part]
        copies = (
            wire.make(mine_at, mine_at, base, here.ffn(2)),
            wire.make(mine_at, mine_at, base + 1, here.ffn(1)),
            wire.make(far_at, far_at, base + 2, here.ffn(1)),
        )
        ended.extend(copies)
        return copies

    r.strips[f, 2 * strip :, :] = r.whole_t[0:late_rows, :]
    strip_far, strip_near, strip_relay = spread_strips(2 * strip, late_rows, c_base + 3)
    strip_far.start()
    strip_near.start()
    ffn_all_side.wait_recv()
    outs = [
        pltpu.make_async_copy(src, dst, r.load_sems.at[i])
        for i, (src, dst) in enumerate(
            (
                (r.whole_f.at[pl.ds(0, 2 * width)], r.ffn_out),
                (r.table_grad, r.table_out),
            )
        )
    ]

    def strip_out(s):
        place = here.member[s]
        return pltpu.make_async_copy(
            r.strips.at[place], r.strips_out.at[place], r.load_sems.at[2 + s]
        )

    outs[0].start()
    r.strips[f, 0 : 2 * strip, :] = r.whole_f[2 * width : early_rows, :]
    early_far, early_near, early_relay = spread_strips(0, 2 * strip, c_base)
    early_far.start()
    early_near.start()

    all_rows().wait_recv()

    if n_dp == several:
        r.table_grad[...] = dot(r.owned[...], r.incoming[...])
    else:
        r.table_grad[...] = jnp.zeros((rows_dev, width), FULL)
        r.padded_in[...] = jnp.zeros_like(r.padded_in)

        def add_rows(g):
            own_marks(g)
            for k in range(several):
                r.padded_in[k * 128 : k * 128 + cap, :] = r.incoming[
                    at(g * several + k, cap), :
                ]
            r.table_grad[...] = r.table_grad[...] + dot(r.owned[...], r.padded_in[...])

        loop(0, n_dp // several, add_rows)
    outs[1].start()
    table_grad = r.table_grad[...]
    squares = squares + total_of(table_grad * table_grad)

    r.small[3, 0] = jnp.broadcast_to(squares, (8, width))
    tell_norm = to_members(r.small.at[3], wire.take(1))
    tell_norm.start()
    ended.append(tell_norm)
    all_shares(1, h_base).wait_recv()
    tell_norm.wait_recv()
    r.small[4, 0] = (r.small[3, 0] + r.small[3, 1]) + (r.small[3, 2] + r.small[3, 3])

    each(1, n_dp, lambda k: share(4, k, h_base + 1).start())
    r.small_dp[1, d] = r.small[4, 0]
    early_far.wait_recv()
    early_relay.start()
    early_near.wait_recv()
    strip_near.wait_recv()
    strip_out(0).start()
    strip_out(1).start()
    strip_far.wait_recv()
    strip_relay.start()
    strip_out(2).start()
    all_shares(4, h_base + 1).wait_recv()
    totals, squares = r.small_dp[0, 0], r.small_dp[1, 0]
    for k in range(1, n_dp):
        totals = totals + r.small_dp[0, k]
        squares = squares + r.small_dp[1, k]
    gains = jnp.where(row8 < 3, totals, 0.0)
    norm = jnp.sqrt(squares + total_of(gains * gains))
    r.sums[...] = jnp.where(row8 == 4, norm, totals)

    all_rows().wait_send()
    all_shares(1, h_base).wait_send()
    all_shares(4, h_base + 1).wait_send()


    def end_line(k):
        cand_line(k).wait_send()

    each(1, n_z, end_line)

    ffn_end()
    strip_end()
    early_relay.wait_recv()
    strip_relay.wait_recv()
    strip_out(3).start()
    for copy in outs + [strip_out(s) for s in range(4)]:
        copy.wait()
    for copy in ended:
        copy.wait_send()
    assert wire.arrived <= r.recv_sems.shape[0]
    assert wire.most <= r.send_sems.shape[0]


def step(n_dp, cap, owner, row, lengths, count, table, wq, wo, w_in, w_back, gains, positions):
    rows_dev, width = table.shape
    span = owner.shape[1] // 4
    heads, n_z = width // HD, n_dp // 2
    shapes = plan(n_dp, cap, rows_dev, span, width, heads)
    names = INPUTS + OUTPUTS + list(shapes) + ["load_sems", "send_sems", "recv_sems"]
    vmem = pl.BlockSpec(memory_space=pltpu.VMEM)
    smem = pl.BlockSpec(memory_space=pltpu.SMEM)
    rest = pl.BlockSpec(memory_space=pl.ANY)
    sends, arrivals = 6 * n_z + 23, 18 * n_z + 48

    def out(kind, *shape):
        return jax.ShapeDtypeStruct(shape, kind)

    return pl.pallas_call(
        functools.partial(step_kernel, n_dp, cap, names),
        out_shape=(
            out(FULL, rows_dev, width),
            out(LOW, 2 * width, width),
            out(LOW, 4, 6 * span // 4, width),
            out(FULL, 8, width),
        ),
        in_specs=[vmem, vmem, smem, vmem, rest, rest, rest, rest, rest, vmem, rest],
        out_specs=(rest, rest, rest, vmem),
        scratch_shapes=[pltpu.VMEM(shape[:-1], shape[-1]) for shape in shapes.values()]
        + [
            pltpu.SemaphoreType.DMA((6,)),
            pltpu.SemaphoreType.DMA((sends,)),
            pltpu.SemaphoreType.DMA((arrivals,)),
        ],
        compiler_params=pltpu.CompilerParams(
            collective_id=0,
            has_side_effects=True,
            vmem_limit_bytes=63 * MIB,
        ),
        name="step",
    )(owner, row, lengths, count, table, wq, wo, w_in, w_back, gains, positions)


STATES = 21
GAINS = 5


def jobs(rows_dev, width):
    quarter = -(-rows_dev // 32) * 8
    result = []
    for first in range(0, rows_dev, quarter):
        result.append((0, first, min(quarter, rows_dev - first)))
    return result + [(3, 0, width), (4, 0, width), (1, 0, width), (6, 0, 2 * width), (2, 0, width)]


def update_kernel(rows_dev, table_grad, ffn_grad, strips, sums, *refs):
    ins, refs = refs[:STATES], refs[STATES:]
    loss_out, rms_out, norm_out = refs[:3]
    outs, refs = refs[3 : 3 + STATES], refs[3 + STATES :]
    held, made, refs = refs[:18], refs[18:36], refs[36:]
    table_s, ffn_s, strips_s, grad_sems, in_sems, out_sems = refs
    width = sums.shape[1]
    work = jobs(rows_dev, width)

    def kept_at(which, i):
        return 3 * (which if which < GAINS else which - 1) + i

    def moves(number):
        which, first, rows = work[number]
        part = pl.ds(first, rows)
        here = [kept_at(which, i) for i in range(3)]
        return (
            [
                pltpu.make_async_copy(
                    ins[3 * which + i].at[part],
                    held[here[i]].at[part],
                    in_sems.at[number, i],
                )
                for i in range(3)
            ],
            [
                pltpu.make_async_copy(
                    made[here[i]].at[part],
                    outs[3 * which + i].at[part],
                    out_sems.at[number, i],
                )
                for i in range(3)
            ],
        )

    grads = [
        pltpu.make_async_copy(table_grad, table_s, grad_sems.at[0]),
        pltpu.make_async_copy(ffn_grad, ffn_s, grad_sems.at[1]),
        pltpu.make_async_copy(strips, strips_s, grad_sems.at[2]),
    ]
    grads[0].start()
    for number in range(len(work)):
        for i, copy in enumerate(moves(number)[0]):
            copy.start(priority=(number + i) % 2)
        if number == 1:
            grads[1].start()
            grads[2].start()
    norm = sums[4:5, 0:1]
    factor = CLIP / jnp.maximum(norm, CLIP)
    corr_one = 1.0 - BETA_ONE**STEP
    corr_two = 1.0 - BETA_TWO**STEP

    def adam(which, rows, lanes, grad, rate):
        if which == GAINS:
            source, target = ins[3 * which : 3 * which + 3], outs[3 * which : 3 * which + 3]
        else:
            first = kept_at(which, 0)
            source, target = held[first : first + 3], made[first : first + 3]
        weight, moment, second = (ref[rows, lanes] for ref in source)
        clipped = raised(grad) * factor
        moment = BETA_ONE * moment + (1.0 - BETA_ONE) * clipped
        second = BETA_TWO * second + (1.0 - BETA_TWO) * clipped * clipped
        target[0][rows, lanes] = weight - rate * (
            moment / corr_one / (jnp.sqrt(second / corr_two) + ADAM_EPS) + DECAY * weight
        )
        target[1][rows, lanes] = moment
        target[2][rows, lanes] = second

    every = slice(None)
    strip = strips_s.shape[1] // 6
    waited = set()

    def need(i):
        if i not in waited:
            waited.add(i)
            grads[i].wait()

    for number, (which, first, rows) in enumerate(work):
        copies_in, copies_out = moves(number)
        need(0 if which == 0 else 1 if which in (3, 4) else 2)
        for copy in copies_in:
            copy.wait()
        if which == 0:
            part = slice(first, first + rows)
            adam(0, part, every, table_s[part, :], LEARN)
        elif which in (3, 4):
            start = (which - 3) * width
            adam(which, every, every, ffn_s[start : start + width, :], LEARN)
        for m in range(4):
            at_rows = slice(m * strip, (m + 1) * strip)
            if which == 1:
                for j, i in enumerate((2, 3, 1)):
                    lanes = slice(j * width, (j + 1) * width)
                    grad = strips_s[m, i * strip : (i + 1) * strip, :]
                    adam(1, at_rows, lanes, grad, LEARN)
            elif which == 2:
                adam(2, at_rows, every, strips_s[m, 0:strip, :], LEARN)
            elif which == 6:
                for u in range(2):
                    at_rows = slice((4 * u + m) * strip, (4 * u + m + 1) * strip)
                    grad = strips_s[m, (4 + u) * strip : (5 + u) * strip, :]
                    adam(6, at_rows, every, grad, LEARN)
        for copy in copies_out:
            copy.start()
    adam(GAINS, every, every, sums[0:3, :], GAIN_LEARN)
    stats = sums[3:4, :]
    roots = jnp.sqrt(stats / (stats[:, 1:2] * float(width)))

    def one(row, i):
        return jnp.sum(jnp.where(iota(row.shape, 1) == i, row, 0.0))

    loss_out[0] = one(stats, 0)
    loss_out[1] = one(stats, 1)
    for i in range(3):
        rms_out[i] = one(roots, 2 + i)
    norm_out[0] = one(sums[4:5, :], 0)
    for number in range(len(work)):
        for copy in moves(number)[1]:
            copy.wait()


def update(table_grad, ffn_grad, strips, sums, states):
    vmem = pl.BlockSpec(memory_space=pltpu.VMEM)
    smem = pl.BlockSpec(memory_space=pltpu.SMEM)
    rest = pl.BlockSpec(memory_space=pl.ANY)
    places = [vmem if i // 3 == GAINS else rest for i in range(STATES)]
    room = [pltpu.VMEM(a.shape, FULL) for i, a in enumerate(states) if i // 3 != GAINS]
    rows_dev, width = table_grad.shape
    number = len(jobs(rows_dev, width))
    return pl.pallas_call(
        functools.partial(update_kernel, rows_dev),
        out_shape=tuple(jax.ShapeDtypeStruct((n,), FULL) for n in (2, 3, 1))
        + tuple(jax.ShapeDtypeStruct(a.shape, FULL) for a in states),
        in_specs=[rest] * 3 + [vmem] + places,
        out_specs=[smem] * 3 + places,
        scratch_shapes=room
        + room
        + [pltpu.VMEM(a.shape, a.dtype) for a in (table_grad, ffn_grad, strips)]
        + [
            pltpu.SemaphoreType.DMA((3,)),
            pltpu.SemaphoreType.DMA((number, 3)),
            pltpu.SemaphoreType.DMA((number, 3)),
        ],
        compiler_params=pltpu.CompilerParams(vmem_limit_bytes=63 * MIB),
        name="update",
    )(table_grad, ffn_grad, strips, sums, *states)


def shards(
    item_owner,
    item_row,
    lengths,
    log_count,
    item_table,
    table_mom,
    table_sec,
    qkv_weight,
    qkv_mom,
    qkv_sec,
    out_weight,
    out_mom,
    out_sec,
    ffn_in,
    ffn_in_mom,
    ffn_in_sec,
    ffn_back,
    ffn_back_mom,
    ffn_back_sec,
    norm_gains,
    gains_mom,
    gains_sec,
    positions,
    positions_mom,
    positions_sec,
):
    n_dp = lax.axis_size("dp")
    tokens = item_owner.shape[0]
    cap = max(2, 4 * tokens // (n_dp * lax.axis_size("ffn")))
    table_grad, ffn_grad, strips, sums = step(
        n_dp,
        cap,
        item_owner.T,
        item_row.T,
        lengths,
        log_count,
        item_table,
        qkv_weight,
        out_weight,
        ffn_in,
        ffn_back,
        norm_gains,
        positions,
    )
    return update(
        table_grad,
        ffn_grad,
        strips,
        sums,
        (
            item_table,
            table_mom,
            table_sec,
            qkv_weight,
            qkv_mom,
            qkv_sec,
            out_weight,
            out_mom,
            out_sec,
            ffn_in,
            ffn_in_mom,
            ffn_in_sec,
            ffn_back,
            ffn_back_mom,
            ffn_back_sec,
            norm_gains,
            gains_mom,
            gains_sec,
            positions,
            positions_mom,
            positions_sec,
        ),
    )


def solution(mesh):
    whole, rows, table = P(), P("dp", None), P(("dp", "ffn"), None)
    wide, tall = P(None, "ffn"), P("ffn", None)
    states = (table,) * 3 + (whole,) * 6 + (wide,) * 3 + (tall,) * 3 + (whole,) * 6
    return jax.shard_map(
        shards,
        mesh=mesh,
        in_specs=(rows, rows, P("dp"), P(("dp", "ffn"))) + states,
        out_specs=(whole,) * 3 + states,
        check_vma=False,
    )
```

```python
import functools
import math
import types

import jax
import jax.numpy as jnp
from jax import lax
from jax.experimental import pallas as pl
from jax.experimental.pallas import tpu as pltpu
from jax.sharding import PartitionSpec as P

MESH = pl.DeviceIdType.MESH
MIB = 1024 * 1024
LOW, FULL = jnp.bfloat16, jnp.float32

EPS = 1e-06
NEG = -1e30
HD = 32
ROOT = math.sqrt(2.0 / math.pi)
LEARN = 0.05
GAIN_LEARN = 0.4
STEP = 5
BETA_ONE = 0.5
BETA_TWO = 0.5
DECAY = 0.01
ADAM_EPS = 1e-08
CLIP = 0.05


def lowered(value):
    return value.astype(LOW)


def raised(value):
    return value.astype(FULL)


def dot(left, right):
    return jnp.dot(left, right, preferred_element_type=FULL)


def against(left, right):
    return lax.dot_general(left, right, (((1,), (1,)), ((), ())), preferred_element_type=FULL)


def across(left, right):
    return lax.dot_general(left, right, (((0,), (0,)), ((), ())), preferred_element_type=FULL)


def iota(shape, dim):
    return lax.broadcasted_iota(jnp.int32, shape, dim)


def loop(first, last, body):
    def step(k, unused):
        body(k)
        return unused

    if last - first == 1:
        body(first)
    elif last > first:
        lax.fori_loop(first, last, step, 0)


def each(first, last, body):
    if last - first <= 8:
        for k in range(first, last):
            body(k)
    else:
        loop(first, last, body)


def at(index, size):
    if isinstance(index, int):
        return pl.ds(index * size, size)
    return pl.ds(pl.multiple_of(index * size, size), size)


def spread(row, lanes):
    return jnp.broadcast_to(row, (lanes, row.shape[1])).T


def turned(block):
    return lowered(raised(block).T)


def total_of(value):
    return jnp.sum(value, keepdims=True)


def one_hot_rows(row, width):
    high = jnp.floor(row * (1.0 / 128.0))
    low = spread(row - high * 128.0, 128)
    base = lowered(jnp.where(low == raised(iota(low.shape, 1)), 1.0, 0.0))
    high = lowered(spread(high, 128))
    zero = jnp.zeros_like(base)
    return jnp.concatenate(
        [jnp.where(high == jnp.asarray(b, LOW), base, zero) for b in range(width // 128)], 1
    )


def one_hot_columns(row, height):
    return jnp.where(raised(iota((height, row.shape[1]), 0)) == row, 1.0, 0.0)


def factor_of(hidden):
    return lax.rsqrt(jnp.mean(hidden * hidden, -1, keepdims=True) + EPS)


def rms_back(hidden, gain, upstream):
    factor = factor_of(hidden)
    scaled = upstream * gain
    inner = jnp.mean(scaled * hidden, -1, keepdims=True)
    grad_hidden = factor * scaled - hidden * (factor * factor * factor * inner)
    return grad_hidden, jnp.sum(upstream * hidden * factor, 0, keepdims=True)


class Peers:
    def __init__(self, n_dp):
        self.n_dp, self.n_z = n_dp, n_dp // 2
        self.d, self.f = lax.axis_index("dp"), lax.axis_index("ffn")
        self.z, self.y = self.d // 2, lax.rem(self.d, 2)
        near = self.f + 1 - 2 * lax.rem(self.f, 2)
        far = lax.rem(self.f + 2, 4)
        self.member = (self.f, near, far, 3 - self.f)

    def ffn(self, s):
        return (self.d, self.member[s])

    def ahead(self, i):
        return self.apart(i // self.n_z, i % self.n_z)

    def behind(self, i):
        return self.apart(i // self.n_z, self.n_z - i % self.n_z)

    def apart(self, ky, kz):
        z = lax.rem(self.z + kz, self.n_z)
        return (z * 2 + self.y + ky - 2 * self.y * ky, self.f)

    def side(self):
        return (self.d + 1 - 2 * self.y, self.f)

    def up(self, k):
        return (lax.rem(self.z + k, self.n_z) * 2 + self.y, self.f)

    def down(self, k):
        return (lax.rem(self.z + self.n_z - k, self.n_z) * 2 + self.y, self.f)

    def greet(self):
        barrier = pltpu.get_barrier_semaphore()

        def hello(where):
            pl.semaphore_signal(barrier, inc=1, device_id=where, device_id_type=MESH)

        for s in (1, 2, 3):
            hello(self.ffn(s))
        each(1, self.n_dp, lambda k: hello(self.ahead(k)))

    def met(self):
        pl.semaphore_wait(pltpu.get_barrier_semaphore(), self.n_dp + 2)


class Number:
    def __init__(self, leave, arrive, shared=False):
        self.leave, self.arrive, self.shared = leave, arrive, shared

    def __add__(self, k):
        return Number(self.leave if self.shared else self.leave + k, self.arrive + k, self.shared)


class Wire:
    def __init__(self, send, recv):
        self.send, self.recv = send, recv
        self.left, self.arrived, self.most = 0, 0, 0

    def take(self, number, arrivals=None, shared=False):
        result = Number(self.left, self.arrived, shared)
        self.left += 1 if shared else number
        self.arrived += number if arrivals is None else arrivals
        self.most = max(self.most, self.left)
        return result

    def renew(self):
        self.left = 0

    def make(self, src, dst, number, where, landing=None):
        return pltpu.make_async_remote_copy(
            src_ref=src,
            dst_ref=dst,
            send_sem=self.send.at[number.leave],
            recv_sem=self.recv.at[(landing or number).arrive],
            device_id=where,
            device_id_type=MESH,
        )


class Joined:
    def __init__(self, copies, all_of_them):
        self.copies, self.all = copies, all_of_them

    def start(self):
        for copy in self.copies:
            copy.start()

    def wait_recv(self):
        self.all.wait_recv()

    def wait_send(self):
        self.all.wait_send()


class Group:
    def __init__(self, *copies):
        self.copies = copies

    def start(self):
        for copy in self.copies:
            copy.start()

    def wait_recv(self):
        for copy in self.copies:
            copy.wait_recv()

    def wait_send(self):
        for copy in self.copies:
            copy.wait_send()


INPUTS = [
    "owner",
    "row",
    "lengths",
    "count",
    "table",
    "wq",
    "wo",
    "w_in",
    "w_back",
    "gains",
    "positions",
]
OUTPUTS = ["table_out", "ffn_out", "strips_out", "sums"]


def plan(n_dp, cap, rows_dev, span, width, heads):
    n_z = n_dp // 2
    filled = n_dp * cap
    padded = -(-rows_dev // 128) * 128
    square = (span, width)
    ffn_part, strip_part = parts(n_dp, span, width)
    return {
        "table_s": (rows_dev, width, FULL),
        "wq_s": (width, 3 * width, FULL),
        "wo_s": (width, width, FULL),
        "positions_s": (2 * span, width, FULL),
        "w_s": (2, width, width, FULL),
        "weights": (4, 2, width, width, LOW),
        "hot": (32 * n_dp, span, LOW),
        "slot_s": (8, span, FULL),
        "kind_s": (8, span, FULL),
        "table_low": (padded, width, LOW),
        "req": (n_dp, 1, 128, jnp.int32),
        "asked": (n_dp, 1, 128, jnp.int32),
        "send_rows": (n_dp, cap, width, LOW),
        "send_bias": (n_dp, 1, 128, FULL),
        "found": (4 * filled, width, LOW),
        "found_bias": (4 * n_dp, 1, 128, FULL),
        "bias_s": (8, span, FULL),
        "cands": (n_dp * span, width, LOW),
        "cand_bias": (n_dp, 8, span, FULL),
        "cand_t": (width, (n_dp if kept(n_dp) else 1) * span, LOW),
        "cand_col": ((n_dp if kept(n_dp) else 1) * span, 128, FULL),
        "logit_s": (6 * span if kept(n_dp) else 2 * span, span, FULL),
        "stat_s": (4, 8, span, FULL),
        "scale_s": (8, 4 * span, FULL),
        "expo_s": (n_dp * span if kept(n_dp) else 16, 4 * span, LOW),
        "wq16": (width, 3 * width, LOW),
        "wo16": (width, width, LOW),
        "h0_s": square + (FULL,),
        "n1_s": square + (LOW,),
        "q_s": square + (LOW,),
        "qt_s": (width, span, LOW),
        "k_s": (2 * span, width, LOW),
        "v_s": (2 * span, width, LOW),
        "kt_s": (width, 2 * span, LOW),
        "vt_s": (width, 2 * span, LOW),
        "mask_s": (2 * span, span, FULL),
        "p_s": (heads, 2 * span, span, FULL),
        "p16_s": (2 * span, heads * span, LOW),
        "stack_s": (heads * span, width, LOW),
        "mixt_s": (width, span, LOW),
        "h1_s": square + (FULL,),
        "h2_s": square + (FULL,),
        "n2t_s": (width, span, LOW),
        "pre_s": (4 * span, width, FULL),
        "act_s": (span, 4 * span, LOW),
        "fin_s": (4 * span, width, LOW),
        "fint_s": (width, 4 * span, LOW),
        "acc_s": (width, 4 * span, FULL),
        "acc_send": (3, width, span, LOW),
        "acc_got": (3, width, span, LOW),
        "mid_send": (3, 8, span, FULL),
        "mid_got": (3, 8, span, FULL),
        "tot_s": (4, 8, span, FULL),
        "cand_send": (n_z, span, width, LOW),
        "side_got": (n_z, span, width, LOW),
        "line_got": (n_z, span, width, LOW),
        "own_s": square + (FULL,),
        "dq_s": (width, span, FULL),
        "kv_s": (2 * span, width, FULL),
        "kv_got": (2 * span, width, FULL),
        "gf_s": (4, 2, width, width, FULL),
        "fnear_send": (2, 2 * width, width, LOW),
        "fnear_got": (2, 2 * width, width, LOW),
        "ffar_send": (2 * width, width, LOW),
        "ffar_got": (2 * width, width, LOW),
        "enear_send": (2, span // 2, width, LOW),
        "enear_got": (2, span // 2, width, LOW),
        "efar_send": (span // 2, width, LOW),
        "efar_got": (span // 2, width, LOW),
        "snear_send": (2, span, width, LOW),
        "snear_got": (2, span, width, LOW),
        "sfar_send": (span, width, LOW),
        "sfar_got": (span, width, LOW),
        "gv_s": square + (LOW,),
        "strip_s": (n_dp * strip_part, width, FULL),
        "fside_send": (n_z * ffn_part, width, LOW),
        "fside_got": (n_z * ffn_part, width, LOW),
        "fline_send": (n_z, ffn_part, width, LOW),
        "fline_got": (n_z, ffn_part, width, LOW),
        "sside_send": (n_z * strip_part, width, LOW),
        "sside_got": (n_z * strip_part, width, LOW),
        "sline_send": (n_z, strip_part, width, LOW),
        "sline_got": (n_z, strip_part, width, LOW),
        "whole_f": (n_dp * ffn_part, width, LOW),
        "whole_t": (n_dp * strip_part, width, LOW),
        "incoming": (filled, width, LOW),
        "place_s": (3 * span if kept(n_dp) else 16, 4 * filled if kept(n_dp) else 128, LOW),
        "placing_s": (3 * span if kept(n_dp) else 16, width, FULL),
        "placed_s": (3 * span if kept(n_dp) else 16, width, LOW),
        "pick_s": (filled if kept(n_dp) else 16, 8 * span, LOW),
        "padded_in": (8 * 128 if cap < 128 else 16, width, LOW),
        "owned": (rows_dev, min(n_dp, 8) * 128, LOW),
        "table_grad": (rows_dev, width, FULL),
        "strips": (4, 6 * span // 4, width, LOW),
        "small": (5, 4, 8, width, FULL),
        "small_dp": (2, n_dp, 8, width, FULL),
    }


def kept(n_dp):
    return n_dp <= 8


def parts(n_dp, span, width):
    return (
        -(-(2 * width + span // 2) // (16 * n_dp)) * 16,
        -(-span // (16 * n_dp)) * 16,
    )


def step_kernel(n_dp, cap, names, *refs):
    r = types.SimpleNamespace(**dict(zip(names, refs)))
    here = Peers(n_dp)
    wire = Wire(r.send_sems, r.recv_sems)
    d, f, n_z = here.d, here.f, here.n_z
    me, near, far, cross = here.member
    span, width = r.h0_s.shape
    heads = width // HD
    scale = HD ** (-0.5)
    half = lax.rem(f, 2)
    begin = half * span
    filled = n_dp * cap
    kinds = 4 * n_dp
    rows_dev = r.table_s.shape[0]
    padded = r.table_low.shape[0]
    ended = []

    here.greet()
    loads = [
        pltpu.make_async_copy(src, dst, r.load_sems.at[i])
        for i, (src, dst) in enumerate(
            (
                (r.table, r.table_s),
                (r.wq, r.wq_s),
                (r.wo, r.wo_s),
                (r.positions, r.positions_s),
                (r.w_in, r.w_s.at[0]),
                (r.w_back, r.w_s.at[1]),
            )
        )
    ]
    for i in (4, 5, 0, 1, 2, 3):
        loads[i].start()

    place = iota((kinds, span), 0)
    slot_of = jnp.zeros((kinds, span), jnp.int32)
    for s in (1, 2, 3):
        slot_of = slot_of + (place >= s * n_dp).astype(jnp.int32)
    steps = place - slot_of * n_dp
    other_y = (steps >= n_z).astype(jnp.int32)
    steps = steps - other_y * n_z + here.z
    steps = jnp.where(steps >= n_z, steps - n_z, steps)
    ahead = steps * 2 + here.y + other_y * (1 - 2 * here.y)
    named = ahead * 4 + jnp.where(
        slot_of == 0, me, jnp.where(slot_of == 1, near, jnp.where(slot_of == 2, far, cross))
    )

    def chunk_of(ref, c):
        return ref[c // 4 : c // 4 + 1, (c % 4) * span : (c % 4 + 1) * span]

    for c in range(8):
        r.hot[c * kinds : (c + 1) * kinds, :] = lowered(
            jnp.where(chunk_of(r.owner, c) == named, 1.0, 0.0)
        )
    before = lowered(jnp.where(iota((span, span), 0) < iota((span, span), 1), 1.0, 0.0))
    carry = jnp.zeros((kinds, 1), FULL)
    place_f = raised(place)
    asking = jnp.zeros((2 * n_dp, 128), FULL)
    for c in range(8):
        ones = raised(r.hot[c * kinds : (c + 1) * kinds, :])
        ranks = dot(r.hot[c * kinds : (c + 1) * kinds, :], before)
        slot = jnp.sum(ones * (ranks + carry), 0, keepdims=True)
        carry = carry + jnp.sum(ones, 1, keepdims=True)
        r.slot_s[c : c + 1, :] = slot
        r.kind_s[c : c + 1, :] = jnp.sum(ones * place_f, 0, keepdims=True)
        row = chunk_of(r.row, c)
        mine = ones[:n_dp]
        sought = jnp.concatenate([mine * raised(row >> 5), mine * raised(row & 31)], 0)
        asking = asking + against(lowered(sought), lowered(one_hot_columns(slot, 128)))
    wanted = (asking[:n_dp] * 32.0 + asking[n_dp:]).astype(jnp.int32)
    for k in range(n_dp):
        r.req[k, 0:1, :] = wanted[k : k + 1, :]
    r.asked[0] = r.req[0]
    q_base = wire.take(n_dp, shared=True)

    def ask(k):
        return wire.make(r.req.at[k], r.asked.at[k], q_base + k, here.ahead(k))

    here.met()
    each(1, n_dp, lambda k: ask(k).start())

    loads[4].wait()
    loads[5].wait()
    r.weights[0] = lowered(r.w_s[...])
    w_base = wire.take(3)
    w_near = wire.make(r.weights.at[0], r.weights.at[1], w_base, here.ffn(1))
    w_far = wire.make(r.weights.at[0], r.weights.at[2], w_base + 1, here.ffn(2))
    w_relay = wire.make(r.weights.at[2], r.weights.at[3], w_base + 2, here.ffn(1))
    w_far.start()
    w_near.start()

    def build_marks():
        for s in range(4):
            for column in range(2):
                chunk_row = pl.ds(column * 4 + here.member[s], 1)
                r.p16_s[0:cap, (2 * s + column) * span : (2 * s + column + 1) * span] = lowered(
                    one_hot_columns(r.slot_s[chunk_row, :], cap)
                )
        where_to = jnp.concatenate(
            [
                r.kind_s[pl.ds(column * 4 + here.member[s], 1), :]
                for s in range(4)
                for column in range(2)
            ],
            1,
        )
        where_to = lowered(jnp.broadcast_to(where_to, (16, 8 * span)))
        return where_to

    zero16 = jnp.zeros((16, 8 * span), LOW)

    def picks(where_to, k):
        wanted = where_to == lowered(jnp.full((16, 8 * span), k, FULL))
        return jnp.concatenate(
            [
                jnp.where(wanted, r.p16_s[i * 16 : (i + 1) * 16, :], zero16)
                for i in range(cap // 16)
            ],
            0,
        )

    def key_of(column, quarter):
        chunk = pl.ds(column * 4 + quarter, 1)
        return r.kind_s[chunk, :] * float(cap) + r.slot_s[chunk, :]

    if kept(n_dp):
        marks_to = build_marks()

        def keep_picks(k):
            r.pick_s[at(k, cap), :] = picks(marks_to, k)

        loop(0, n_dp, keep_picks)
        for i, (column, quarter) in enumerate(((1, f), (0, f), (0, near))):
            r.place_s[at(i, span), :] = one_hot_rows(key_of(column, quarter), 4 * filled)

    loads[0].wait()
    r.table_low[0:rows_dev, :] = lowered(r.table_s[...])
    if padded > rows_dev:
        r.table_low[rows_dev:padded, :] = jnp.zeros((padded - rows_dev, width), LOW)
    counts = lowered(jnp.broadcast_to(raised(r.count[...].reshape(1, rows_dev)), (8, rows_dev)))
    if padded > rows_dev:
        counts = jnp.concatenate([counts, jnp.zeros((8, padded - rows_dev), LOW)], 1)
    r_base, b_base = wire.take(n_dp, shared=True), wire.take(1)
    others = pl.ds(1, n_dp - 1)

    def reply(k):
        return wire.make(r.send_rows.at[k], r.found.at[at(k, cap)], r_base + k, here.behind(k))

    def reply_bias(k):
        return wire.make(r.send_bias.at[k], r.found_bias.at[k], b_base, here.behind(k))

    def all_replies():
        rest = r.found.at[pl.ds(cap, filled - cap)]
        return wire.make(r.send_rows.at[others], rest, r_base, here.side())

    def all_biases():
        return wire.make(r.send_bias.at[others], r.found_bias.at[others], b_base, here.side())

    def fetch(k):
        chosen = one_hot_rows(raised(r.asked[k]), padded)
        return lowered(dot(chosen, r.table_low[...]))[:cap], against(counts, chosen)[0:1, :]

    def serve(k):
        ask(k).wait_recv()
        rows, bias = fetch(k)
        r.send_rows[k] = rows
        r.send_bias[k] = bias
        reply(k).start()
        reply_bias(k).start()

    loop(1, n_dp, serve)
    rows, bias = fetch(0)
    r.found[0:cap, :] = rows
    r.found_bias[0] = bias
    cuts = [(k, 1) for k in range(n_dp)]
    passes = [wire.take(len(cuts), shared=True) for i in range(3)]
    bias_passes = [wire.take(1) for i in range(3)]

    def pass_on(i, source, target, number, who):
        sem = bias_passes[number] if i == len(cuts) else passes[number] + i
        if i == len(cuts):
            src, dst = (r.found_bias.at[at(slot, n_dp)] for slot in (source, target))
        else:
            first, several = cuts[i]
            src, dst = (
                r.found.at[pl.ds((slot * n_dp + first) * cap, several * cap)]
                for slot in (source, target)
            )
        return wire.make(src, dst, sem, here.ffn(who))

    def all_passes(source, number):
        rows = r.found.at[at(source, filled)]
        return wire.make(rows, rows, passes[number], here.side())

    def to_far(i):
        return pass_on(i, 0, 2, 0, 2)

    def to_near(i):
        return pass_on(i, 0, 1, 1, 1)

    def relay(i):
        return pass_on(i, 2, 3, 2, 1)

    def take_on(i):
        first, several = cuts[i]
        for k in range(max(first, 1), first + several):
            reply(k).wait_recv()
        to_far(i).start()
        to_near(i).start()

    def relay_on(i):
        to_far(i).wait_recv()
        relay(i).start()

    for i in range(len(cuts)):
        take_on(i)
        if i > 1:
            relay_on(i - 2)
    all_biases().wait_recv()
    to_far(len(cuts)).start()
    to_near(len(cuts)).start()
    w_far.wait_recv()
    w_relay.start()
    relay_on(len(cuts) - 2)
    for i in range(len(cuts)):
        to_near(i).wait_recv()
    if kept(n_dp):
        r.placing_s[...] = dot(r.place_s[:, : 2 * filled], r.found[0 : 2 * filled, :])
    relay_on(len(cuts) - 1)
    relay_on(len(cuts))
    loads[1].wait()
    loads[2].wait()
    r.wq16[...] = lowered(r.wq_s[...])
    r.wo16[...] = lowered(r.wo_s[...])
    for i in range(len(cuts)):
        relay(i).wait_recv()

    if kept(n_dp):
        far_rows = dot(r.place_s[:, 2 * filled :], r.found[2 * filled :, :])
        r.placed_s[...] = lowered(r.placing_s[...] + far_rows)

    def chosen_rows(i):
        if kept(n_dp):
            return r.placed_s[at(i, span), :]
        column, quarter = ((1, f), (0, f), (0, near))[i]
        return lowered(dot(one_hot_rows(key_of(column, quarter), 4 * filled), r.found[...]))

    r.cands[0:span, :] = chosen_rows(0)
    to_near(len(cuts)).wait_recv()
    relay(len(cuts)).wait_recv()
    bias_rows = lowered(r.found_bias[:, 0, :].T)
    lane = iota((1, span), 1)
    length = r.lengths[f // 2]
    valid_lane = jnp.where(lane + begin < length, 1.0, 0.0)
    valid_col = jnp.where(iota((span, 1), 0) + begin < length, 1.0, 0.0)
    chunk = 4 + f
    marks = one_hot_columns(r.slot_s[pl.ds(chunk, 1), :], 128)
    bias = jnp.sum(dot(bias_rows, r.hot[at(chunk, kinds), :]) * marks, 0, keepdims=True)
    r.bias_s[...] = jnp.broadcast_to(bias, (8, span))
    r.cand_bias[0] = jnp.broadcast_to(jnp.where(lane + begin < length, -bias, NEG), (8, span))
    z_base, y_base = wire.take(0, 3 * n_z), wire.take(3 * n_z)
    u_base = wire.take(6 * n_z, 0)
    has_up, has_down = here.z + 1 < n_z, here.z > 0

    def slot(k, ky):
        if isinstance(k, int) and k == 0:
            return ky
        return 1 + k + ky * (n_z - 1)

    half_rows = span // 2

    def half_of(i, h):
        first = i * span + h * half_rows
        if not isinstance(first, int):
            first = pl.multiple_of(first, half_rows)
        return r.cands.at[pl.ds(first, half_rows)]

    def offer_line(source, target, number, where):
        i, j = slot(source, 0), slot(target, 0)
        first, second = (
            wire.make(
                half_of(i, h),
                half_of(j, h),
                number + 2 * n_z * h,
                where,
                z_base + (n_z * h + target),
            )
            for h in range(2)
        )
        bias = wire.make(
            r.cand_bias.at[i],
            r.cand_bias.at[j],
            number + 4 * n_z,
            where,
            z_base + (2 * n_z + target),
        )
        return first, Group(second, bias)

    def send_up(a):
        return offer_line(a, a + 1, u_base + a, here.up(1))

    def send_down(b):
        source = b if isinstance(b, int) and b == 0 else n_z - b
        return offer_line(source, n_z - 1 - b, u_base + (n_z + b), here.down(1))

    def offer_side(k):
        i, j = slot(k, 0), slot(k, 1)
        first, second = (
            wire.make(half_of(i, h), half_of(j, h), y_base + (n_z * h + k), here.side())
            for h in range(2)
        )
        bias = wire.make(
            r.cand_bias.at[i], r.cand_bias.at[j], y_base + (2 * n_z + k), here.side()
        )
        return first, Group(second, bias)

    for h in range(2):
        pl.when(has_up)(lambda: send_up(0)[h].start())
        pl.when(has_down)(lambda: send_down(0)[h].start())
    for h in range(2):
        offer_side(0)[h].start()

    def hand_on(j):
        @pl.when(here.z >= j)
        def from_below():
            for h in range(2):
                offer_line(0, j, u_base, here.up(1))[h].wait_recv()
                pl.when(has_up)(lambda: send_up(j)[h].start())
                offer_side(j)[h].start()

        @pl.when(here.z + j < n_z)
        def from_above():
            for h in range(2):
                offer_line(0, n_z - j, u_base, here.up(1))[h].wait_recv()
                pl.when(has_down)(lambda: send_down(j)[h].start())
                offer_side(n_z - j)[h].start()

    loads[3].wait()
    gain1, gain2, gain3 = r.gains[0:1, :], r.gains[1:2, :], r.gains[2:3, :]
    hidden0 = raised(chosen_rows(1)) + r.positions_s[at(half, span), :]
    r.h0_s[...] = hidden0
    normed1 = lowered(hidden0 * factor_of(hidden0) * gain1)
    r.n1_s[...] = normed1
    r.q_s[...] = lowered(dot(normed1, r.wq16[:, :width]))
    r.k_s[0:span, :] = lowered(dot(normed1, r.wq16[:, width : 2 * width]))
    r.v_s[0:span, :] = lowered(dot(normed1, r.wq16[:, 2 * width :]))
    hidden0 = raised(chosen_rows(2)) + r.positions_s[at(1 - half, span), :]
    normed1 = lowered(hidden0 * factor_of(hidden0) * gain1)
    r.k_s[span:, :] = lowered(dot(normed1, r.wq16[:, width : 2 * width]))
    r.v_s[span:, :] = lowered(dot(normed1, r.wq16[:, 2 * width :]))
    r.qt_s[...] = turned(r.q_s[...])
    r.kt_s[...] = turned(r.k_s[...])
    r.vt_s[...] = turned(r.v_s[...])
    key_at = iota((2 * span, span), 0)
    key_at = jnp.where(key_at < span, key_at + begin, key_at - begin)
    allowed = (key_at <= iota((2 * span, span), 1) + begin) & (key_at < length)
    r.mask_s[...] = jnp.where(allowed, 0.0, NEG)
    row_head = iota((width, span), 0) // HD
    lane_head = iota((span, width), 1) // HD

    def forward_head(h):
        rows = at(h, HD)
        mine = jnp.where(row_head == h, raised(r.qt_s[...]), 0.0)
        scores = dot(r.k_s[...], lowered(mine)) * scale + r.mask_s[...]
        expo = jnp.exp(scores - jnp.max(scores, 0, keepdims=True))
        probs = expo / jnp.sum(expo, 0, keepdims=True)
        r.p_s[h] = probs
        low_probs = lowered(probs)
        r.p16_s[:, at(h, span)] = low_probs
        r.mixt_s[rows, :] = lowered(dot(r.vt_s[rows, :], low_probs))

    loop(0, heads * 3 // 4, forward_head)
    hand_on(1)
    loop(heads * 3 // 4, heads, forward_head)
    attn = dot(turned(r.mixt_s[...]), r.wo16[...])
    hidden1 = r.h0_s[...] + attn
    r.h1_s[...] = hidden1
    sum_attn = total_of(valid_col * attn * attn)
    normed2 = lowered(hidden1 * factor_of(hidden1) * gain2)
    r.n2t_s[...] = turned(normed2)
    w_near.wait_recv()
    w_relay.wait_recv()
    for s in range(4):
        pre = dot(normed2, r.weights[s, 0])
        r.pre_s[s * span : (s + 1) * span, :] = pre
        inner = jnp.tanh(ROOT * (pre + 0.044715 * pre * pre * pre))
        r.act_s[:, s * span : (s + 1) * span] = lowered(0.5 * pre * (1.0 + inner))
    branch = dot(r.act_s[...], jnp.concatenate([r.weights[s, 1] for s in range(4)], 0))
    hidden2 = r.h1_s[...] + branch
    r.h2_s[...] = hidden2
    sum_ffn = total_of(valid_col * branch * branch)
    sum_hid = total_of(valid_col * hidden2 * hidden2)
    final = lowered(hidden2 * factor_of(hidden2) * gain3)
    r.fin_s[0:span, :] = final
    f_base = wire.take(3)
    fin = [r.fin_s.at[at(s, span)] for s in range(4)]
    fin_near = wire.make(fin[0], fin[1], f_base, here.ffn(1))
    fin_far = wire.make(fin[0], fin[2], f_base + 1, here.ffn(2))
    fin_relay = wire.make(fin[2], fin[3], f_base + 2, here.ffn(1))
    fin_far.start()
    fin_near.start()
    ended += [fin_far, fin_near, fin_relay]

    def turn_fin(s):
        r.fint_s[:, s * span : (s + 1) * span] = turned(r.fin_s[s * span : (s + 1) * span, :])

    turn_fin(0)
    if n_z > 2:
        hand_on(2)

    def prepare(i):
        if kept(n_dp):
            r.cand_t[:, at(i, span)] = turned(r.cands[at(i, span), :])
            r.cand_col[at(i, span), :] = spread(r.cand_bias[i, 0:1, :], 128)

    def columns(i, number):
        if kept(n_dp):
            return r.cand_col[slots(i, number), :]
        rows = [spread(r.cand_bias[i + j, 0:1, :], 128) for j in range(number)]
        return jnp.concatenate(rows, 0)

    def slots(i, number):
        if isinstance(i, int):
            return pl.ds(i * span, number * span)
        return pl.ds(pl.multiple_of(i * span, span), number * span)

    prepare(0)
    for copy in offer_side(0):
        copy.wait_recv()
    prepare(1)
    r.acc_s[...] = jnp.zeros_like(r.acc_s)
    for s in range(4):
        r.stat_s[s, 0:1, :] = jnp.full((1, span), NEG, FULL)
        r.stat_s[s, 1:2, :] = jnp.zeros((1, span), FULL)

    def count_in(s, i, number, group):
        lanes = slice(s * span, (s + 1) * span)
        rows = slots(i, number)
        first = s % 2 * 3 * span if kept(n_dp) else 0
        held = slice(first, first + number * span)
        logits = dot(r.cands[rows, :], r.fint_s[:, lanes])
        r.logit_s[held, :] = logits + jnp.concatenate([columns(i, number)] * (span // 128), 1)
        top = r.stat_s[s, 0:1, :]
        higher = jnp.maximum(top, jnp.max(r.logit_s[held, :], 0, keepdims=True))
        shrink = jnp.exp(top - higher)
        expo = jnp.exp(r.logit_s[held, :] - higher)
        r.stat_s[s, 0:1, :] = higher
        r.stat_s[s, 1:2, :] = r.stat_s[s, 1:2, :] * shrink + jnp.sum(expo, 0, keepdims=True)
        if kept(n_dp):
            low_expo = lowered(expo)
            r.expo_s[rows, lanes] = low_expo
            r.stat_s[s, 2 + group : 3 + group, :] = higher
            part = dot(r.cand_t[:, rows], low_expo)
        else:
            part = across(r.cands[rows, :], lowered(expo))
        r.acc_s[:, lanes] = r.acc_s[:, lanes] * shrink + part

    def count(s, group):
        first = (0, 2, n_z + 1)[group]
        number = (2, n_z - 1, n_z - 1)[group]
        if number <= 3:
            if number:
                count_in(s, first, number, group)
        else:
            loop(first, first + number, lambda i: count_in(s, i, 1, group))

    count(0, 0)
    fin_near.wait_recv()
    turn_fin(1)
    count(1, 0)
    fin_far.wait_recv()
    fin_relay.start()
    turn_fin(2)
    loop(3, n_z, hand_on)
    count(2, 0)
    fin_relay.wait_recv()
    turn_fin(3)
    count(3, 0)
    loop(2, n_z + 1, prepare)
    count(3, 1)
    count(2, 1)
    count(0, 1)
    count(1, 1)

    def prepare_side(k):
        for copy in offer_side(k):
            copy.wait_recv()
        prepare(slot(k, 1))

    loop(1, n_z, prepare_side)

    a_base = wire.take(6)

    def give(i, who):
        return Group(
            wire.make(r.acc_send.at[i], r.acc_got.at[i], a_base + 2 * i, here.ffn(who)),
            wire.make(r.mid_send.at[i], r.mid_got.at[i], a_base + 2 * i + 1, here.ffn(who)),
        )

    gives = [give(0, 1), give(1, 1), give(2, 2)]
    ended += gives

    def fill(i, s):
        r.acc_send[i] = lowered(r.acc_s[:, s * span : (s + 1) * span])
        r.mid_send[i] = r.stat_s[s]
        gives[i].start()

    def merge(s, i):
        gives[i].wait_recv()
        lanes = slice(s * span, (s + 1) * span)
        top, other = r.stat_s[s, 0:1, :], r.mid_got[i, 0:1, :]
        higher = jnp.maximum(top, other)
        left, right = jnp.exp(top - higher), jnp.exp(other - higher)
        r.acc_s[:, lanes] = r.acc_s[:, lanes] * left + raised(r.acc_got[i]) * right
        r.stat_s[s, 0:1, :] = higher
        r.stat_s[s, 1:2, :] = r.stat_s[s, 1:2, :] * left + r.mid_got[i, 1:2, :] * right

    count(3, 2)
    fill(0, 3)
    count(2, 2)
    merge(2, 0)
    fill(2, 2)
    count(1, 2)
    fill(1, 1)
    count(0, 2)
    merge(0, 1)
    merge(0, 2)
    total = r.stat_s[0, 1:2, :]
    log_total = r.stat_s[0, 0:1, :] + jnp.log(total)
    r.tot_s[0] = jnp.broadcast_to(jnp.where(valid_lane > 0, log_total, -NEG), (8, span))
    for copy in (
        all_passes(0, 0),
        all_passes(0, 1),
        all_passes(2, 2),
        to_far(len(cuts)),
        to_near(len(cuts)),
        relay(len(cuts)),
    ):
        copy.wait_send()

    t_base = wire.take(1)

    def to_members(ref, number):
        three = ref.at[pl.ds(1, 3)]
        return Joined(
            [wire.make(ref.at[0], ref.at[s], number, here.ffn(s)) for s in (1, 2, 3)],
            wire.make(three, three, number, here.side()),
        )

    tell = to_members(r.tot_s, t_base)
    tell.start()
    ended.append(tell)
    if not kept(n_dp):
        r.cand_t[...] = turned(r.cands[0:span, :])
    target_t = raised(r.cand_t[:, 0:span])
    positive = (
        jnp.sum(raised(r.fint_s[:, :span]) * target_t, 0, keepdims=True) - r.bias_s[0:1, :]
    )
    loss = total_of(valid_lane * (log_total - positive))
    grad_final = ((r.acc_s[:, 0:span] / total - target_t) * valid_lane).T

    grad_h2, gain_grad3 = rms_back(r.h2_s[...], gain3, grad_final)
    up = lowered(grad_h2)
    r.h2_s[...] = grad_h2
    for s in (1, 3, 2, 0):
        lanes = slice(s * span, (s + 1) * span)
        r.gf_s[s, 1] = across(r.act_s[:, lanes], up)
        grad_act = against(up, r.weights[s, 1])
        pre = r.pre_s[s * span : (s + 1) * span, :]
        inner = jnp.tanh(ROOT * (pre + 0.044715 * pre * pre * pre))
        slope = 0.5 * (1.0 + inner) + 0.5 * pre * (1.0 - inner * inner) * (
            ROOT * (1.0 + 3.0 * 0.044715 * pre * pre)
        )
        grad_pre = lowered(grad_act * slope)
        r.gf_s[s, 0] = dot(r.n2t_s[...], grad_pre)
        r.act_s[:, lanes] = grad_pre
    for i, s in enumerate((1, 3)):
        for j in range(2):
            r.fnear_send[i, j * width : (j + 1) * width, :] = lowered(r.gf_s[s, j])
    all_asks = wire.make(r.req.at[others], r.req.at[others], q_base, here.side())
    for copy in (all_asks, all_replies(), all_biases(), w_far, w_near, w_relay):
        copy.wait_send()
    def end_offers(j):
        for h in range(2):
            pl.when(has_up & (here.z >= j))(lambda: send_up(j)[h].wait_send())
            pl.when(has_down & (here.z + j < n_z))(lambda: send_down(j)[h].wait_send())
            offer_side(j)[h].wait_send()

    each(0, n_z, end_offers)
    for copy in ended:
        copy.wait_send()
    ended.clear()
    wire.renew()
    e_base = wire.take(6)
    f_near = wire.make(r.fnear_send, r.fnear_got, e_base, here.ffn(1))
    f_far = wire.make(r.ffar_send, r.ffar_got, e_base + 1, here.ffn(2))
    s_near = wire.make(r.snear_send, r.snear_got, e_base + 2, here.ffn(1))
    s_far = wire.make(r.sfar_send, r.sfar_got, e_base + 3, here.ffn(2))
    e_near = wire.make(r.enear_send, r.enear_got, e_base + 4, here.ffn(1))
    e_far = wire.make(r.efar_send, r.efar_got, e_base + 5, here.ffn(2))
    ended += [f_near, f_far, s_near, s_far, e_near, e_far]
    f_near.start()

    tell.wait_recv()
    if kept(n_dp):
        for s in range(4):
            for group in range(3):
                level = r.stat_s[s, 2 + group : 3 + group, :] - r.tot_s[s, 0:1, :]
                r.scale_s[group : group + 1, s * span : (s + 1) * span] = jnp.exp(level)
    side_base, line_base = wire.take(n_z), wire.take(n_z)

    def cand_side(k):
        return wire.make(r.cand_send.at[k], r.side_got.at[k], side_base + k, here.side())

    def cand_line(k):
        return wire.make(r.cand_send.at[k], r.line_got.at[k], line_base + k, here.down(k))

    def cand_grad(i):
        if kept(n_dp):
            group = jnp.where(i < 2, 0, jnp.where(i <= n_z, 1, 2))
            share_of = r.scale_s[pl.ds(group, 1), :]
            weights = raised(r.expo_s[at(i, span), :]) * share_of
            return dot(lowered(weights), r.fin_s[...])
        column = jnp.concatenate([columns(i, 1)] * (4 * span // 128), 1)
        level = jnp.concatenate([r.tot_s[s, 0:1, :] for s in range(4)], 1)
        logits = dot(r.cands[at(i, span), :], r.fint_s[...]) + column
        return dot(lowered(jnp.exp(logits - level)), r.fin_s[...])

    def slot_at(k, ky):
        return jnp.where(k == 0, ky, 1 + k + ky * (n_z - 1))

    def side_step(k):
        r.cand_send[k] = lowered(cand_grad(slot_at(k, 1)))
        cand_side(k).start()

    def line_step(k):
        grad = cand_grad(slot_at(k, 0))
        cand_side(k).wait_send()
        cand_side(k).wait_recv()
        r.cand_send[k] = lowered(grad + raised(r.side_got[k]))
        cand_line(k).start()

    middle = n_z // 2
    side_step(middle)
    loop(1, middle, side_step)
    loop(middle + 1, n_z, side_step)
    if middle:
        side_step(0)

    grad_normed2 = against(
        r.act_s[...], jnp.concatenate([r.weights[s, 0] for s in range(4)], 1)
    )
    grad_h1_norm, gain_grad2 = rms_back(r.h1_s[...], gain2, grad_normed2)
    grad_h1 = r.h2_s[...] + grad_h1_norm
    r.h1_s[...] = grad_h1
    f_near.wait_recv()
    for j in range(2):
        rows = slice(j * width, (j + 1) * width)
        r.ffar_send[rows, :] = lowered(r.gf_s[2, j] + raised(r.fnear_got[1, rows, :]))
    f_far.start()

    attn_up = lowered(grad_h1)
    r.acc_s[:, 3 * width :] = dot(r.mixt_s[...], attn_up)
    grad_mixed = lowered(against(attn_up, r.wo16[...]))
    grad_mixed_f = raised(grad_mixed)
    r.mixt_s[...] = turned(grad_mixed)
    for h in range(heads):
        r.stack_s[h * span : (h + 1) * span, :] = lowered(
            jnp.where(lane_head == h, grad_mixed_f, 0.0)
        )
    r.kv_s[...] = dot(r.p16_s[...], r.stack_s[...])
    r.logit_s[span : 2 * span, :] = r.kv_s[span:, :]
    r.own_s[...] = r.kv_s[0:span, :]
    k_base = wire.take(2)

    def lend(i):
        rows = at(i, span)
        return wire.make(r.logit_s.at[rows], r.kv_got.at[rows], k_base + i, here.ffn(1))

    lend_k, lend_v = lend(0), lend(1)
    ended += [lend_k, lend_v]
    lend_v.start()

    def backward_head(h):
        rows = at(h, HD)
        mine = jnp.where(row_head == h, raised(r.mixt_s[...]), 0.0)
        grad_probs = dot(r.v_s[...], lowered(mine))
        probs = r.p_s[h]
        inner = jnp.sum(probs * grad_probs, 0, keepdims=True)
        grad_scores = lowered(probs * (grad_probs - inner))
        r.p16_s[:, at(h, span)] = grad_scores
        r.dq_s[rows, :] = dot(r.kt_s[rows, :], grad_scores) * scale

    loop(0, heads // 2, backward_head)
    if middle:
        line_step(middle)
    strip = span // 4
    halves = (jnp.where(half == 0, 1.0, 0.0), jnp.where(half == 1, 1.0, 0.0))

    def strip_at(s):
        return pl.ds(pl.multiple_of(here.member[s] * strip, strip), strip)

    def early_pieces(s):
        yield 0, r.acc_s[strip_at(s), 3 * width :]
        yield strip, r.acc_s[strip_at(s), 2 * width : 3 * width]

    def pieces(s):
        for j in range(2):
            yield j * strip, r.acc_s[strip_at(s), j * width : (j + 1) * width]
        for u in range(2):
            yield (2 + u) * strip, r.h0_s[strip_at(s), :] * halves[u]

    lend_v.wait_recv()
    r.gv_s[...] = lowered(r.own_s[...] + r.kv_got[span:, :])
    r.acc_s[:, 2 * width : 3 * width] = across(r.n1_s[...], r.gv_s[...])
    for i, s in enumerate((1, 3)):
        for first, value in early_pieces(s):
            r.enear_send[i, first : first + strip, :] = lowered(value)
    e_near.start()
    loop(heads // 2, heads, backward_head)
    loop(1, middle, line_step)
    e_near.wait_recv()
    for first, value in early_pieces(2):
        got = raised(r.enear_got[1, first : first + strip, :])
        r.efar_send[first : first + strip, :] = lowered(value + got)
    e_far.start()
    queries = raised(r.q_s[...])
    for h in range(heads):
        r.stack_s[h * span : (h + 1) * span, :] = lowered(jnp.where(lane_head == h, queries, 0.0))
    r.kv_s[...] = dot(r.p16_s[...], r.stack_s[...]) * scale
    r.logit_s[0:span, :] = r.kv_s[span:, :]
    lend_k.start()
    loop(middle + 1, n_z, line_step)
    r.h2_s[...] = cand_grad(0)
    ffn_part, strip_part = parts(n_dp, span, width)
    f_far.wait_recv()
    for j in range(2):
        rows = slice(j * width, (j + 1) * width)
        r.pre_s[rows, :] = (
            r.gf_s[0, j] + raised(r.fnear_got[0, rows, :]) + raised(r.ffar_got[rows, :])
        )
    e_far.wait_recv()
    early_rows = 2 * width + 2 * strip
    for first, value in early_pieces(0):
        rows = slice(first, first + strip)
        r.pre_s[2 * width + first : 2 * width + first + strip, :] = (
            value + raised(r.enear_got[0, rows, :]) + raised(r.efar_got[rows, :])
        )
    if n_dp * ffn_part > early_rows:
        r.pre_s[early_rows : n_dp * ffn_part, :] = jnp.zeros(
            (n_dp * ffn_part - early_rows, width), FULL
        )
    m_base = wire.take(2 + 2 * n_z)

    def sum_dp(source, size, side_send, side_got, line_send, line_got, base):
        def rows_of(k, y):
            return at(y * n_z + lax.rem(here.z + k, n_z), size)

        across_y = wire.make(side_send, side_got, base, here.side())

        def along(k):
            return wire.make(line_send.at[k], line_got.at[k], base + 1 + k, here.up(k))

        def begin_side():
            def fill_side(k):
                side_send[at(k, size), :] = lowered(source[rows_of(k, 1 - here.y), :])

            loop(0, n_z, fill_side)
            across_y.start()

        def begin_line():
            across_y.wait_recv()

            def fill_line(k):
                line_send[k] = lowered(
                    source[rows_of(k, here.y), :] + raised(side_got[at(k, size), :])
                )
                along(k).start()

            loop(1, n_z, fill_line)

        def finish():
            value = source[rows_of(0, here.y), :] + raised(side_got[0:size, :])
            for k in range(1, n_z):
                along(k).wait_recv()
                value = value + raised(line_got[k])
            return value

        def end():
            across_y.wait_send()
            each(1, n_z, lambda k: along(k).wait_send())

        return begin_side, begin_line, finish, end

    ffn_side, ffn_line, ffn_finish, ffn_end = sum_dp(
        r.pre_s,
        ffn_part,
        r.fside_send,
        r.fside_got,
        r.fline_send,
        r.fline_got,
        m_base,
    )
    strip_side, strip_line, strip_finish, strip_end = sum_dp(
        r.strip_s,
        strip_part,
        r.sside_send,
        r.sside_got,
        r.sline_send,
        r.sline_got,
        m_base + 1 + n_z,
    )
    ffn_side()


    grad_q = lowered(r.dq_s[...].T)
    lend_k.wait_recv()
    grad_qk = jnp.concatenate(
        [grad_q, lowered(r.kv_s[0:span, :] + r.kv_got[0:span, :])],
        1,
    )
    grad_united = jnp.concatenate([grad_qk, r.gv_s[...]], 1)
    grad_h0_norm, gain_grad1 = rms_back(r.h0_s[...], gain1, against(grad_united, r.wq16[...]))
    grad_h0 = r.h1_s[...] + grad_h0_norm
    r.h0_s[...] = grad_h0

    r.acc_s[:, : 2 * width] = across(r.n1_s[...], grad_qk)

    for i, s in enumerate((1, 3)):
        for first, value in pieces(s):
            r.snear_send[i, first : first + strip, :] = lowered(value)
    s_near.start()

    o_base = wire.take(6)

    def chunk(s, column):
        return r.found.at[at(2 * s + column, span)]

    def row_copies(column):
        return (
            wire.make(chunk(0, column), chunk(2, column), o_base + 3 * column, here.ffn(2)),
            wire.make(chunk(0, column), chunk(1, column), o_base + 3 * column + 1, here.ffn(1)),
            wire.make(chunk(2, column), chunk(3, column), o_base + 3 * column + 2, here.ffn(1)),
        )

    in_far, in_near, in_relay = row_copies(0)
    out_far, out_near, out_relay = row_copies(1)
    ended += [in_far, in_near, in_relay, out_far, out_near, out_relay]
    r.found[0:span, :] = lowered(grad_h0)
    in_far.start()
    in_near.start()

    lane8 = iota((1, width), 1)
    row8 = iota((8, width), 0)
    stats = jnp.where(lane8 == 0, loss, 0.0)
    for i, number in enumerate((total_of(valid_lane), sum_hid, sum_attn, sum_ffn)):
        stats = jnp.where(lane8 == i + 1, number, stats)
    small = jnp.where(row8 == 0, gain_grad1, 0.0)
    small = jnp.where(row8 == 1, gain_grad2, small)
    small = jnp.where(row8 == 2, gain_grad3, small)
    r.small[0, 0] = jnp.where(row8 == 3, stats, small)
    l_base = wire.take(1)

    tell_small = to_members(r.small.at[0], l_base)
    tell_small.start()
    ended.append(tell_small)

    s_near.wait_recv()
    for first, value in pieces(2):
        got = raised(r.snear_got[1, first : first + strip, :])
        r.sfar_send[first : first + strip, :] = lowered(value + got)
    s_far.start()
    cand_side(0).wait_send()
    cand_side(0).wait_recv()
    r.own_s[...] = (
        r.h2_s[...] + raised(r.side_got[0]) - valid_col * raised(r.fin_s[0:span, :])
    )

    def add_line(k):
        cand_line(k).wait_recv()
        r.own_s[...] = r.own_s[...] + raised(r.line_got[k])

    loop(1, n_z, add_line)
    r.found[span : 2 * span, :] = lowered(r.own_s[...])
    out_far.start()
    out_near.start()

    ffn_line()

    in_far.wait_recv()
    in_relay.start()

    s_far.wait_recv()
    for first, value in pieces(0):
        rows = slice(first, first + strip)
        r.strip_s[rows, :] = (
            value + raised(r.snear_got[0, rows, :]) + raised(r.sfar_got[rows, :])
        )
    late_rows = 4 * strip
    if n_dp * strip_part > late_rows:
        r.strip_s[late_rows:, :] = jnp.zeros((n_dp * strip_part - late_rows, width), FULL)
    strip_side()

    order = here.y * n_z + here.z
    v_base = wire.take(4)

    def gather_dp(ref, size, base):
        own_part = ref.at[at(order, size)]
        own_column = ref.at[at(here.y, n_z * size)]

        def line(k):
            return wire.make(own_part, own_part, base, here.up(k))

        others = ref.at[pl.ds(0, (n_z - 1) * size)]
        lines = Joined(
            [line(k) for k in range(1, n_z)], wire.make(others, others, base, here.side())
        )
        return lines, wire.make(own_column, own_column, base + 1, here.side())

    ffn_all, ffn_all_side = gather_dp(r.whole_f, ffn_part, v_base)
    strip_all, strip_all_side = gather_dp(r.whole_t, strip_part, v_base + 2)
    ended += [ffn_all, strip_all, ffn_all_side, strip_all_side]
    mine = ffn_finish()
    squares = total_of(mine * mine)
    r.whole_f[at(order, ffn_part), :] = lowered(mine)
    ffn_all.start()
    tell_small.wait_recv()
    r.small[1, 0] = (r.small[0, 0] + r.small[0, 1]) + (r.small[0, 2] + r.small[0, 3])
    h_base = wire.take(2)

    def share(row, k, number):
        return wire.make(r.small.at[row, 0], r.small_dp.at[row // 4, d], number, here.ahead(k))

    def all_shares(row, number):
        others = r.small_dp.at[row // 4, pl.ds(0, n_dp - 1)]
        return wire.make(others, others, number, here.side())

    each(1, n_dp, lambda k: share(1, k, h_base).start())
    r.small_dp[0, d] = r.small[1, 0]

    out_far.wait_recv()
    out_relay.start()

    strip_line()

    in_near.wait_recv()
    in_relay.wait_recv()
    out_near.wait_recv()
    out_relay.wait_recv()

    g_base = wire.take(1)

    def outgoing(k):
        return pl.ds(pl.multiple_of(8 * span + k * cap, cap), cap)

    def ship(k):
        return wire.make(
            r.found.at[outgoing(k)], r.incoming.at[at(k, cap)], g_base, here.ahead(k)
        )

    def all_rows():
        rows = pl.ds(8 * span + cap, (n_dp - 1) * cap)
        landed = r.incoming.at[pl.ds(cap, (n_dp - 1) * cap)]
        return wire.make(r.found.at[rows], landed, g_base, here.side())

    places = pl.ds(8 * span, filled)
    if kept(n_dp):
        r.found[places, :] = lowered(dot(r.pick_s[...], r.found[0 : 8 * span, :]))
    else:
        marks_to = build_marks()

        def choose(k):
            chosen = picks(marks_to, k)
            r.found[outgoing(k), :] = lowered(dot(chosen, r.found[0 : 8 * span, :]))

        loop(0, n_dp, choose)
    ship(n_z).start()
    r.incoming[0:cap, :] = r.found[outgoing(0), :]

    mine = strip_finish()
    squares = squares + total_of(mine * mine)
    r.whole_t[at(order, strip_part), :] = lowered(mine)
    strip_all.start()
    each(1, n_z, lambda k: ship(k).start())
    each(n_z + 1, n_dp, lambda k: ship(k).start())

    several = min(n_dp, 8)

    def own_marks(g):
        for k in range(several):
            r.owned[:, k * 128 : (k + 1) * 128] = lowered(
                one_hot_columns(raised(r.asked[g * several + k]), rows_dev)
            )

    if n_dp == several:
        own_marks(0)

    ffn_all.wait_recv()
    ffn_all_side.start()

    strip_all.wait_recv()
    strip_all_side.start()

    strip_all_side.wait_recv()
    c_base = wire.take(6)

    def spread_strips(first, rows, base):
        part = pl.ds(first, rows)
        mine_at, far_at = r.strips.at[f, part], r.strips.at[far, part]
        copies = (
            wire.make(mine_at, mine_at, base, here.ffn(2)),
            wire.make(mine_at, mine_at, base + 1, here.ffn(1)),
            wire.make(far_at, far_at, base + 2, here.ffn(1)),
        )
        ended.extend(copies)
        return copies

    r.strips[f, 2 * strip :, :] = r.whole_t[0:late_rows, :]
    strip_far, strip_near, strip_relay = spread_strips(2 * strip, late_rows, c_base + 3)
    strip_far.start()
    strip_near.start()
    ffn_all_side.wait_recv()
    outs = [
        pltpu.make_async_copy(src, dst, r.load_sems.at[i])
        for i, (src, dst) in enumerate(
            (
                (r.whole_f.at[pl.ds(0, 2 * width)], r.ffn_out),
                (r.table_grad, r.table_out),
            )
        )
    ]

    def strip_out(s):
        place = here.member[s]
        return pltpu.make_async_copy(
            r.strips.at[place], r.strips_out.at[place], r.load_sems.at[2 + s]
        )

    outs[0].start()
    r.strips[f, 0 : 2 * strip, :] = r.whole_f[2 * width : early_rows, :]
    early_far, early_near, early_relay = spread_strips(0, 2 * strip, c_base)
    early_far.start()
    early_near.start()

    all_rows().wait_recv()

    if n_dp == several:
        r.table_grad[...] = dot(r.owned[...], r.incoming[...])
    else:
        r.table_grad[...] = jnp.zeros((rows_dev, width), FULL)
        r.padded_in[...] = jnp.zeros_like(r.padded_in)

        def add_rows(g):
            own_marks(g)
            for k in range(several):
                r.padded_in[k * 128 : k * 128 + cap, :] = r.incoming[
                    at(g * several + k, cap), :
                ]
            r.table_grad[...] = r.table_grad[...] + dot(r.owned[...], r.padded_in[...])

        loop(0, n_dp // several, add_rows)
    outs[1].start()
    table_grad = r.table_grad[...]
    squares = squares + total_of(table_grad * table_grad)

    r.small[3, 0] = jnp.broadcast_to(squares, (8, width))
    tell_norm = to_members(r.small.at[3], wire.take(1))
    tell_norm.start()
    ended.append(tell_norm)
    all_shares(1, h_base).wait_recv()
    tell_norm.wait_recv()
    r.small[4, 0] = (r.small[3, 0] + r.small[3, 1]) + (r.small[3, 2] + r.small[3, 3])

    each(1, n_dp, lambda k: share(4, k, h_base + 1).start())
    r.small_dp[1, d] = r.small[4, 0]
    early_far.wait_recv()
    early_relay.start()
    early_near.wait_recv()
    strip_near.wait_recv()
    strip_out(0).start()
    strip_out(1).start()
    strip_far.wait_recv()
    strip_relay.start()
    strip_out(2).start()
    all_shares(4, h_base + 1).wait_recv()
    totals, squares = r.small_dp[0, 0], r.small_dp[1, 0]
    for k in range(1, n_dp):
        totals = totals + r.small_dp[0, k]
        squares = squares + r.small_dp[1, k]
    gains = jnp.where(row8 < 3, totals, 0.0)
    norm = jnp.sqrt(squares + total_of(gains * gains))
    r.sums[...] = jnp.where(row8 == 4, norm, totals)

    all_rows().wait_send()
    all_shares(1, h_base).wait_send()
    all_shares(4, h_base + 1).wait_send()


    def end_line(k):
        cand_line(k).wait_send()

    each(1, n_z, end_line)

    ffn_end()
    strip_end()
    early_relay.wait_recv()
    strip_relay.wait_recv()
    strip_out(3).start()
    for copy in outs + [strip_out(s) for s in range(4)]:
        copy.wait()
    for copy in ended:
        copy.wait_send()
    assert wire.arrived <= r.recv_sems.shape[0]
    assert wire.most <= r.send_sems.shape[0]


def step(n_dp, cap, owner, row, lengths, count, table, wq, wo, w_in, w_back, gains, positions):
    rows_dev, width = table.shape
    span = owner.shape[1] // 4
    heads, n_z = width // HD, n_dp // 2
    shapes = plan(n_dp, cap, rows_dev, span, width, heads)
    names = INPUTS + OUTPUTS + list(shapes) + ["load_sems", "send_sems", "recv_sems"]
    vmem = pl.BlockSpec(memory_space=pltpu.VMEM)
    smem = pl.BlockSpec(memory_space=pltpu.SMEM)
    rest = pl.BlockSpec(memory_space=pl.ANY)
    sends, arrivals = 9 * n_z + 23, 20 * n_z + 48

    def out(kind, *shape):
        return jax.ShapeDtypeStruct(shape, kind)

    return pl.pallas_call(
        functools.partial(step_kernel, n_dp, cap, names),
        out_shape=(
            out(FULL, rows_dev, width),
            out(LOW, 2 * width, width),
            out(LOW, 4, 6 * span // 4, width),
            out(FULL, 8, width),
        ),
        in_specs=[vmem, vmem, smem, vmem, rest, rest, rest, rest, rest, vmem, rest],
        out_specs=(rest, rest, rest, vmem),
        scratch_shapes=[pltpu.VMEM(shape[:-1], shape[-1]) for shape in shapes.values()]
        + [
            pltpu.SemaphoreType.DMA((6,)),
            pltpu.SemaphoreType.DMA((sends,)),
            pltpu.SemaphoreType.DMA((arrivals,)),
        ],
        compiler_params=pltpu.CompilerParams(
            collective_id=0,
            has_side_effects=True,
            vmem_limit_bytes=63 * MIB,
        ),
        name="step",
    )(owner, row, lengths, count, table, wq, wo, w_in, w_back, gains, positions)


STATES = 21
GAINS = 5


def jobs(rows_dev, width):
    quarter = -(-rows_dev // 32) * 8
    result = []
    for first in range(0, rows_dev, quarter):
        result.append((0, first, min(quarter, rows_dev - first)))
    return result + [(3, 0, width), (4, 0, width), (1, 0, width), (6, 0, 2 * width), (2, 0, width)]


def update_kernel(rows_dev, table_grad, ffn_grad, strips, sums, *refs):
    ins, refs = refs[:STATES], refs[STATES:]
    loss_out, rms_out, norm_out = refs[:3]
    outs, refs = refs[3 : 3 + STATES], refs[3 + STATES :]
    held, made, refs = refs[:18], refs[18:36], refs[36:]
    table_s, ffn_s, strips_s, grad_sems, in_sems, out_sems = refs
    width = sums.shape[1]
    work = jobs(rows_dev, width)

    def kept_at(which, i):
        return 3 * (which if which < GAINS else which - 1) + i

    def moves(number):
        which, first, rows = work[number]
        part = pl.ds(first, rows)
        here = [kept_at(which, i) for i in range(3)]
        return (
            [
                pltpu.make_async_copy(
                    ins[3 * which + i].at[part],
                    held[here[i]].at[part],
                    in_sems.at[number, i],
                )
                for i in range(3)
            ],
            [
                pltpu.make_async_copy(
                    made[here[i]].at[part],
                    outs[3 * which + i].at[part],
                    out_sems.at[number, i],
                )
                for i in range(3)
            ],
        )

    grads = [
        pltpu.make_async_copy(table_grad, table_s, grad_sems.at[0]),
        pltpu.make_async_copy(ffn_grad, ffn_s, grad_sems.at[1]),
        pltpu.make_async_copy(strips, strips_s, grad_sems.at[2]),
    ]
    grads[0].start()
    for number in range(len(work)):
        for i, copy in enumerate(moves(number)[0]):
            copy.start(priority=(number + i) % 2)
        if number == 1:
            grads[1].start()
            grads[2].start()
    norm = sums[4:5, 0:1]
    factor = CLIP / jnp.maximum(norm, CLIP)
    corr_one = 1.0 - BETA_ONE**STEP
    corr_two = 1.0 - BETA_TWO**STEP

    def adam(which, rows, lanes, grad, rate):
        if which == GAINS:
            source, target = ins[3 * which : 3 * which + 3], outs[3 * which : 3 * which + 3]
        else:
            first = kept_at(which, 0)
            source, target = held[first : first + 3], made[first : first + 3]
        weight, moment, second = (ref[rows, lanes] for ref in source)
        clipped = raised(grad) * factor
        moment = BETA_ONE * moment + (1.0 - BETA_ONE) * clipped
        second = BETA_TWO * second + (1.0 - BETA_TWO) * clipped * clipped
        target[0][rows, lanes] = weight - rate * (
            moment / corr_one / (jnp.sqrt(second / corr_two) + ADAM_EPS) + DECAY * weight
        )
        target[1][rows, lanes] = moment
        target[2][rows, lanes] = second

    every = slice(None)
    strip = strips_s.shape[1] // 6
    waited = set()

    def need(i):
        if i not in waited:
            waited.add(i)
            grads[i].wait()

    for number, (which, first, rows) in enumerate(work):
        copies_in, copies_out = moves(number)
        need(0 if which == 0 else 1 if which in (3, 4) else 2)
        for copy in copies_in:
            copy.wait()
        if which == 0:
            part = slice(first, first + rows)
            adam(0, part, every, table_s[part, :], LEARN)
        elif which in (3, 4):
            start = (which - 3) * width
            adam(which, every, every, ffn_s[start : start + width, :], LEARN)
        for m in range(4):
            at_rows = slice(m * strip, (m + 1) * strip)
            if which == 1:
                for j, i in enumerate((2, 3, 1)):
                    lanes = slice(j * width, (j + 1) * width)
                    grad = strips_s[m, i * strip : (i + 1) * strip, :]
                    adam(1, at_rows, lanes, grad, LEARN)
            elif which == 2:
                adam(2, at_rows, every, strips_s[m, 0:strip, :], LEARN)
            elif which == 6:
                for u in range(2):
                    at_rows = slice((4 * u + m) * strip, (4 * u + m + 1) * strip)
                    grad = strips_s[m, (4 + u) * strip : (5 + u) * strip, :]
                    adam(6, at_rows, every, grad, LEARN)
        for copy in copies_out:
            copy.start()
    adam(GAINS, every, every, sums[0:3, :], GAIN_LEARN)
    stats = sums[3:4, :]
    roots = jnp.sqrt(stats / (stats[:, 1:2] * float(width)))

    def one(row, i):
        return jnp.sum(jnp.where(iota(row.shape, 1) == i, row, 0.0))

    loss_out[0] = one(stats, 0)
    loss_out[1] = one(stats, 1)
    for i in range(3):
        rms_out[i] = one(roots, 2 + i)
    norm_out[0] = one(sums[4:5, :], 0)
    for number in range(len(work)):
        for copy in moves(number)[1]:
            copy.wait()


def update(table_grad, ffn_grad, strips, sums, states):
    vmem = pl.BlockSpec(memory_space=pltpu.VMEM)
    smem = pl.BlockSpec(memory_space=pltpu.SMEM)
    rest = pl.BlockSpec(memory_space=pl.ANY)
    places = [vmem if i // 3 == GAINS else rest for i in range(STATES)]
    room = [pltpu.VMEM(a.shape, FULL) for i, a in enumerate(states) if i // 3 != GAINS]
    rows_dev, width = table_grad.shape
    number = len(jobs(rows_dev, width))
    return pl.pallas_call(
        functools.partial(update_kernel, rows_dev),
        out_shape=tuple(jax.ShapeDtypeStruct((n,), FULL) for n in (2, 3, 1))
        + tuple(jax.ShapeDtypeStruct(a.shape, FULL) for a in states),
        in_specs=[rest] * 3 + [vmem] + places,
        out_specs=[smem] * 3 + places,
        scratch_shapes=room
        + room
        + [pltpu.VMEM(a.shape, a.dtype) for a in (table_grad, ffn_grad, strips)]
        + [
            pltpu.SemaphoreType.DMA((3,)),
            pltpu.SemaphoreType.DMA((number, 3)),
            pltpu.SemaphoreType.DMA((number, 3)),
        ],
        compiler_params=pltpu.CompilerParams(vmem_limit_bytes=63 * MIB),
        name="update",
    )(table_grad, ffn_grad, strips, sums, *states)


def shards(
    item_owner,
    item_row,
    lengths,
    log_count,
    item_table,
    table_mom,
    table_sec,
    qkv_weight,
    qkv_mom,
    qkv_sec,
    out_weight,
    out_mom,
    out_sec,
    ffn_in,
    ffn_in_mom,
    ffn_in_sec,
    ffn_back,
    ffn_back_mom,
    ffn_back_sec,
    norm_gains,
    gains_mom,
    gains_sec,
    positions,
    positions_mom,
    positions_sec,
):
    n_dp = lax.axis_size("dp")
    tokens = item_owner.shape[0]
    cap = max(2, 4 * tokens // (n_dp * lax.axis_size("ffn")))
    table_grad, ffn_grad, strips, sums = step(
        n_dp,
        cap,
        item_owner.T,
        item_row.T,
        lengths,
        log_count,
        item_table,
        qkv_weight,
        out_weight,
        ffn_in,
        ffn_back,
        norm_gains,
        positions,
    )
    return update(
        table_grad,
        ffn_grad,
        strips,
        sums,
        (
            item_table,
            table_mom,
            table_sec,
            qkv_weight,
            qkv_mom,
            qkv_sec,
            out_weight,
            out_mom,
            out_sec,
            ffn_in,
            ffn_in_mom,
            ffn_in_sec,
            ffn_back,
            ffn_back_mom,
            ffn_back_sec,
            norm_gains,
            gains_mom,
            gains_sec,
            positions,
            positions_mom,
            positions_sec,
        ),
    )


def solution(mesh):
    whole, rows, table = P(), P("dp", None), P(("dp", "ffn"), None)
    wide, tall = P(None, "ffn"), P("ffn", None)
    states = (table,) * 3 + (whole,) * 6 + (wide,) * 3 + (tall,) * 3 + (whole,) * 6
    return jax.shard_map(
        shards,
        mesh=mesh,
        in_specs=(rows, rows, P("dp"), P(("dp", "ffn"))) + states,
        out_specs=(whole,) * 3 + states,
        check_vma=False,
    )
```

```python
import functools
import math
import types

import jax
import jax.numpy as jnp
from jax import lax
from jax.experimental import pallas as pl
from jax.experimental.pallas import tpu as pltpu
from jax.sharding import PartitionSpec as P

MESH = pl.DeviceIdType.MESH
MIB = 1024 * 1024
LOW, FULL = jnp.bfloat16, jnp.float32

EPS = 1e-06
NEG = -1e30
HD = 32
ROOT = math.sqrt(2.0 / math.pi)
LEARN = 0.05
GAIN_LEARN = 0.4
STEP = 5
BETA_ONE = 0.5
BETA_TWO = 0.5
DECAY = 0.01
ADAM_EPS = 1e-08
CLIP = 0.05


def lowered(value):
    return value.astype(LOW)


def raised(value):
    return value.astype(FULL)


def dot(left, right):
    return jnp.dot(left, right, preferred_element_type=FULL)


def against(left, right):
    return lax.dot_general(left, right, (((1,), (1,)), ((), ())), preferred_element_type=FULL)


def across(left, right):
    return lax.dot_general(left, right, (((0,), (0,)), ((), ())), preferred_element_type=FULL)


def iota(shape, dim):
    return lax.broadcasted_iota(jnp.int32, shape, dim)


def loop(first, last, body):
    def step(k, unused):
        body(k)
        return unused

    if last - first == 1:
        body(first)
    elif last > first:
        lax.fori_loop(first, last, step, 0)


def each(first, last, body):
    if last - first <= 8:
        for k in range(first, last):
            body(k)
    else:
        loop(first, last, body)


def at(index, size):
    if isinstance(index, int):
        return pl.ds(index * size, size)
    return pl.ds(pl.multiple_of(index * size, size), size)


def spread(row, lanes):
    return jnp.broadcast_to(row, (lanes, row.shape[1])).T


def turned(block):
    return lowered(raised(block).T)


def total_of(value):
    return jnp.sum(value, keepdims=True)


def one_hot_rows(row, width):
    high = jnp.floor(row * (1.0 / 128.0))
    low = spread(row - high * 128.0, 128)
    base = lowered(jnp.where(low == raised(iota(low.shape, 1)), 1.0, 0.0))
    high = lowered(spread(high, 128))
    zero = jnp.zeros_like(base)
    return jnp.concatenate(
        [jnp.where(high == jnp.asarray(b, LOW), base, zero) for b in range(width // 128)], 1
    )


def one_hot_columns(row, height):
    return jnp.where(raised(iota((height, row.shape[1]), 0)) == row, 1.0, 0.0)


def factor_of(hidden):
    return lax.rsqrt(jnp.mean(hidden * hidden, -1, keepdims=True) + EPS)


def rms_back(hidden, gain, upstream):
    factor = factor_of(hidden)
    scaled = upstream * gain
    inner = jnp.mean(scaled * hidden, -1, keepdims=True)
    grad_hidden = factor * scaled - hidden * (factor * factor * factor * inner)
    return grad_hidden, jnp.sum(upstream * hidden * factor, 0, keepdims=True)


class Peers:
    def __init__(self, n_dp):
        self.n_dp, self.n_z = n_dp, n_dp // 2
        self.d, self.f = lax.axis_index("dp"), lax.axis_index("ffn")
        self.z, self.y = self.d // 2, lax.rem(self.d, 2)
        near = self.f + 1 - 2 * lax.rem(self.f, 2)
        far = lax.rem(self.f + 2, 4)
        self.member = (self.f, near, far, 3 - self.f)

    def ffn(self, s):
        return (self.d, self.member[s])

    def ahead(self, i):
        return self.apart(i // self.n_z, i % self.n_z)

    def behind(self, i):
        return self.apart(i // self.n_z, self.n_z - i % self.n_z)

    def apart(self, ky, kz):
        z = lax.rem(self.z + kz, self.n_z)
        return (z * 2 + self.y + ky - 2 * self.y * ky, self.f)

    def side(self):
        return (self.d + 1 - 2 * self.y, self.f)

    def up(self, k):
        return (lax.rem(self.z + k, self.n_z) * 2 + self.y, self.f)

    def down(self, k):
        return (lax.rem(self.z + self.n_z - k, self.n_z) * 2 + self.y, self.f)

    def greet(self):
        barrier = pltpu.get_barrier_semaphore()

        def hello(where):
            pl.semaphore_signal(barrier, inc=1, device_id=where, device_id_type=MESH)

        for s in (1, 2, 3):
            hello(self.ffn(s))
        each(1, self.n_dp, lambda k: hello(self.ahead(k)))

    def met(self):
        pl.semaphore_wait(pltpu.get_barrier_semaphore(), self.n_dp + 2)


class Number:
    def __init__(self, leave, arrive, shared=False):
        self.leave, self.arrive, self.shared = leave, arrive, shared

    def __add__(self, k):
        return Number(self.leave if self.shared else self.leave + k, self.arrive + k, self.shared)


class Wire:
    def __init__(self, send, recv):
        self.send, self.recv = send, recv
        self.left, self.arrived, self.most = 0, 0, 0

    def take(self, number, arrivals=None, shared=False):
        result = Number(self.left, self.arrived, shared)
        self.left += 1 if shared else number
        self.arrived += number if arrivals is None else arrivals
        self.most = max(self.most, self.left)
        return result

    def renew(self):
        self.left = 0

    def make(self, src, dst, number, where, landing=None):
        return pltpu.make_async_remote_copy(
            src_ref=src,
            dst_ref=dst,
            send_sem=self.send.at[number.leave],
            recv_sem=self.recv.at[(landing or number).arrive],
            device_id=where,
            device_id_type=MESH,
        )


class Joined:
    def __init__(self, copies, all_of_them):
        self.copies, self.all = copies, all_of_them

    def start(self):
        for copy in self.copies:
            copy.start()

    def wait_recv(self):
        self.all.wait_recv()

    def wait_send(self):
        self.all.wait_send()


class Group:
    def __init__(self, *copies):
        self.copies = copies

    def start(self):
        for copy in self.copies:
            copy.start()

    def wait_recv(self):
        for copy in self.copies:
            copy.wait_recv()

    def wait_send(self):
        for copy in self.copies:
            copy.wait_send()


INPUTS = [
    "owner",
    "row",
    "lengths",
    "count",
    "table",
    "wq",
    "wo",
    "w_in",
    "w_back",
    "gains",
    "positions",
]
OUTPUTS = ["table_out", "ffn_out", "strips_out", "sums"]


def plan(n_dp, cap, rows_dev, span, width, heads):
    n_z = n_dp // 2
    filled = n_dp * cap
    padded = -(-rows_dev // 128) * 128
    square = (span, width)
    ffn_part, strip_part = parts(n_dp, span, width)
    return {
        "table_s": (rows_dev, width, FULL),
        "wq_s": (width, 3 * width, FULL),
        "wo_s": (width, width, FULL),
        "positions_s": (2 * span, width, FULL),
        "w_s": (2, width, width, FULL),
        "weights": (4, 2, width, width, LOW),
        "hot": (32 * n_dp, span, LOW),
        "slot_s": (8, span, FULL),
        "kind_s": (8, span, FULL),
        "table_low": (padded, width, LOW),
        "req": (n_dp, 1, 128, jnp.int32),
        "asked": (n_dp, 1, 128, jnp.int32),
        "send_rows": (n_dp, cap, width, LOW),
        "send_bias": (n_dp, 1, 128, FULL),
        "found": (4 * filled, width, LOW),
        "found_bias": (4 * n_dp, 1, 128, FULL),
        "bias_s": (8, span, FULL),
        "cands": (n_dp * span, width, LOW),
        "cand_bias": (n_dp, 8, span, FULL),
        "cand_t": (width, (n_dp if kept(n_dp) else 1) * span, LOW),
        "cand_col": ((n_dp if kept(n_dp) else 1) * span, 128, FULL),
        "logit_s": (6 * span if kept(n_dp) else 2 * span, span, FULL),
        "stat_s": (4, 8, span, FULL),
        "scale_s": (8, 4 * span, FULL),
        "expo_s": (n_dp * span if kept(n_dp) else 16, 4 * span, LOW),
        "wq16": (width, 3 * width, LOW),
        "wo16": (width, width, LOW),
        "h0_s": square + (FULL,),
        "n1_s": square + (LOW,),
        "q_s": square + (LOW,),
        "qt_s": (width, span, LOW),
        "k_s": (2 * span, width, LOW),
        "v_s": (2 * span, width, LOW),
        "kt_s": (width, 2 * span, LOW),
        "vt_s": (width, 2 * span, LOW),
        "mask_s": (2 * span, span, FULL),
        "p_s": (heads, 2 * span, span, FULL),
        "p16_s": (2 * span, heads * span, LOW),
        "stack_s": (heads * span, width, LOW),
        "mixt_s": (width, span, LOW),
        "h1_s": square + (FULL,),
        "h2_s": square + (FULL,),
        "n2t_s": (width, span, LOW),
        "pre_s": (4 * span, width, FULL),
        "act_s": (span, 4 * span, LOW),
        "fin_s": (4 * span, width, LOW),
        "fint_s": (width, 4 * span, LOW),
        "acc_s": (width, 4 * span, FULL),
        "acc_send": (3, width, span, LOW),
        "acc_got": (3, width, span, LOW),
        "mid_send": (3, 8, span, FULL),
        "mid_got": (3, 8, span, FULL),
        "tot_s": (4, 8, span, FULL),
        "cand_send": (n_z, span, width, LOW),
        "side_got": (n_z, span, width, LOW),
        "line_got": (n_z, span, width, LOW),
        "own_s": square + (FULL,),
        "dq_s": (width, span, FULL),
        "kv_s": (2 * span, width, FULL),
        "kv_got": (2 * span, width, FULL),
        "gf_s": (4, 2, width, width, FULL),
        "fnear_send": (2, 2 * width, width, LOW),
        "fnear_got": (2, 2 * width, width, LOW),
        "ffar_send": (2 * width, width, LOW),
        "ffar_got": (2 * width, width, LOW),
        "enear_send": (2, span // 2, width, LOW),
        "enear_got": (2, span // 2, width, LOW),
        "efar_send": (span // 2, width, LOW),
        "efar_got": (span // 2, width, LOW),
        "snear_send": (2, span, width, LOW),
        "snear_got": (2, span, width, LOW),
        "sfar_send": (span, width, LOW),
        "sfar_got": (span, width, LOW),
        "gv_s": square + (LOW,),
        "strip_s": (n_dp * strip_part, width, FULL),
        "fside_send": (n_z * ffn_part, width, LOW),
        "fside_got": (n_z * ffn_part, width, LOW),
        "fline_send": (n_z, ffn_part, width, LOW),
        "fline_got": (n_z, ffn_part, width, LOW),
        "sside_send": (n_z * strip_part, width, LOW),
        "sside_got": (n_z * strip_part, width, LOW),
        "sline_send": (n_z, strip_part, width, LOW),
        "sline_got": (n_z, strip_part, width, LOW),
        "whole_f": (n_dp * ffn_part, width, LOW),
        "whole_t": (n_dp * strip_part, width, LOW),
        "incoming": (filled, width, LOW),
        "place_s": (3 * span if kept(n_dp) else 16, 4 * filled if kept(n_dp) else 128, LOW),
        "placing_s": (3 * span if kept(n_dp) else 16, width, FULL),
        "placed_s": (3 * span if kept(n_dp) else 16, width, LOW),
        "pick_s": (filled if kept(n_dp) else 16, 8 * span, LOW),
        "padded_in": (8 * 128 if cap < 128 else 16, width, LOW),
        "owned": (rows_dev, min(n_dp, 8) * 128, LOW),
        "table_grad": (rows_dev, width, FULL),
        "strips": (4, 6 * span // 4, width, LOW),
        "small": (5, 4, 8, width, FULL),
        "small_dp": (2, n_dp, 8, width, FULL),
    }


def kept(n_dp):
    return n_dp <= 8


def parts(n_dp, span, width):
    return (
        -(-(2 * width + span // 2) // (16 * n_dp)) * 16,
        -(-span // (16 * n_dp)) * 16,
    )


def step_kernel(n_dp, cap, names, *refs):
    r = types.SimpleNamespace(**dict(zip(names, refs)))
    here = Peers(n_dp)
    wire = Wire(r.send_sems, r.recv_sems)
    d, f, n_z = here.d, here.f, here.n_z
    me, near, far, cross = here.member
    span, width = r.h0_s.shape
    heads = width // HD
    scale = HD ** (-0.5)
    half = lax.rem(f, 2)
    begin = half * span
    filled = n_dp * cap
    kinds = 4 * n_dp
    rows_dev = r.table_s.shape[0]
    padded = r.table_low.shape[0]
    ended = []

    here.greet()
    loads = [
        pltpu.make_async_copy(src, dst, r.load_sems.at[i])
        for i, (src, dst) in enumerate(
            (
                (r.table, r.table_s),
                (r.wq, r.wq_s),
                (r.wo, r.wo_s),
                (r.positions, r.positions_s),
                (r.w_in, r.w_s.at[0]),
                (r.w_back, r.w_s.at[1]),
            )
        )
    ]
    for i in (4, 5, 0, 1, 2, 3):
        loads[i].start()

    place = iota((kinds, span), 0)
    slot_of = jnp.zeros((kinds, span), jnp.int32)
    for s in (1, 2, 3):
        slot_of = slot_of + (place >= s * n_dp).astype(jnp.int32)
    steps = place - slot_of * n_dp
    other_y = (steps >= n_z).astype(jnp.int32)
    steps = steps - other_y * n_z + here.z
    steps = jnp.where(steps >= n_z, steps - n_z, steps)
    ahead = steps * 2 + here.y + other_y * (1 - 2 * here.y)
    named = ahead * 4 + jnp.where(
        slot_of == 0, me, jnp.where(slot_of == 1, near, jnp.where(slot_of == 2, far, cross))
    )

    def chunk_of(ref, c):
        return ref[c // 4 : c // 4 + 1, (c % 4) * span : (c % 4 + 1) * span]

    for c in range(8):
        r.hot[c * kinds : (c + 1) * kinds, :] = lowered(
            jnp.where(chunk_of(r.owner, c) == named, 1.0, 0.0)
        )
    before = lowered(jnp.where(iota((span, span), 0) < iota((span, span), 1), 1.0, 0.0))
    carry = jnp.zeros((kinds, 1), FULL)
    place_f = raised(place)
    asking = jnp.zeros((2 * n_dp, 128), FULL)
    for c in range(8):
        ones = raised(r.hot[c * kinds : (c + 1) * kinds, :])
        ranks = dot(r.hot[c * kinds : (c + 1) * kinds, :], before)
        slot = jnp.sum(ones * (ranks + carry), 0, keepdims=True)
        carry = carry + jnp.sum(ones, 1, keepdims=True)
        r.slot_s[c : c + 1, :] = slot
        r.kind_s[c : c + 1, :] = jnp.sum(ones * place_f, 0, keepdims=True)
        row = chunk_of(r.row, c)
        mine = ones[:n_dp]
        sought = jnp.concatenate([mine * raised(row >> 5), mine * raised(row & 31)], 0)
        asking = asking + against(lowered(sought), lowered(one_hot_columns(slot, 128)))
    wanted = (asking[:n_dp] * 32.0 + asking[n_dp:]).astype(jnp.int32)
    for k in range(n_dp):
        r.req[k, 0:1, :] = wanted[k : k + 1, :]
    r.asked[0] = r.req[0]
    q_base = wire.take(n_dp, shared=True)

    def ask(k):
        return wire.make(r.req.at[k], r.asked.at[k], q_base + k, here.ahead(k))

    here.met()
    each(1, n_dp, lambda k: ask(k).start())

    loads[4].wait()
    loads[5].wait()
    r.weights[0] = lowered(r.w_s[...])
    w_base = wire.take(3)
    w_near = wire.make(r.weights.at[0], r.weights.at[1], w_base, here.ffn(1))
    w_far = wire.make(r.weights.at[0], r.weights.at[2], w_base + 1, here.ffn(2))
    w_relay = wire.make(r.weights.at[2], r.weights.at[3], w_base + 2, here.ffn(1))
    w_far.start()
    w_near.start()

    def build_marks():
        for s in range(4):
            for column in range(2):
                chunk_row = pl.ds(column * 4 + here.member[s], 1)
                r.p16_s[0:cap, (2 * s + column) * span : (2 * s + column + 1) * span] = lowered(
                    one_hot_columns(r.slot_s[chunk_row, :], cap)
                )
        where_to = jnp.concatenate(
            [
                r.kind_s[pl.ds(column * 4 + here.member[s], 1), :]
                for s in range(4)
                for column in range(2)
            ],
            1,
        )
        where_to = lowered(jnp.broadcast_to(where_to, (16, 8 * span)))
        return where_to

    zero16 = jnp.zeros((16, 8 * span), LOW)

    def picks(where_to, k):
        wanted = where_to == lowered(jnp.full((16, 8 * span), k, FULL))
        return jnp.concatenate(
            [
                jnp.where(wanted, r.p16_s[i * 16 : (i + 1) * 16, :], zero16)
                for i in range(cap // 16)
            ],
            0,
        )

    def key_of(column, quarter):
        chunk = pl.ds(column * 4 + quarter, 1)
        return r.kind_s[chunk, :] * float(cap) + r.slot_s[chunk, :]

    if kept(n_dp):
        marks_to = build_marks()

        def keep_picks(k):
            r.pick_s[at(k, cap), :] = picks(marks_to, k)

        loop(0, n_dp, keep_picks)
        for i, (column, quarter) in enumerate(((1, f), (0, f), (0, near))):
            r.place_s[at(i, span), :] = one_hot_rows(key_of(column, quarter), 4 * filled)

    loads[0].wait()
    r.table_low[0:rows_dev, :] = lowered(r.table_s[...])
    if padded > rows_dev:
        r.table_low[rows_dev:padded, :] = jnp.zeros((padded - rows_dev, width), LOW)
    counts = lowered(jnp.broadcast_to(raised(r.count[...].reshape(1, rows_dev)), (8, rows_dev)))
    if padded > rows_dev:
        counts = jnp.concatenate([counts, jnp.zeros((8, padded - rows_dev), LOW)], 1)
    r_base, b_base = wire.take(n_dp, shared=True), wire.take(1)
    others = pl.ds(1, n_dp - 1)

    def reply(k):
        return wire.make(r.send_rows.at[k], r.found.at[at(k, cap)], r_base + k, here.behind(k))

    def reply_bias(k):
        return wire.make(r.send_bias.at[k], r.found_bias.at[k], b_base, here.behind(k))

    def all_replies():
        rest = r.found.at[pl.ds(cap, filled - cap)]
        return wire.make(r.send_rows.at[others], rest, r_base, here.side())

    def all_biases():
        return wire.make(r.send_bias.at[others], r.found_bias.at[others], b_base, here.side())

    def fetch(k):
        chosen = one_hot_rows(raised(r.asked[k]), padded)
        return lowered(dot(chosen, r.table_low[...]))[:cap], against(counts, chosen)[0:1, :]

    def serve(k):
        ask(k).wait_recv()
        rows, bias = fetch(k)
        r.send_rows[k] = rows
        r.send_bias[k] = bias
        reply(k).start()
        reply_bias(k).start()

    loop(1, n_dp, serve)
    rows, bias = fetch(0)
    r.found[0:cap, :] = rows
    r.found_bias[0] = bias
    cuts = [(k, 1) for k in range(n_dp)]
    passes = [wire.take(len(cuts), shared=True) for i in range(3)]
    bias_passes = [wire.take(1) for i in range(3)]

    def pass_on(i, source, target, number, who):
        sem = bias_passes[number] if i == len(cuts) else passes[number] + i
        if i == len(cuts):
            src, dst = (r.found_bias.at[at(slot, n_dp)] for slot in (source, target))
        else:
            first, several = cuts[i]
            src, dst = (
                r.found.at[pl.ds((slot * n_dp + first) * cap, several * cap)]
                for slot in (source, target)
            )
        return wire.make(src, dst, sem, here.ffn(who))

    def all_passes(source, number):
        rows = r.found.at[at(source, filled)]
        return wire.make(rows, rows, passes[number], here.side())

    def to_far(i):
        return pass_on(i, 0, 2, 0, 2)

    def to_near(i):
        return pass_on(i, 0, 1, 1, 1)

    def relay(i):
        return pass_on(i, 2, 3, 2, 1)

    def take_on(i):
        first, several = cuts[i]
        for k in range(max(first, 1), first + several):
            reply(k).wait_recv()
        to_far(i).start()
        to_near(i).start()

    def relay_on(i):
        to_far(i).wait_recv()
        relay(i).start()

    for i in range(len(cuts)):
        take_on(i)
        if i > 1:
            relay_on(i - 2)
    all_biases().wait_recv()
    to_far(len(cuts)).start()
    to_near(len(cuts)).start()
    w_far.wait_recv()
    w_relay.start()
    relay_on(len(cuts) - 2)
    for i in range(len(cuts)):
        to_near(i).wait_recv()
    if kept(n_dp):
        r.placing_s[...] = dot(r.place_s[:, : 2 * filled], r.found[0 : 2 * filled, :])
    relay_on(len(cuts) - 1)
    relay_on(len(cuts))
    loads[1].wait()
    loads[2].wait()
    r.wq16[...] = lowered(r.wq_s[...])
    r.wo16[...] = lowered(r.wo_s[...])
    for i in range(len(cuts)):
        relay(i).wait_recv()

    if kept(n_dp):
        far_rows = dot(r.place_s[:, 2 * filled :], r.found[2 * filled :, :])
        r.placed_s[...] = lowered(r.placing_s[...] + far_rows)

    def chosen_rows(i):
        if kept(n_dp):
            return r.placed_s[at(i, span), :]
        column, quarter = ((1, f), (0, f), (0, near))[i]
        return lowered(dot(one_hot_rows(key_of(column, quarter), 4 * filled), r.found[...]))

    r.cands[0:span, :] = chosen_rows(0)
    to_near(len(cuts)).wait_recv()
    relay(len(cuts)).wait_recv()
    bias_rows = lowered(r.found_bias[:, 0, :].T)
    lane = iota((1, span), 1)
    length = r.lengths[f // 2]
    valid_lane = jnp.where(lane + begin < length, 1.0, 0.0)
    valid_col = jnp.where(iota((span, 1), 0) + begin < length, 1.0, 0.0)
    chunk = 4 + f
    marks = one_hot_columns(r.slot_s[pl.ds(chunk, 1), :], 128)
    bias = jnp.sum(dot(bias_rows, r.hot[at(chunk, kinds), :]) * marks, 0, keepdims=True)
    r.bias_s[...] = jnp.broadcast_to(bias, (8, span))
    r.cand_bias[0] = jnp.broadcast_to(jnp.where(lane + begin < length, -bias, NEG), (8, span))
    z_base, y_base = wire.take(0, 3 * n_z), wire.take(3 * n_z)
    u_base = wire.take(6 * n_z, 0)
    has_up, has_down = here.z + 1 < n_z, here.z > 0

    def slot(k, ky):
        if isinstance(k, int) and k == 0:
            return ky
        return 1 + k + ky * (n_z - 1)

    half_rows = span // 2

    def half_of(i, h):
        first = i * span + h * half_rows
        if not isinstance(first, int):
            first = pl.multiple_of(first, half_rows)
        return r.cands.at[pl.ds(first, half_rows)]

    def offer_line(source, target, number, where):
        i, j = slot(source, 0), slot(target, 0)
        first, second = (
            wire.make(
                half_of(i, h),
                half_of(j, h),
                number + 2 * n_z * h,
                where,
                z_base + (n_z * h + target),
            )
            for h in range(2)
        )
        bias = wire.make(
            r.cand_bias.at[i],
            r.cand_bias.at[j],
            number + 4 * n_z,
            where,
            z_base + (2 * n_z + target),
        )
        return first, Group(second, bias)

    def send_up(a):
        return offer_line(a, a + 1, u_base + a, here.up(1))

    def send_down(b):
        source = b if isinstance(b, int) and b == 0 else n_z - b
        return offer_line(source, n_z - 1 - b, u_base + (n_z + b), here.down(1))

    def offer_side(k):
        i, j = slot(k, 0), slot(k, 1)
        first, second = (
            wire.make(half_of(i, h), half_of(j, h), y_base + (n_z * h + k), here.side())
            for h in range(2)
        )
        bias = wire.make(
            r.cand_bias.at[i], r.cand_bias.at[j], y_base + (2 * n_z + k), here.side()
        )
        return first, Group(second, bias)

    for h in range(2):
        pl.when(has_up)(lambda: send_up(0)[h].start())
        pl.when(has_down)(lambda: send_down(0)[h].start())
    for h in range(2):
        offer_side(0)[h].start()

    def hand_on(j):
        @pl.when(here.z >= j)
        def from_below():
            for h in range(2):
                offer_line(0, j, u_base, here.up(1))[h].wait_recv()
                pl.when(has_up)(lambda: send_up(j)[h].start())
                offer_side(j)[h].start()

        @pl.when(here.z + j < n_z)
        def from_above():
            for h in range(2):
                offer_line(0, n_z - j, u_base, here.up(1))[h].wait_recv()
                pl.when(has_down)(lambda: send_down(j)[h].start())
                offer_side(n_z - j)[h].start()

    loads[3].wait()
    gain1, gain2, gain3 = r.gains[0:1, :], r.gains[1:2, :], r.gains[2:3, :]
    hidden0 = raised(chosen_rows(1)) + r.positions_s[at(half, span), :]
    r.h0_s[...] = hidden0
    normed1 = lowered(hidden0 * factor_of(hidden0) * gain1)
    r.n1_s[...] = normed1
    r.q_s[...] = lowered(dot(normed1, r.wq16[:, :width]))
    r.k_s[0:span, :] = lowered(dot(normed1, r.wq16[:, width : 2 * width]))
    r.v_s[0:span, :] = lowered(dot(normed1, r.wq16[:, 2 * width :]))
    hidden0 = raised(chosen_rows(2)) + r.positions_s[at(1 - half, span), :]
    normed1 = lowered(hidden0 * factor_of(hidden0) * gain1)
    r.k_s[span:, :] = lowered(dot(normed1, r.wq16[:, width : 2 * width]))
    r.v_s[span:, :] = lowered(dot(normed1, r.wq16[:, 2 * width :]))
    r.qt_s[...] = turned(r.q_s[...])
    r.kt_s[...] = turned(r.k_s[...])
    r.vt_s[...] = turned(r.v_s[...])
    key_at = iota((2 * span, span), 0)
    key_at = jnp.where(key_at < span, key_at + begin, key_at - begin)
    allowed = (key_at <= iota((2 * span, span), 1) + begin) & (key_at < length)
    r.mask_s[...] = jnp.where(allowed, 0.0, NEG)
    row_head = iota((width, span), 0) // HD
    lane_head = iota((span, width), 1) // HD

    def forward_head(h):
        rows = at(h, HD)
        mine = jnp.where(row_head == h, raised(r.qt_s[...]), 0.0)
        scores = dot(r.k_s[...], lowered(mine)) * scale + r.mask_s[...]
        expo = jnp.exp(scores - jnp.max(scores, 0, keepdims=True))
        probs = expo / jnp.sum(expo, 0, keepdims=True)
        r.p_s[h] = probs
        low_probs = lowered(probs)
        r.p16_s[:, at(h, span)] = low_probs
        r.mixt_s[rows, :] = lowered(dot(r.vt_s[rows, :], low_probs))

    loop(0, heads * 3 // 4, forward_head)
    hand_on(1)
    loop(heads * 3 // 4, heads, forward_head)
    attn = dot(turned(r.mixt_s[...]), r.wo16[...])
    hidden1 = r.h0_s[...] + attn
    r.h1_s[...] = hidden1
    sum_attn = total_of(valid_col * attn * attn)
    normed2 = lowered(hidden1 * factor_of(hidden1) * gain2)
    r.n2t_s[...] = turned(normed2)
    w_near.wait_recv()
    w_relay.wait_recv()
    for s in range(4):
        pre = dot(normed2, r.weights[s, 0])
        r.pre_s[s * span : (s + 1) * span, :] = pre
        inner = jnp.tanh(ROOT * (pre + 0.044715 * pre * pre * pre))
        r.act_s[:, s * span : (s + 1) * span] = lowered(0.5 * pre * (1.0 + inner))
    branch = dot(r.act_s[...], jnp.concatenate([r.weights[s, 1] for s in range(4)], 0))
    hidden2 = r.h1_s[...] + branch
    r.h2_s[...] = hidden2
    sum_ffn = total_of(valid_col * branch * branch)
    sum_hid = total_of(valid_col * hidden2 * hidden2)
    final = lowered(hidden2 * factor_of(hidden2) * gain3)
    r.fin_s[0:span, :] = final
    f_base = wire.take(3)
    fin = [r.fin_s.at[at(s, span)] for s in range(4)]
    fin_near = wire.make(fin[0], fin[1], f_base, here.ffn(1))
    fin_far = wire.make(fin[0], fin[2], f_base + 1, here.ffn(2))
    fin_relay = wire.make(fin[2], fin[3], f_base + 2, here.ffn(1))
    fin_far.start()
    fin_near.start()
    ended += [fin_far, fin_near, fin_relay]

    def turn_fin(s):
        r.fint_s[:, s * span : (s + 1) * span] = turned(r.fin_s[s * span : (s + 1) * span, :])

    turn_fin(0)
    if n_z > 2:
        hand_on(2)

    def prepare(i):
        if kept(n_dp):
            r.cand_t[:, at(i, span)] = turned(r.cands[at(i, span), :])
            r.cand_col[at(i, span), :] = spread(r.cand_bias[i, 0:1, :], 128)

    def columns(i, number):
        if kept(n_dp):
            return r.cand_col[slots(i, number), :]
        rows = [spread(r.cand_bias[i + j, 0:1, :], 128) for j in range(number)]
        return jnp.concatenate(rows, 0)

    def slots(i, number):
        if isinstance(i, int):
            return pl.ds(i * span, number * span)
        return pl.ds(pl.multiple_of(i * span, span), number * span)

    prepare(0)
    for copy in offer_side(0):
        copy.wait_recv()
    prepare(1)
    r.acc_s[...] = jnp.zeros_like(r.acc_s)
    for s in range(4):
        r.stat_s[s, 0:1, :] = jnp.full((1, span), NEG, FULL)
        r.stat_s[s, 1:2, :] = jnp.zeros((1, span), FULL)

    def count_in(s, i, number, group):
        lanes = slice(s * span, (s + 1) * span)
        rows = slots(i, number)
        first = s % 2 * 3 * span if kept(n_dp) else 0
        held = slice(first, first + number * span)
        logits = dot(r.cands[rows, :], r.fint_s[:, lanes])
        r.logit_s[held, :] = logits + jnp.concatenate([columns(i, number)] * (span // 128), 1)
        top = r.stat_s[s, 0:1, :]
        higher = jnp.maximum(top, jnp.max(r.logit_s[held, :], 0, keepdims=True))
        shrink = jnp.exp(top - higher)
        expo = jnp.exp(r.logit_s[held, :] - higher)
        r.stat_s[s, 0:1, :] = higher
        r.stat_s[s, 1:2, :] = r.stat_s[s, 1:2, :] * shrink + jnp.sum(expo, 0, keepdims=True)
        if kept(n_dp):
            low_expo = lowered(expo)
            r.expo_s[rows, lanes] = low_expo
            r.stat_s[s, 2 + group : 3 + group, :] = higher
            part = dot(r.cand_t[:, rows], low_expo)
        else:
            part = across(r.cands[rows, :], lowered(expo))
        r.acc_s[:, lanes] = r.acc_s[:, lanes] * shrink + part

    def count(s, group):
        first = (0, 2, n_z + 1)[group]
        number = (2, n_z - 1, n_z - 1)[group]
        if number <= 3:
            if number:
                count_in(s, first, number, group)
        else:
            loop(first, first + number, lambda i: count_in(s, i, 1, group))

    count(0, 0)
    fin_near.wait_recv()
    turn_fin(1)
    count(1, 0)
    fin_far.wait_recv()
    fin_relay.start()
    turn_fin(2)
    loop(3, n_z, hand_on)
    count(2, 0)
    fin_relay.wait_recv()
    turn_fin(3)
    count(3, 0)
    loop(2, n_z + 1, prepare)
    count(3, 1)
    count(2, 1)
    count(0, 1)
    count(1, 1)

    def prepare_side(k):
        for copy in offer_side(k):
            copy.wait_recv()
        prepare(slot(k, 1))

    loop(1, n_z, prepare_side)

    a_base = wire.take(6)

    def give(i, who):
        return Group(
            wire.make(r.acc_send.at[i], r.acc_got.at[i], a_base + 2 * i, here.ffn(who)),
            wire.make(r.mid_send.at[i], r.mid_got.at[i], a_base + 2 * i + 1, here.ffn(who)),
        )

    gives = [give(0, 1), give(1, 1), give(2, 2)]
    ended += gives

    def fill(i, s):
        r.acc_send[i] = lowered(r.acc_s[:, s * span : (s + 1) * span])
        r.mid_send[i] = r.stat_s[s]
        gives[i].start()

    def merge(s, i):
        gives[i].wait_recv()
        lanes = slice(s * span, (s + 1) * span)
        top, other = r.stat_s[s, 0:1, :], r.mid_got[i, 0:1, :]
        higher = jnp.maximum(top, other)
        left, right = jnp.exp(top - higher), jnp.exp(other - higher)
        r.acc_s[:, lanes] = r.acc_s[:, lanes] * left + raised(r.acc_got[i]) * right
        r.stat_s[s, 0:1, :] = higher
        r.stat_s[s, 1:2, :] = r.stat_s[s, 1:2, :] * left + r.mid_got[i, 1:2, :] * right

    count(3, 2)
    fill(0, 3)
    count(2, 2)
    merge(2, 0)
    fill(2, 2)
    count(1, 2)
    fill(1, 1)
    count(0, 2)
    merge(0, 1)
    for s in range(4):
        rows = slice(s * span, (s + 1) * span)
        pre = r.pre_s[rows, :]
        inner = jnp.tanh(ROOT * (pre + 0.044715 * pre * pre * pre))
        r.pre_s[rows, :] = 0.5 * (1.0 + inner) + 0.5 * pre * (1.0 - inner * inner) * (
            ROOT * (1.0 + 3.0 * 0.044715 * pre * pre)
        )
    merge(0, 2)
    total = r.stat_s[0, 1:2, :]
    log_total = r.stat_s[0, 0:1, :] + jnp.log(total)
    r.tot_s[0] = jnp.broadcast_to(jnp.where(valid_lane > 0, log_total, -NEG), (8, span))
    for copy in (
        all_passes(0, 0),
        all_passes(0, 1),
        all_passes(2, 2),
        to_far(len(cuts)),
        to_near(len(cuts)),
        relay(len(cuts)),
    ):
        copy.wait_send()

    t_base = wire.take(1)

    def to_members(ref, number):
        three = ref.at[pl.ds(1, 3)]
        return Joined(
            [wire.make(ref.at[0], ref.at[s], number, here.ffn(s)) for s in (1, 2, 3)],
            wire.make(three, three, number, here.side()),
        )

    tell = to_members(r.tot_s, t_base)
    tell.start()
    ended.append(tell)
    if not kept(n_dp):
        r.cand_t[...] = turned(r.cands[0:span, :])
    target_t = raised(r.cand_t[:, 0:span])
    positive = (
        jnp.sum(raised(r.fint_s[:, :span]) * target_t, 0, keepdims=True) - r.bias_s[0:1, :]
    )
    loss = total_of(valid_lane * (log_total - positive))
    grad_final = ((r.acc_s[:, 0:span] / total - target_t) * valid_lane).T

    grad_h2, gain_grad3 = rms_back(r.h2_s[...], gain3, grad_final)
    up = lowered(grad_h2)
    r.h2_s[...] = grad_h2
    for s in (1, 3, 2, 0):
        lanes = slice(s * span, (s + 1) * span)
        r.gf_s[s, 1] = across(r.act_s[:, lanes], up)
        grad_act = against(up, r.weights[s, 1])
        grad_pre = lowered(grad_act * r.pre_s[s * span : (s + 1) * span, :])
        r.gf_s[s, 0] = dot(r.n2t_s[...], grad_pre)
        r.act_s[:, lanes] = grad_pre
    for i, s in enumerate((1, 3)):
        for j in range(2):
            r.fnear_send[i, j * width : (j + 1) * width, :] = lowered(r.gf_s[s, j])
    all_asks = wire.make(r.req.at[others], r.req.at[others], q_base, here.side())
    for copy in (all_asks, all_replies(), all_biases(), w_far, w_near, w_relay):
        copy.wait_send()
    def end_offers(j):
        for h in range(2):
            pl.when(has_up & (here.z >= j))(lambda: send_up(j)[h].wait_send())
            pl.when(has_down & (here.z + j < n_z))(lambda: send_down(j)[h].wait_send())
            offer_side(j)[h].wait_send()

    each(0, n_z, end_offers)
    for copy in ended:
        copy.wait_send()
    ended.clear()
    wire.renew()
    e_base = wire.take(6)
    f_near = wire.make(r.fnear_send, r.fnear_got, e_base, here.ffn(1))
    f_far = wire.make(r.ffar_send, r.ffar_got, e_base + 1, here.ffn(2))
    s_near = wire.make(r.snear_send, r.snear_got, e_base + 2, here.ffn(1))
    s_far = wire.make(r.sfar_send, r.sfar_got, e_base + 3, here.ffn(2))
    e_near = wire.make(r.enear_send, r.enear_got, e_base + 4, here.ffn(1))
    e_far = wire.make(r.efar_send, r.efar_got, e_base + 5, here.ffn(2))
    ended += [f_near, f_far, s_near, s_far, e_near, e_far]
    f_near.start()

    grad_normed2 = against(
        r.act_s[...], jnp.concatenate([r.weights[s, 0] for s in range(4)], 1)
    )
    grad_h1_norm, gain_grad2 = rms_back(r.h1_s[...], gain2, grad_normed2)
    grad_h1 = r.h2_s[...] + grad_h1_norm
    r.h1_s[...] = grad_h1
    tell.wait_recv()
    if kept(n_dp):
        for s in range(4):
            for group in range(3):
                level = r.stat_s[s, 2 + group : 3 + group, :] - r.tot_s[s, 0:1, :]
                r.scale_s[group : group + 1, s * span : (s + 1) * span] = jnp.exp(level)
    side_base, line_base = wire.take(n_z), wire.take(n_z)

    def cand_side(k):
        return wire.make(r.cand_send.at[k], r.side_got.at[k], side_base + k, here.side())

    def cand_line(k):
        return wire.make(r.cand_send.at[k], r.line_got.at[k], line_base + k, here.down(k))

    def cand_grad(i):
        if kept(n_dp):
            group = jnp.where(i < 2, 0, jnp.where(i <= n_z, 1, 2))
            share_of = r.scale_s[pl.ds(group, 1), :]
            weights = raised(r.expo_s[at(i, span), :]) * share_of
            return dot(lowered(weights), r.fin_s[...])
        column = jnp.concatenate([columns(i, 1)] * (4 * span // 128), 1)
        level = jnp.concatenate([r.tot_s[s, 0:1, :] for s in range(4)], 1)
        logits = dot(r.cands[at(i, span), :], r.fint_s[...]) + column
        return dot(lowered(jnp.exp(logits - level)), r.fin_s[...])

    def slot_at(k, ky):
        return jnp.where(k == 0, ky, 1 + k + ky * (n_z - 1))

    def side_step(k):
        r.cand_send[k] = lowered(cand_grad(slot_at(k, 1)))
        cand_side(k).start()

    def line_step(k):
        grad = cand_grad(slot_at(k, 0))
        cand_side(k).wait_send()
        cand_side(k).wait_recv()
        r.cand_send[k] = lowered(grad + raised(r.side_got[k]))
        cand_line(k).start()

    middle = n_z // 2
    side_step(middle)
    loop(1, middle, side_step)
    loop(middle + 1, n_z, side_step)
    if middle:
        side_step(0)

    f_near.wait_recv()
    for j in range(2):
        rows = slice(j * width, (j + 1) * width)
        r.ffar_send[rows, :] = lowered(r.gf_s[2, j] + raised(r.fnear_got[1, rows, :]))
    f_far.start()

    attn_up = lowered(grad_h1)
    r.acc_s[:, 3 * width :] = dot(r.mixt_s[...], attn_up)
    grad_mixed = lowered(against(attn_up, r.wo16[...]))
    grad_mixed_f = raised(grad_mixed)
    r.mixt_s[...] = turned(grad_mixed)
    for h in range(heads):
        r.stack_s[h * span : (h + 1) * span, :] = lowered(
            jnp.where(lane_head == h, grad_mixed_f, 0.0)
        )
    r.kv_s[...] = dot(r.p16_s[...], r.stack_s[...])
    r.logit_s[span : 2 * span, :] = r.kv_s[span:, :]
    r.own_s[...] = r.kv_s[0:span, :]
    k_base = wire.take(2)

    def lend(i):
        rows = at(i, span)
        return wire.make(r.logit_s.at[rows], r.kv_got.at[rows], k_base + i, here.ffn(1))

    lend_k, lend_v = lend(0), lend(1)
    ended += [lend_k, lend_v]
    lend_v.start()

    def backward_head(h):
        rows = at(h, HD)
        mine = jnp.where(row_head == h, raised(r.mixt_s[...]), 0.0)
        grad_probs = dot(r.v_s[...], lowered(mine))
        probs = r.p_s[h]
        inner = jnp.sum(probs * grad_probs, 0, keepdims=True)
        grad_scores = lowered(probs * (grad_probs - inner))
        r.p16_s[:, at(h, span)] = grad_scores
        r.dq_s[rows, :] = dot(r.kt_s[rows, :], grad_scores) * scale

    loop(0, heads // 2, backward_head)
    if middle:
        line_step(middle)
    strip = span // 4
    halves = (jnp.where(half == 0, 1.0, 0.0), jnp.where(half == 1, 1.0, 0.0))

    def strip_at(s):
        return pl.ds(pl.multiple_of(here.member[s] * strip, strip), strip)

    def early_pieces(s):
        yield 0, r.acc_s[strip_at(s), 3 * width :]
        yield strip, r.acc_s[strip_at(s), 2 * width : 3 * width]

    def pieces(s):
        for j in range(2):
            yield j * strip, r.acc_s[strip_at(s), j * width : (j + 1) * width]
        for u in range(2):
            yield (2 + u) * strip, r.h0_s[strip_at(s), :] * halves[u]

    lend_v.wait_recv()
    r.gv_s[...] = lowered(r.own_s[...] + r.kv_got[span:, :])
    r.acc_s[:, 2 * width : 3 * width] = across(r.n1_s[...], r.gv_s[...])
    for i, s in enumerate((1, 3)):
        for first, value in early_pieces(s):
            r.enear_send[i, first : first + strip, :] = lowered(value)
    e_near.start()
    loop(heads // 2, heads, backward_head)
    loop(1, middle, line_step)
    e_near.wait_recv()
    for first, value in early_pieces(2):
        got = raised(r.enear_got[1, first : first + strip, :])
        r.efar_send[first : first + strip, :] = lowered(value + got)
    e_far.start()
    queries = raised(r.q_s[...])
    for h in range(heads):
        r.stack_s[h * span : (h + 1) * span, :] = lowered(jnp.where(lane_head == h, queries, 0.0))
    r.kv_s[...] = dot(r.p16_s[...], r.stack_s[...]) * scale
    r.logit_s[0:span, :] = r.kv_s[span:, :]
    lend_k.start()
    loop(middle + 1, n_z, line_step)
    r.h2_s[...] = cand_grad(0)
    ffn_part, strip_part = parts(n_dp, span, width)
    f_far.wait_recv()
    for j in range(2):
        rows = slice(j * width, (j + 1) * width)
        r.pre_s[rows, :] = (
            r.gf_s[0, j] + raised(r.fnear_got[0, rows, :]) + raised(r.ffar_got[rows, :])
        )
    e_far.wait_recv()
    early_rows = 2 * width + 2 * strip
    for first, value in early_pieces(0):
        rows = slice(first, first + strip)
        r.pre_s[2 * width + first : 2 * width + first + strip, :] = (
            value + raised(r.enear_got[0, rows, :]) + raised(r.efar_got[rows, :])
        )
    if n_dp * ffn_part > early_rows:
        r.pre_s[early_rows : n_dp * ffn_part, :] = jnp.zeros(
            (n_dp * ffn_part - early_rows, width), FULL
        )
    m_base = wire.take(2 + 2 * n_z)

    def sum_dp(source, size, side_send, side_got, line_send, line_got, base):
        def rows_of(k, y):
            return at(y * n_z + lax.rem(here.z + k, n_z), size)

        across_y = wire.make(side_send, side_got, base, here.side())

        def along(k):
            return wire.make(line_send.at[k], line_got.at[k], base + 1 + k, here.up(k))

        def begin_side():
            def fill_side(k):
                side_send[at(k, size), :] = lowered(source[rows_of(k, 1 - here.y), :])

            loop(0, n_z, fill_side)
            across_y.start()

        def begin_line():
            across_y.wait_recv()

            def fill_line(k):
                line_send[k] = lowered(
                    source[rows_of(k, here.y), :] + raised(side_got[at(k, size), :])
                )
                along(k).start()

            loop(1, n_z, fill_line)

        def finish():
            value = source[rows_of(0, here.y), :] + raised(side_got[0:size, :])
            for k in range(1, n_z):
                along(k).wait_recv()
                value = value + raised(line_got[k])
            return value

        def end():
            across_y.wait_send()
            each(1, n_z, lambda k: along(k).wait_send())

        return begin_side, begin_line, finish, end

    ffn_side, ffn_line, ffn_finish, ffn_end = sum_dp(
        r.pre_s,
        ffn_part,
        r.fside_send,
        r.fside_got,
        r.fline_send,
        r.fline_got,
        m_base,
    )
    strip_side, strip_line, strip_finish, strip_end = sum_dp(
        r.strip_s,
        strip_part,
        r.sside_send,
        r.sside_got,
        r.sline_send,
        r.sline_got,
        m_base + 1 + n_z,
    )
    ffn_side()


    grad_q = lowered(r.dq_s[...].T)
    lend_k.wait_recv()
    grad_qk = jnp.concatenate(
        [grad_q, lowered(r.kv_s[0:span, :] + r.kv_got[0:span, :])],
        1,
    )
    grad_united = jnp.concatenate([grad_qk, r.gv_s[...]], 1)
    grad_h0_norm, gain_grad1 = rms_back(r.h0_s[...], gain1, against(grad_united, r.wq16[...]))
    grad_h0 = r.h1_s[...] + grad_h0_norm
    r.h0_s[...] = grad_h0

    r.acc_s[:, : 2 * width] = across(r.n1_s[...], grad_qk)

    for i, s in enumerate((1, 3)):
        for first, value in pieces(s):
            r.snear_send[i, first : first + strip, :] = lowered(value)
    s_near.start()

    o_base = wire.take(6)

    def chunk(s, column):
        return r.found.at[at(2 * s + column, span)]

    def row_copies(column):
        return (
            wire.make(chunk(0, column), chunk(2, column), o_base + 3 * column, here.ffn(2)),
            wire.make(chunk(0, column), chunk(1, column), o_base + 3 * column + 1, here.ffn(1)),
            wire.make(chunk(2, column), chunk(3, column), o_base + 3 * column + 2, here.ffn(1)),
        )

    in_far, in_near, in_relay = row_copies(0)
    out_far, out_near, out_relay = row_copies(1)
    ended += [in_far, in_near, in_relay, out_far, out_near, out_relay]
    r.found[0:span, :] = lowered(grad_h0)
    in_far.start()
    in_near.start()

    lane8 = iota((1, width), 1)
    row8 = iota((8, width), 0)
    stats = jnp.where(lane8 == 0, loss, 0.0)
    for i, number in enumerate((total_of(valid_lane), sum_hid, sum_attn, sum_ffn)):
        stats = jnp.where(lane8 == i + 1, number, stats)
    small = jnp.where(row8 == 0, gain_grad1, 0.0)
    small = jnp.where(row8 == 1, gain_grad2, small)
    small = jnp.where(row8 == 2, gain_grad3, small)
    r.small[0, 0] = jnp.where(row8 == 3, stats, small)
    l_base = wire.take(1)

    tell_small = to_members(r.small.at[0], l_base)
    tell_small.start()
    ended.append(tell_small)

    s_near.wait_recv()
    for first, value in pieces(2):
        got = raised(r.snear_got[1, first : first + strip, :])
        r.sfar_send[first : first + strip, :] = lowered(value + got)
    s_far.start()
    cand_side(0).wait_send()
    cand_side(0).wait_recv()
    r.own_s[...] = (
        r.h2_s[...] + raised(r.side_got[0]) - valid_col * raised(r.fin_s[0:span, :])
    )

    def add_line(k):
        cand_line(k).wait_recv()
        r.own_s[...] = r.own_s[...] + raised(r.line_got[k])

    loop(1, n_z, add_line)
    r.found[span : 2 * span, :] = lowered(r.own_s[...])
    out_far.start()
    out_near.start()

    ffn_line()

    in_far.wait_recv()
    in_relay.start()

    s_far.wait_recv()
    for first, value in pieces(0):
        rows = slice(first, first + strip)
        r.strip_s[rows, :] = (
            value + raised(r.snear_got[0, rows, :]) + raised(r.sfar_got[rows, :])
        )
    late_rows = 4 * strip
    if n_dp * strip_part > late_rows:
        r.strip_s[late_rows:, :] = jnp.zeros((n_dp * strip_part - late_rows, width), FULL)
    strip_side()

    order = here.y * n_z + here.z
    v_base = wire.take(4)

    def gather_dp(ref, size, base):
        own_part = ref.at[at(order, size)]
        own_column = ref.at[at(here.y, n_z * size)]

        def line(k):
            return wire.make(own_part, own_part, base, here.up(k))

        others = ref.at[pl.ds(0, (n_z - 1) * size)]
        lines = Joined(
            [line(k) for k in range(1, n_z)], wire.make(others, others, base, here.side())
        )
        return lines, wire.make(own_column, own_column, base + 1, here.side())

    ffn_all, ffn_all_side = gather_dp(r.whole_f, ffn_part, v_base)
    strip_all, strip_all_side = gather_dp(r.whole_t, strip_part, v_base + 2)
    ended += [ffn_all, strip_all, ffn_all_side, strip_all_side]
    mine = ffn_finish()
    squares = total_of(mine * mine)
    r.whole_f[at(order, ffn_part), :] = lowered(mine)
    ffn_all.start()
    tell_small.wait_recv()
    r.small[1, 0] = (r.small[0, 0] + r.small[0, 1]) + (r.small[0, 2] + r.small[0, 3])
    h_base = wire.take(2)

    def share(row, k, number):
        return wire.make(r.small.at[row, 0], r.small_dp.at[row // 4, d], number, here.ahead(k))

    def all_shares(row, number):
        others = r.small_dp.at[row // 4, pl.ds(0, n_dp - 1)]
        return wire.make(others, others, number, here.side())

    each(1, n_dp, lambda k: share(1, k, h_base).start())
    r.small_dp[0, d] = r.small[1, 0]

    out_far.wait_recv()
    out_relay.start()

    strip_line()

    in_near.wait_recv()
    in_relay.wait_recv()
    out_near.wait_recv()
    out_relay.wait_recv()

    g_base = wire.take(1)

    def outgoing(k):
        return pl.ds(pl.multiple_of(8 * span + k * cap, cap), cap)

    def ship(k):
        return wire.make(
            r.found.at[outgoing(k)], r.incoming.at[at(k, cap)], g_base, here.ahead(k)
        )

    def all_rows():
        rows = pl.ds(8 * span + cap, (n_dp - 1) * cap)
        landed = r.incoming.at[pl.ds(cap, (n_dp - 1) * cap)]
        return wire.make(r.found.at[rows], landed, g_base, here.side())

    places = pl.ds(8 * span, filled)
    if kept(n_dp):
        r.found[places, :] = lowered(dot(r.pick_s[...], r.found[0 : 8 * span, :]))
    else:
        marks_to = build_marks()

        def choose(k):
            chosen = picks(marks_to, k)
            r.found[outgoing(k), :] = lowered(dot(chosen, r.found[0 : 8 * span, :]))

        loop(0, n_dp, choose)
    ship(n_z).start()
    r.incoming[0:cap, :] = r.found[outgoing(0), :]

    mine = strip_finish()
    squares = squares + total_of(mine * mine)
    r.whole_t[at(order, strip_part), :] = lowered(mine)
    strip_all.start()
    each(1, n_z, lambda k: ship(k).start())
    each(n_z + 1, n_dp, lambda k: ship(k).start())

    several = min(n_dp, 8)

    def own_marks(g):
        for k in range(several):
            r.owned[:, k * 128 : (k + 1) * 128] = lowered(
                one_hot_columns(raised(r.asked[g * several + k]), rows_dev)
            )

    if n_dp == several:
        own_marks(0)

    ffn_all.wait_recv()
    ffn_all_side.start()

    strip_all.wait_recv()
    strip_all_side.start()
    for copy in ended:
        copy.wait_send()
    ended.clear()

    def end_line(k):
        cand_line(k).wait_send()

    each(1, n_z, end_line)

    ffn_end()
    strip_end()

    strip_all_side.wait_recv()
    c_base = wire.take(6)

    def spread_strips(first, rows, base):
        part = pl.ds(first, rows)
        mine_at, far_at = r.strips.at[f, part], r.strips.at[far, part]
        copies = (
            wire.make(mine_at, mine_at, base, here.ffn(2)),
            wire.make(mine_at, mine_at, base + 1, here.ffn(1)),
            wire.make(far_at, far_at, base + 2, here.ffn(1)),
        )
        ended.extend(copies)
        return copies

    r.strips[f, 2 * strip :, :] = r.whole_t[0:late_rows, :]
    strip_far, strip_near, strip_relay = spread_strips(2 * strip, late_rows, c_base + 3)
    strip_far.start()
    strip_near.start()
    ffn_all_side.wait_recv()
    outs = [
        pltpu.make_async_copy(src, dst, r.load_sems.at[i])
        for i, (src, dst) in enumerate(
            (
                (r.whole_f.at[pl.ds(0, 2 * width)], r.ffn_out),
                (r.table_grad, r.table_out),
            )
        )
    ]

    def strip_out(s):
        place = here.member[s]
        return pltpu.make_async_copy(
            r.strips.at[place], r.strips_out.at[place], r.load_sems.at[2 + s]
        )

    outs[0].start()
    r.strips[f, 0 : 2 * strip, :] = r.whole_f[2 * width : early_rows, :]
    early_far, early_near, early_relay = spread_strips(0, 2 * strip, c_base)
    early_far.start()
    early_near.start()

    all_rows().wait_recv()

    if n_dp == several:
        for first in range(0, rows_dev, 208):
            rows = slice(first, min(first + 208, rows_dev))
            value = dot(r.owned[rows, :], r.incoming[...])
            r.table_grad[rows, :] = value
            squares = squares + total_of(value * value)
    else:
        r.table_grad[...] = jnp.zeros((rows_dev, width), FULL)
        r.padded_in[...] = jnp.zeros_like(r.padded_in)

        def add_rows(g):
            own_marks(g)
            for k in range(several):
                r.padded_in[k * 128 : k * 128 + cap, :] = r.incoming[
                    at(g * several + k, cap), :
                ]
            r.table_grad[...] = r.table_grad[...] + dot(r.owned[...], r.padded_in[...])

        loop(0, n_dp // several, add_rows)
        table_grad = r.table_grad[...]
        squares = squares + total_of(table_grad * table_grad)
    outs[1].start()

    r.small[3, 0] = jnp.broadcast_to(squares, (8, width))
    tell_norm = to_members(r.small.at[3], wire.take(1))
    tell_norm.start()
    ended.append(tell_norm)
    all_shares(1, h_base).wait_recv()
    tell_norm.wait_recv()
    r.small[4, 0] = (r.small[3, 0] + r.small[3, 1]) + (r.small[3, 2] + r.small[3, 3])

    each(1, n_dp, lambda k: share(4, k, h_base + 1).start())
    r.small_dp[1, d] = r.small[4, 0]
    early_far.wait_recv()
    early_relay.start()
    early_near.wait_recv()
    strip_near.wait_recv()
    strip_out(0).start()
    strip_out(1).start()
    strip_far.wait_recv()
    strip_relay.start()
    strip_out(2).start()
    all_shares(4, h_base + 1).wait_recv()
    totals, squares = r.small_dp[0, 0], r.small_dp[1, 0]
    for k in range(1, n_dp):
        totals = totals + r.small_dp[0, k]
        squares = squares + r.small_dp[1, k]
    gains = jnp.where(row8 < 3, totals, 0.0)
    norm = jnp.sqrt(squares + total_of(gains * gains))
    r.sums[...] = jnp.where(row8 == 4, norm, totals)

    all_rows().wait_send()
    all_shares(1, h_base).wait_send()
    all_shares(4, h_base + 1).wait_send()


    early_relay.wait_recv()
    strip_relay.wait_recv()
    strip_out(3).start()
    for copy in outs + [strip_out(s) for s in range(4)]:
        copy.wait()
    for copy in ended:
        copy.wait_send()
    assert wire.arrived <= r.recv_sems.shape[0]
    assert wire.most <= r.send_sems.shape[0]


def step(n_dp, cap, owner, row, lengths, count, table, wq, wo, w_in, w_back, gains, positions):
    rows_dev, width = table.shape
    span = owner.shape[1] // 4
    heads, n_z = width // HD, n_dp // 2
    shapes = plan(n_dp, cap, rows_dev, span, width, heads)
    names = INPUTS + OUTPUTS + list(shapes) + ["load_sems", "send_sems", "recv_sems"]
    vmem = pl.BlockSpec(memory_space=pltpu.VMEM)
    smem = pl.BlockSpec(memory_space=pltpu.SMEM)
    rest = pl.BlockSpec(memory_space=pl.ANY)
    sends, arrivals = 9 * n_z + 23, 20 * n_z + 48

    def out(kind, *shape):
        return jax.ShapeDtypeStruct(shape, kind)

    return pl.pallas_call(
        functools.partial(step_kernel, n_dp, cap, names),
        out_shape=(
            out(FULL, rows_dev, width),
            out(LOW, 2 * width, width),
            out(LOW, 4, 6 * span // 4, width),
            out(FULL, 8, width),
        ),
        in_specs=[vmem, vmem, smem, vmem, rest, rest, rest, rest, rest, vmem, rest],
        out_specs=(rest, rest, rest, vmem),
        scratch_shapes=[pltpu.VMEM(shape[:-1], shape[-1]) for shape in shapes.values()]
        + [
            pltpu.SemaphoreType.DMA((6,)),
            pltpu.SemaphoreType.DMA((sends,)),
            pltpu.SemaphoreType.DMA((arrivals,)),
        ],
        compiler_params=pltpu.CompilerParams(
            collective_id=0,
            has_side_effects=True,
            vmem_limit_bytes=63 * MIB,
        ),
        name="step",
    )(owner, row, lengths, count, table, wq, wo, w_in, w_back, gains, positions)


STATES = 21
GAINS = 5


def jobs(rows_dev, width):
    quarter = -(-rows_dev // 32) * 8
    result = []
    for first in range(0, rows_dev, quarter):
        result.append((0, first, min(quarter, rows_dev - first)))
    return result + [(3, 0, width), (4, 0, width), (1, 0, width), (6, 0, 2 * width), (2, 0, width)]


def update_kernel(rows_dev, table_grad, ffn_grad, strips, sums, *refs):
    ins, refs = refs[:STATES], refs[STATES:]
    loss_out, rms_out, norm_out = refs[:3]
    outs, refs = refs[3 : 3 + STATES], refs[3 + STATES :]
    held, made, refs = refs[:18], refs[18:36], refs[36:]
    table_s, ffn_s, strips_s, grad_sems, in_sems, out_sems = refs
    width = sums.shape[1]
    work = jobs(rows_dev, width)

    def kept_at(which, i):
        return 3 * (which if which < GAINS else which - 1) + i

    def moves(number):
        which, first, rows = work[number]
        part = pl.ds(first, rows)
        here = [kept_at(which, i) for i in range(3)]
        return (
            [
                pltpu.make_async_copy(
                    ins[3 * which + i].at[part],
                    held[here[i]].at[part],
                    in_sems.at[number, i],
                )
                for i in range(3)
            ],
            [
                pltpu.make_async_copy(
                    made[here[i]].at[part],
                    outs[3 * which + i].at[part],
                    out_sems.at[number, i],
                )
                for i in range(3)
            ],
        )

    grads = [
        pltpu.make_async_copy(table_grad, table_s, grad_sems.at[0]),
        pltpu.make_async_copy(ffn_grad, ffn_s, grad_sems.at[1]),
        pltpu.make_async_copy(strips, strips_s, grad_sems.at[2]),
    ]
    grads[0].start()
    for number in range(len(work)):
        for i, copy in enumerate(moves(number)[0]):
            copy.start(priority=(number + i) % 2)
        if number == 1:
            grads[1].start()
            grads[2].start()
    norm = sums[4:5, 0:1]
    factor = CLIP / jnp.maximum(norm, CLIP)
    corr_one = 1.0 - BETA_ONE**STEP
    corr_two = 1.0 - BETA_TWO**STEP

    def adam(which, rows, lanes, grad, rate):
        if which == GAINS:
            source, target = ins[3 * which : 3 * which + 3], outs[3 * which : 3 * which + 3]
        else:
            first = kept_at(which, 0)
            source, target = held[first : first + 3], made[first : first + 3]
        weight, moment, second = (ref[rows, lanes] for ref in source)
        clipped = raised(grad) * factor
        moment = BETA_ONE * moment + (1.0 - BETA_ONE) * clipped
        second = BETA_TWO * second + (1.0 - BETA_TWO) * clipped * clipped
        target[0][rows, lanes] = weight - rate * (
            moment / corr_one / (jnp.sqrt(second / corr_two) + ADAM_EPS) + DECAY * weight
        )
        target[1][rows, lanes] = moment
        target[2][rows, lanes] = second

    every = slice(None)
    strip = strips_s.shape[1] // 6
    waited = set()

    def need(i):
        if i not in waited:
            waited.add(i)
            grads[i].wait()

    for number, (which, first, rows) in enumerate(work):
        copies_in, copies_out = moves(number)
        need(0 if which == 0 else 1 if which in (3, 4) else 2)
        for copy in copies_in:
            copy.wait()
        if which == 0:
            part = slice(first, first + rows)
            adam(0, part, every, table_s[part, :], LEARN)
        elif which in (3, 4):
            start = (which - 3) * width
            adam(which, every, every, ffn_s[start : start + width, :], LEARN)
        for m in range(4):
            at_rows = slice(m * strip, (m + 1) * strip)
            if which == 1:
                for j, i in enumerate((2, 3, 1)):
                    lanes = slice(j * width, (j + 1) * width)
                    grad = strips_s[m, i * strip : (i + 1) * strip, :]
                    adam(1, at_rows, lanes, grad, LEARN)
            elif which == 2:
                adam(2, at_rows, every, strips_s[m, 0:strip, :], LEARN)
            elif which == 6:
                for u in range(2):
                    at_rows = slice((4 * u + m) * strip, (4 * u + m + 1) * strip)
                    grad = strips_s[m, (4 + u) * strip : (5 + u) * strip, :]
                    adam(6, at_rows, every, grad, LEARN)
        for copy in copies_out:
            copy.start()
    adam(GAINS, every, every, sums[0:3, :], GAIN_LEARN)
    stats = sums[3:4, :]
    roots = jnp.sqrt(stats / (stats[:, 1:2] * float(width)))

    def one(row, i):
        return jnp.sum(jnp.where(iota(row.shape, 1) == i, row, 0.0))

    loss_out[0] = one(stats, 0)
    loss_out[1] = one(stats, 1)
    for i in range(3):
        rms_out[i] = one(roots, 2 + i)
    norm_out[0] = one(sums[4:5, :], 0)
    for number in range(len(work)):
        for copy in moves(number)[1]:
            copy.wait()


def update(table_grad, ffn_grad, strips, sums, states):
    vmem = pl.BlockSpec(memory_space=pltpu.VMEM)
    smem = pl.BlockSpec(memory_space=pltpu.SMEM)
    rest = pl.BlockSpec(memory_space=pl.ANY)
    places = [vmem if i // 3 == GAINS else rest for i in range(STATES)]
    room = [pltpu.VMEM(a.shape, FULL) for i, a in enumerate(states) if i // 3 != GAINS]
    rows_dev, width = table_grad.shape
    number = len(jobs(rows_dev, width))
    return pl.pallas_call(
        functools.partial(update_kernel, rows_dev),
        out_shape=tuple(jax.ShapeDtypeStruct((n,), FULL) for n in (2, 3, 1))
        + tuple(jax.ShapeDtypeStruct(a.shape, FULL) for a in states),
        in_specs=[rest] * 3 + [vmem] + places,
        out_specs=[smem] * 3 + places,
        scratch_shapes=room
        + room
        + [pltpu.VMEM(a.shape, a.dtype) for a in (table_grad, ffn_grad, strips)]
        + [
            pltpu.SemaphoreType.DMA((3,)),
            pltpu.SemaphoreType.DMA((number, 3)),
            pltpu.SemaphoreType.DMA((number, 3)),
        ],
        compiler_params=pltpu.CompilerParams(vmem_limit_bytes=63 * MIB),
        name="update",
    )(table_grad, ffn_grad, strips, sums, *states)


def shards(
    item_owner,
    item_row,
    lengths,
    log_count,
    item_table,
    table_mom,
    table_sec,
    qkv_weight,
    qkv_mom,
    qkv_sec,
    out_weight,
    out_mom,
    out_sec,
    ffn_in,
    ffn_in_mom,
    ffn_in_sec,
    ffn_back,
    ffn_back_mom,
    ffn_back_sec,
    norm_gains,
    gains_mom,
    gains_sec,
    positions,
    positions_mom,
    positions_sec,
):
    n_dp = lax.axis_size("dp")
    tokens = item_owner.shape[0]
    cap = max(2, 4 * tokens // (n_dp * lax.axis_size("ffn")))
    table_grad, ffn_grad, strips, sums = step(
        n_dp,
        cap,
        item_owner.T,
        item_row.T,
        lengths,
        log_count,
        item_table,
        qkv_weight,
        out_weight,
        ffn_in,
        ffn_back,
        norm_gains,
        positions,
    )
    return update(
        table_grad,
        ffn_grad,
        strips,
        sums,
        (
            item_table,
            table_mom,
            table_sec,
            qkv_weight,
            qkv_mom,
            qkv_sec,
            out_weight,
            out_mom,
            out_sec,
            ffn_in,
            ffn_in_mom,
            ffn_in_sec,
            ffn_back,
            ffn_back_mom,
            ffn_back_sec,
            norm_gains,
            gains_mom,
            gains_sec,
            positions,
            positions_mom,
            positions_sec,
        ),
    )


def solution(mesh):
    whole, rows, table = P(), P("dp", None), P(("dp", "ffn"), None)
    wide, tall = P(None, "ffn"), P("ffn", None)
    states = (table,) * 3 + (whole,) * 6 + (wide,) * 3 + (tall,) * 3 + (whole,) * 6
    return jax.shard_map(
        shards,
        mesh=mesh,
        in_specs=(rows, rows, P("dp"), P(("dp", "ffn"))) + states,
        out_specs=(whole,) * 3 + states,
        check_vma=False,
    )
```

```python
import functools
import math
import types

import jax
import jax.numpy as jnp
from jax import lax
from jax.experimental import pallas as pl
from jax.experimental.pallas import tpu as pltpu
from jax.sharding import PartitionSpec as P

MESH = pl.DeviceIdType.MESH
MIB = 1024 * 1024
LOW, FULL = jnp.bfloat16, jnp.float32

EPS = 1e-06
NEG = -1e30
HD = 32
ROOT = math.sqrt(2.0 / math.pi)
LEARN = 0.05
GAIN_LEARN = 0.4
STEP = 5
BETA_ONE = 0.5
BETA_TWO = 0.5
DECAY = 0.01
ADAM_EPS = 1e-08
CLIP = 0.05


def lowered(value):
    return value.astype(LOW)


def raised(value):
    return value.astype(FULL)


def dot(left, right):
    return jnp.dot(left, right, preferred_element_type=FULL)


def against(left, right):
    return lax.dot_general(left, right, (((1,), (1,)), ((), ())), preferred_element_type=FULL)


def across(left, right):
    return lax.dot_general(left, right, (((0,), (0,)), ((), ())), preferred_element_type=FULL)


def iota(shape, dim):
    return lax.broadcasted_iota(jnp.int32, shape, dim)


def loop(first, last, body):
    def step(k, unused):
        body(k)
        return unused

    if last - first == 1:
        body(first)
    elif last > first:
        lax.fori_loop(first, last, step, 0)


def each(first, last, body):
    if last - first <= 8:
        for k in range(first, last):
            body(k)
    else:
        loop(first, last, body)


def at(index, size):
    if isinstance(index, int):
        return pl.ds(index * size, size)
    return pl.ds(pl.multiple_of(index * size, size), size)


def spread(row, lanes):
    return jnp.broadcast_to(row, (lanes, row.shape[1])).T


def turned(block):
    return lowered(raised(block).T)


def total_of(value):
    return jnp.sum(value, keepdims=True)


def one_hot_rows(row, width):
    high = jnp.floor(row * (1.0 / 128.0))
    low = spread(row - high * 128.0, 128)
    base = lowered(jnp.where(low == raised(iota(low.shape, 1)), 1.0, 0.0))
    high = lowered(spread(high, 128))
    zero = jnp.zeros_like(base)
    return jnp.concatenate(
        [jnp.where(high == jnp.asarray(b, LOW), base, zero) for b in range(width // 128)], 1
    )


def one_hot_columns(row, height):
    return jnp.where(raised(iota((height, row.shape[1]), 0)) == row, 1.0, 0.0)


def factor_of(hidden):
    return lax.rsqrt(jnp.mean(hidden * hidden, -1, keepdims=True) + EPS)


def rms_back(hidden, gain, upstream):
    factor = factor_of(hidden)
    scaled = upstream * gain
    inner = jnp.mean(scaled * hidden, -1, keepdims=True)
    grad_hidden = factor * scaled - hidden * (factor * factor * factor * inner)
    return grad_hidden, jnp.sum(upstream * hidden * factor, 0, keepdims=True)


class Peers:
    def __init__(self, n_dp):
        self.n_dp, self.n_z = n_dp, n_dp // 2
        self.d, self.f = lax.axis_index("dp"), lax.axis_index("ffn")
        self.z, self.y = self.d // 2, lax.rem(self.d, 2)
        near = self.f + 1 - 2 * lax.rem(self.f, 2)
        far = lax.rem(self.f + 2, 4)
        self.member = (self.f, near, far, 3 - self.f)

    def ffn(self, s):
        return (self.d, self.member[s])

    def ahead(self, i):
        return self.apart(i // self.n_z, i % self.n_z)

    def behind(self, i):
        return self.apart(i // self.n_z, self.n_z - i % self.n_z)

    def apart(self, ky, kz):
        z = lax.rem(self.z + kz, self.n_z)
        return (z * 2 + self.y + ky - 2 * self.y * ky, self.f)

    def side(self):
        return (self.d + 1 - 2 * self.y, self.f)

    def up(self, k):
        return (lax.rem(self.z + k, self.n_z) * 2 + self.y, self.f)

    def down(self, k):
        return (lax.rem(self.z + self.n_z - k, self.n_z) * 2 + self.y, self.f)

    def greet(self):
        barrier = pltpu.get_barrier_semaphore()

        def hello(where):
            pl.semaphore_signal(barrier, inc=1, device_id=where, device_id_type=MESH)

        for s in (1, 2, 3):
            hello(self.ffn(s))
        each(1, self.n_dp, lambda k: hello(self.ahead(k)))

    def met(self):
        pl.semaphore_wait(pltpu.get_barrier_semaphore(), self.n_dp + 2)


class Number:
    def __init__(self, leave, arrive, shared=False):
        self.leave, self.arrive, self.shared = leave, arrive, shared

    def __add__(self, k):
        return Number(self.leave if self.shared else self.leave + k, self.arrive + k, self.shared)


class Wire:
    def __init__(self, send, recv):
        self.send, self.recv = send, recv
        self.left, self.arrived, self.most = 0, 0, 0

    def take(self, number, arrivals=None, shared=False):
        result = Number(self.left, self.arrived, shared)
        self.left += 1 if shared else number
        self.arrived += number if arrivals is None else arrivals
        self.most = max(self.most, self.left)
        return result

    def renew(self):
        self.left = 0

    def make(self, src, dst, number, where, landing=None):
        return pltpu.make_async_remote_copy(
            src_ref=src,
            dst_ref=dst,
            send_sem=self.send.at[number.leave],
            recv_sem=self.recv.at[(landing or number).arrive],
            device_id=where,
            device_id_type=MESH,
        )


class Joined:
    def __init__(self, copies, all_of_them):
        self.copies, self.all = copies, all_of_them

    def start(self):
        for copy in self.copies:
            copy.start()

    def wait_recv(self):
        self.all.wait_recv()

    def wait_send(self):
        self.all.wait_send()


class Group:
    def __init__(self, *copies):
        self.copies = copies

    def start(self):
        for copy in self.copies:
            copy.start()

    def wait_recv(self):
        for copy in self.copies:
            copy.wait_recv()

    def wait_send(self):
        for copy in self.copies:
            copy.wait_send()


INPUTS = [
    "owner",
    "row",
    "lengths",
    "count",
    "table",
    "wq",
    "wo",
    "w_in",
    "w_back",
    "gains",
    "positions",
]
OUTPUTS = ["table_out", "ffn_out", "strips_out", "sums"]


def plan(n_dp, cap, rows_dev, span, width, heads):
    n_z = n_dp // 2
    filled = n_dp * cap
    padded = -(-rows_dev // 128) * 128
    square = (span, width)
    ffn_part, strip_part = parts(n_dp, span, width)
    return {
        "table_s": (rows_dev, width, FULL),
        "wq_s": (width, 3 * width, FULL),
        "wo_s": (width, width, FULL),
        "positions_s": (2 * span, width, FULL),
        "w_s": (2, width, width, FULL),
        "weights": (4, 2, width, width, LOW),
        "hot": (32 * n_dp, span, LOW),
        "slot_s": (8, span, FULL),
        "kind_s": (8, span, FULL),
        "table_low": (padded, width, LOW),
        "req": (n_dp, 1, 128, jnp.int32),
        "asked": (n_dp, 1, 128, jnp.int32),
        "send_rows": (n_dp, cap, width, LOW),
        "send_bias": (n_dp, 1, 128, FULL),
        "found": (4 * filled, width, LOW),
        "found_bias": (4 * n_dp, 1, 128, FULL),
        "bias_s": (8, span, FULL),
        "cands": (n_dp * span, width, LOW),
        "cand_bias": (n_dp, 8, span, FULL),
        "cand_t": (width, (n_dp if kept(n_dp) else 1) * span, LOW),
        "cand_col": ((n_dp if kept(n_dp) else 1) * span, 128, FULL),
        "logit_s": (6 * span if kept(n_dp) else 2 * span, span, FULL),
        "stat_s": (4, 8, span, FULL),
        "scale_s": (8, 4 * span, FULL),
        "expo_s": (n_dp * span if kept(n_dp) else 16, 4 * span, LOW),
        "wq16": (width, 3 * width, LOW),
        "wo16": (width, width, LOW),
        "h0_s": square + (FULL,),
        "n1_s": square + (LOW,),
        "q_s": square + (LOW,),
        "qt_s": (width, span, LOW),
        "k_s": (2 * span, width, LOW),
        "v_s": (2 * span, width, LOW),
        "kt_s": (width, 2 * span, LOW),
        "vt_s": (width, 2 * span, LOW),
        "mask_s": (2 * span, span, FULL),
        "p_s": (heads, 2 * span, span, FULL),
        "p16_s": (2 * span, heads * span, LOW),
        "stack_s": (heads * span, width, LOW),
        "mixt_s": (width, span, LOW),
        "h1_s": square + (FULL,),
        "h2_s": square + (FULL,),
        "n2t_s": (width, span, LOW),
        "pre_s": (4 * span, width, FULL),
        "act_s": (span, 4 * span, LOW),
        "fin_s": (4 * span, width, LOW),
        "fint_s": (width, 4 * span, LOW),
        "acc_s": (width, 4 * span, FULL),
        "acc_send": (3, width, span, LOW),
        "acc_got": (3, width, span, LOW),
        "mid_send": (3, 8, span, FULL),
        "mid_got": (3, 8, span, FULL),
        "tot_s": (4, 8, span, FULL),
        "cand_send": (n_z, span, width, LOW),
        "side_got": (n_z, span, width, LOW),
        "line_got": (n_z, span, width, LOW),
        "own_s": square + (FULL,),
        "dq_s": (width, span, FULL),
        "kv_s": (2 * span, width, FULL),
        "kv_got": (2 * span, width, FULL),
        "gf_s": (4, 2, width, width, FULL),
        "fnear_send": (2, 2 * width, width, LOW),
        "fnear_got": (2, 2 * width, width, LOW),
        "ffar_send": (2 * width, width, LOW),
        "ffar_got": (2 * width, width, LOW),
        "enear_send": (2, span // 2, width, LOW),
        "enear_got": (2, span // 2, width, LOW),
        "efar_send": (span // 2, width, LOW),
        "efar_got": (span // 2, width, LOW),
        "snear_send": (2, span, width, LOW),
        "snear_got": (2, span, width, LOW),
        "sfar_send": (span, width, LOW),
        "sfar_got": (span, width, LOW),
        "gv_s": square + (LOW,),
        "strip_s": (n_dp * strip_part, width, FULL),
        "fside_send": (n_z * ffn_part, width, LOW),
        "fside_got": (n_z * ffn_part, width, LOW),
        "fline_send": (n_z, ffn_part, width, LOW),
        "fline_got": (n_z, ffn_part, width, LOW),
        "sside_send": (n_z * strip_part, width, LOW),
        "sside_got": (n_z * strip_part, width, LOW),
        "sline_send": (n_z, strip_part, width, LOW),
        "sline_got": (n_z, strip_part, width, LOW),
        "whole_f": (n_dp * ffn_part, width, LOW),
        "whole_t": (n_dp * strip_part, width, LOW),
        "incoming": (filled, width, LOW),
        "place_s": (3 * span if kept(n_dp) else 16, 4 * filled if kept(n_dp) else 128, LOW),
        "placing_s": (3 * span if kept(n_dp) else 16, width, FULL),
        "placed_s": (3 * span if kept(n_dp) else 16, width, LOW),
        "pick_s": (filled if kept(n_dp) else 16, 8 * span, LOW),
        "padded_in": (8 * 128 if cap < 128 else 16, width, LOW),
        "owned": (rows_dev, min(n_dp, 8) * 128, LOW),
        "table_grad": (rows_dev, width, FULL),
        "strips": (4, 6 * span // 4, width, LOW),
        "small": (5, 4, 8, width, FULL),
        "small_dp": (2, n_dp, 8, width, FULL),
    }


def kept(n_dp):
    return n_dp <= 8


def parts(n_dp, span, width):
    return (
        -(-(2 * width + span // 2) // (16 * n_dp)) * 16,
        -(-span // (16 * n_dp)) * 16,
    )


def step_kernel(n_dp, cap, names, *refs):
    r = types.SimpleNamespace(**dict(zip(names, refs)))
    here = Peers(n_dp)
    wire = Wire(r.send_sems, r.recv_sems)
    d, f, n_z = here.d, here.f, here.n_z
    me, near, far, cross = here.member
    span, width = r.h0_s.shape
    heads = width // HD
    scale = HD ** (-0.5)
    half = lax.rem(f, 2)
    begin = half * span
    filled = n_dp * cap
    kinds = 4 * n_dp
    rows_dev = r.table_s.shape[0]
    padded = r.table_low.shape[0]
    ended = []

    here.greet()
    loads = [
        pltpu.make_async_copy(src, dst, r.load_sems.at[i])
        for i, (src, dst) in enumerate(
            (
                (r.table, r.table_s),
                (r.wq, r.wq_s),
                (r.wo, r.wo_s),
                (r.positions, r.positions_s),
                (r.w_in, r.w_s.at[0]),
                (r.w_back, r.w_s.at[1]),
            )
        )
    ]
    for i in (4, 5, 0, 1, 2, 3):
        loads[i].start()

    place = iota((kinds, span), 0)
    slot_of = jnp.zeros((kinds, span), jnp.int32)
    for s in (1, 2, 3):
        slot_of = slot_of + (place >= s * n_dp).astype(jnp.int32)
    steps = place - slot_of * n_dp
    other_y = (steps >= n_z).astype(jnp.int32)
    steps = steps - other_y * n_z + here.z
    steps = jnp.where(steps >= n_z, steps - n_z, steps)
    ahead = steps * 2 + here.y + other_y * (1 - 2 * here.y)
    named = ahead * 4 + jnp.where(
        slot_of == 0, me, jnp.where(slot_of == 1, near, jnp.where(slot_of == 2, far, cross))
    )

    def chunk_of(ref, c):
        return ref[c // 4 : c // 4 + 1, (c % 4) * span : (c % 4 + 1) * span]

    for c in range(8):
        r.hot[c * kinds : (c + 1) * kinds, :] = lowered(
            jnp.where(chunk_of(r.owner, c) == named, 1.0, 0.0)
        )
    before = lowered(jnp.where(iota((span, span), 0) < iota((span, span), 1), 1.0, 0.0))
    carry = jnp.zeros((kinds, 1), FULL)
    place_f = raised(place)
    asking = jnp.zeros((2 * n_dp, 128), FULL)
    for c in range(8):
        ones = raised(r.hot[c * kinds : (c + 1) * kinds, :])
        ranks = dot(r.hot[c * kinds : (c + 1) * kinds, :], before)
        slot = jnp.sum(ones * (ranks + carry), 0, keepdims=True)
        carry = carry + jnp.sum(ones, 1, keepdims=True)
        r.slot_s[c : c + 1, :] = slot
        r.kind_s[c : c + 1, :] = jnp.sum(ones * place_f, 0, keepdims=True)
        row = chunk_of(r.row, c)
        mine = ones[:n_dp]
        sought = jnp.concatenate([mine * raised(row >> 5), mine * raised(row & 31)], 0)
        asking = asking + against(lowered(sought), lowered(one_hot_columns(slot, 128)))
    wanted = (asking[:n_dp] * 32.0 + asking[n_dp:]).astype(jnp.int32)
    for k in range(n_dp):
        r.req[k, 0:1, :] = wanted[k : k + 1, :]
    r.asked[0] = r.req[0]
    q_base = wire.take(n_dp, shared=True)

    def ask(k):
        return wire.make(r.req.at[k], r.asked.at[k], q_base + k, here.ahead(k))

    here.met()
    each(1, n_dp, lambda k: ask(k).start())

    loads[4].wait()
    loads[5].wait()
    r.weights[0] = lowered(r.w_s[...])
    w_base = wire.take(3)
    w_near = wire.make(r.weights.at[0], r.weights.at[1], w_base, here.ffn(1))
    w_far = wire.make(r.weights.at[0], r.weights.at[2], w_base + 1, here.ffn(2))
    w_relay = wire.make(r.weights.at[2], r.weights.at[3], w_base + 2, here.ffn(1))
    w_far.start()
    w_near.start()

    def build_marks():
        for s in range(4):
            for column in range(2):
                chunk_row = pl.ds(column * 4 + here.member[s], 1)
                r.p16_s[0:cap, (2 * s + column) * span : (2 * s + column + 1) * span] = lowered(
                    one_hot_columns(r.slot_s[chunk_row, :], cap)
                )
        where_to = jnp.concatenate(
            [
                r.kind_s[pl.ds(column * 4 + here.member[s], 1), :]
                for s in range(4)
                for column in range(2)
            ],
            1,
        )
        where_to = lowered(jnp.broadcast_to(where_to, (16, 8 * span)))
        return where_to

    zero16 = jnp.zeros((16, 8 * span), LOW)

    def picks(where_to, k):
        wanted = where_to == lowered(jnp.full((16, 8 * span), k, FULL))
        return jnp.concatenate(
            [
                jnp.where(wanted, r.p16_s[i * 16 : (i + 1) * 16, :], zero16)
                for i in range(cap // 16)
            ],
            0,
        )

    def key_of(column, quarter):
        chunk = pl.ds(column * 4 + quarter, 1)
        return r.kind_s[chunk, :] * float(cap) + r.slot_s[chunk, :]

    if kept(n_dp):
        marks_to = build_marks()

        def keep_picks(k):
            r.pick_s[at(k, cap), :] = picks(marks_to, k)

        loop(0, n_dp, keep_picks)
        for i, (column, quarter) in enumerate(((1, f), (0, f), (0, near))):
            r.place_s[at(i, span), :] = one_hot_rows(key_of(column, quarter), 4 * filled)

    loads[0].wait()
    r.table_low[0:rows_dev, :] = lowered(r.table_s[...])
    if padded > rows_dev:
        r.table_low[rows_dev:padded, :] = jnp.zeros((padded - rows_dev, width), LOW)
    counts = lowered(jnp.broadcast_to(raised(r.count[...].reshape(1, rows_dev)), (8, rows_dev)))
    if padded > rows_dev:
        counts = jnp.concatenate([counts, jnp.zeros((8, padded - rows_dev), LOW)], 1)
    r_base, b_base = wire.take(n_dp, shared=True), wire.take(1)
    others = pl.ds(1, n_dp - 1)

    def reply(k):
        return wire.make(r.send_rows.at[k], r.found.at[at(k, cap)], r_base + k, here.behind(k))

    def reply_bias(k):
        return wire.make(r.send_bias.at[k], r.found_bias.at[k], b_base, here.behind(k))

    def all_replies():
        rest = r.found.at[pl.ds(cap, filled - cap)]
        return wire.make(r.send_rows.at[others], rest, r_base, here.side())

    def all_biases():
        return wire.make(r.send_bias.at[others], r.found_bias.at[others], b_base, here.side())

    def fetch(k):
        chosen = one_hot_rows(raised(r.asked[k]), padded)
        return lowered(dot(chosen, r.table_low[...]))[:cap], against(counts, chosen)[0:1, :]

    def serve(k):
        ask(k).wait_recv()
        rows, bias = fetch(k)
        r.send_rows[k] = rows
        r.send_bias[k] = bias
        reply(k).start()
        reply_bias(k).start()

    loop(1, n_dp, serve)
    rows, bias = fetch(0)
    r.found[0:cap, :] = rows
    r.found_bias[0] = bias
    cuts = [(k, 1) for k in range(n_dp)]
    passes = [wire.take(len(cuts), shared=True) for i in range(3)]
    bias_passes = [wire.take(1) for i in range(3)]

    def pass_on(i, source, target, number, who):
        sem = bias_passes[number] if i == len(cuts) else passes[number] + i
        if i == len(cuts):
            src, dst = (r.found_bias.at[at(slot, n_dp)] for slot in (source, target))
        else:
            first, several = cuts[i]
            src, dst = (
                r.found.at[pl.ds((slot * n_dp + first) * cap, several * cap)]
                for slot in (source, target)
            )
        return wire.make(src, dst, sem, here.ffn(who))

    def all_passes(source, number):
        rows = r.found.at[at(source, filled)]
        return wire.make(rows, rows, passes[number], here.side())

    def to_far(i):
        return pass_on(i, 0, 2, 0, 2)

    def to_near(i):
        return pass_on(i, 0, 1, 1, 1)

    def relay(i):
        return pass_on(i, 2, 3, 2, 1)

    def take_on(i):
        first, several = cuts[i]
        for k in range(max(first, 1), first + several):
            reply(k).wait_recv()
        to_far(i).start()
        to_near(i).start()

    def relay_on(i):
        to_far(i).wait_recv()
        relay(i).start()

    for i in range(len(cuts)):
        take_on(i)
        if i > 1:
            relay_on(i - 2)
    all_biases().wait_recv()
    to_far(len(cuts)).start()
    to_near(len(cuts)).start()
    w_far.wait_recv()
    w_relay.start()
    relay_on(len(cuts) - 2)
    for i in range(len(cuts)):
        to_near(i).wait_recv()
    if kept(n_dp):
        r.placing_s[...] = dot(r.place_s[:, : 2 * filled], r.found[0 : 2 * filled, :])
    relay_on(len(cuts) - 1)
    relay_on(len(cuts))
    loads[1].wait()
    loads[2].wait()
    r.wq16[...] = lowered(r.wq_s[...])
    r.wo16[...] = lowered(r.wo_s[...])
    for i in range(len(cuts)):
        relay(i).wait_recv()

    if kept(n_dp):
        far_rows = dot(r.place_s[:, 2 * filled :], r.found[2 * filled :, :])
        r.placed_s[...] = lowered(r.placing_s[...] + far_rows)

    def chosen_rows(i):
        if kept(n_dp):
            return r.placed_s[at(i, span), :]
        column, quarter = ((1, f), (0, f), (0, near))[i]
        return lowered(dot(one_hot_rows(key_of(column, quarter), 4 * filled), r.found[...]))

    r.cands[0:span, :] = chosen_rows(0)
    to_near(len(cuts)).wait_recv()
    relay(len(cuts)).wait_recv()
    bias_rows = lowered(r.found_bias[:, 0, :].T)
    lane = iota((1, span), 1)
    length = r.lengths[f // 2]
    valid_lane = jnp.where(lane + begin < length, 1.0, 0.0)
    valid_col = jnp.where(iota((span, 1), 0) + begin < length, 1.0, 0.0)
    chunk = 4 + f
    marks = one_hot_columns(r.slot_s[pl.ds(chunk, 1), :], 128)
    bias = jnp.sum(dot(bias_rows, r.hot[at(chunk, kinds), :]) * marks, 0, keepdims=True)
    r.bias_s[...] = jnp.broadcast_to(bias, (8, span))
    r.cand_bias[0] = jnp.broadcast_to(jnp.where(lane + begin < length, -bias, NEG), (8, span))
    z_base, y_base = wire.take(0, 3 * n_z), wire.take(3 * n_z)
    u_base = wire.take(6 * n_z, 0)
    has_up, has_down = here.z + 1 < n_z, here.z > 0

    def slot(k, ky):
        if isinstance(k, int) and k == 0:
            return ky
        return 1 + k + ky * (n_z - 1)

    half_rows = span // 2

    def half_of(i, h):
        first = i * span + h * half_rows
        if not isinstance(first, int):
            first = pl.multiple_of(first, half_rows)
        return r.cands.at[pl.ds(first, half_rows)]

    def offer_line(source, target, number, where):
        i, j = slot(source, 0), slot(target, 0)
        first, second = (
            wire.make(
                half_of(i, h),
                half_of(j, h),
                number + 2 * n_z * h,
                where,
                z_base + (n_z * h + target),
            )
            for h in range(2)
        )
        bias = wire.make(
            r.cand_bias.at[i],
            r.cand_bias.at[j],
            number + 4 * n_z,
            where,
            z_base + (2 * n_z + target),
        )
        return first, Group(second, bias)

    def send_up(a):
        return offer_line(a, a + 1, u_base + a, here.up(1))

    def send_down(b):
        source = b if isinstance(b, int) and b == 0 else n_z - b
        return offer_line(source, n_z - 1 - b, u_base + (n_z + b), here.down(1))

    def offer_side(k):
        i, j = slot(k, 0), slot(k, 1)
        first, second = (
            wire.make(half_of(i, h), half_of(j, h), y_base + (n_z * h + k), here.side())
            for h in range(2)
        )
        bias = wire.make(
            r.cand_bias.at[i], r.cand_bias.at[j], y_base + (2 * n_z + k), here.side()
        )
        return first, Group(second, bias)

    for h in range(2):
        pl.when(has_up)(lambda: send_up(0)[h].start())
        pl.when(has_down)(lambda: send_down(0)[h].start())
    for h in range(2):
        offer_side(0)[h].start()

    def hand_on(j):
        @pl.when(here.z >= j)
        def from_below():
            for h in range(2):
                offer_line(0, j, u_base, here.up(1))[h].wait_recv()
                pl.when(has_up)(lambda: send_up(j)[h].start())
                offer_side(j)[h].start()

        @pl.when(here.z + j < n_z)
        def from_above():
            for h in range(2):
                offer_line(0, n_z - j, u_base, here.up(1))[h].wait_recv()
                pl.when(has_down)(lambda: send_down(j)[h].start())
                offer_side(n_z - j)[h].start()

    loads[3].wait()
    gain1, gain2, gain3 = r.gains[0:1, :], r.gains[1:2, :], r.gains[2:3, :]
    hidden0 = raised(chosen_rows(1)) + r.positions_s[at(half, span), :]
    r.h0_s[...] = hidden0
    normed1 = lowered(hidden0 * factor_of(hidden0) * gain1)
    r.n1_s[...] = normed1
    r.q_s[...] = lowered(dot(normed1, r.wq16[:, :width]))
    r.k_s[0:span, :] = lowered(dot(normed1, r.wq16[:, width : 2 * width]))
    r.v_s[0:span, :] = lowered(dot(normed1, r.wq16[:, 2 * width :]))
    hidden0 = raised(chosen_rows(2)) + r.positions_s[at(1 - half, span), :]
    normed1 = lowered(hidden0 * factor_of(hidden0) * gain1)
    r.k_s[span:, :] = lowered(dot(normed1, r.wq16[:, width : 2 * width]))
    r.v_s[span:, :] = lowered(dot(normed1, r.wq16[:, 2 * width :]))
    r.qt_s[...] = turned(r.q_s[...])
    r.kt_s[...] = turned(r.k_s[...])
    r.vt_s[...] = turned(r.v_s[...])
    key_at = iota((2 * span, span), 0)
    key_at = jnp.where(key_at < span, key_at + begin, key_at - begin)
    allowed = (key_at <= iota((2 * span, span), 1) + begin) & (key_at < length)
    r.mask_s[...] = jnp.where(allowed, 0.0, NEG)
    row_head = iota((width, span), 0) // HD
    lane_head = iota((span, width), 1) // HD

    def forward_head(h):
        rows = at(h, HD)
        mine = jnp.where(row_head == h, raised(r.qt_s[...]), 0.0)
        scores = dot(r.k_s[...], lowered(mine)) * scale + r.mask_s[...]
        expo = jnp.exp(scores - jnp.max(scores, 0, keepdims=True))
        probs = expo / jnp.sum(expo, 0, keepdims=True)
        r.p_s[h] = probs
        low_probs = lowered(probs)
        r.p16_s[:, at(h, span)] = low_probs
        r.mixt_s[rows, :] = lowered(dot(r.vt_s[rows, :], low_probs))

    loop(0, heads * 3 // 4, forward_head)
    hand_on(1)
    loop(heads * 3 // 4, heads, forward_head)
    attn = dot(turned(r.mixt_s[...]), r.wo16[...])
    hidden1 = r.h0_s[...] + attn
    r.h1_s[...] = hidden1
    sum_attn = total_of(valid_col * attn * attn)
    normed2 = lowered(hidden1 * factor_of(hidden1) * gain2)
    r.n2t_s[...] = turned(normed2)
    w_near.wait_recv()
    w_relay.wait_recv()
    for s in range(4):
        pre = dot(normed2, r.weights[s, 0])
        r.pre_s[s * span : (s + 1) * span, :] = pre
        inner = jnp.tanh(ROOT * (pre + 0.044715 * pre * pre * pre))
        r.act_s[:, s * span : (s + 1) * span] = lowered(0.5 * pre * (1.0 + inner))
    branch = dot(r.act_s[...], jnp.concatenate([r.weights[s, 1] for s in range(4)], 0))
    hidden2 = r.h1_s[...] + branch
    r.h2_s[...] = hidden2
    sum_ffn = total_of(valid_col * branch * branch)
    sum_hid = total_of(valid_col * hidden2 * hidden2)
    final = lowered(hidden2 * factor_of(hidden2) * gain3)
    r.fin_s[0:span, :] = final
    f_base = wire.take(3)
    fin = [r.fin_s.at[at(s, span)] for s in range(4)]
    fin_near = wire.make(fin[0], fin[1], f_base, here.ffn(1))
    fin_far = wire.make(fin[0], fin[2], f_base + 1, here.ffn(2))
    fin_relay = wire.make(fin[2], fin[3], f_base + 2, here.ffn(1))
    fin_far.start()
    fin_near.start()
    ended += [fin_far, fin_near, fin_relay]

    def turn_fin(s):
        r.fint_s[:, s * span : (s + 1) * span] = turned(r.fin_s[s * span : (s + 1) * span, :])

    turn_fin(0)
    if n_z > 2:
        hand_on(2)

    def prepare(i):
        if kept(n_dp):
            r.cand_t[:, at(i, span)] = turned(r.cands[at(i, span), :])
            r.cand_col[at(i, span), :] = spread(r.cand_bias[i, 0:1, :], 128)

    def columns(i, number):
        if kept(n_dp):
            return r.cand_col[slots(i, number), :]
        rows = [spread(r.cand_bias[i + j, 0:1, :], 128) for j in range(number)]
        return jnp.concatenate(rows, 0)

    def slots(i, number):
        if isinstance(i, int):
            return pl.ds(i * span, number * span)
        return pl.ds(pl.multiple_of(i * span, span), number * span)

    prepare(0)
    for copy in offer_side(0):
        copy.wait_recv()
    prepare(1)
    r.acc_s[...] = jnp.zeros_like(r.acc_s)
    for s in range(4):
        r.stat_s[s, 0:1, :] = jnp.full((1, span), NEG, FULL)
        r.stat_s[s, 1:2, :] = jnp.zeros((1, span), FULL)

    def count_in(s, i, number, group):
        lanes = slice(s * span, (s + 1) * span)
        rows = slots(i, number)
        first = s % 2 * 3 * span if kept(n_dp) else 0
        held = slice(first, first + number * span)
        logits = dot(r.cands[rows, :], r.fint_s[:, lanes])
        r.logit_s[held, :] = logits + jnp.concatenate([columns(i, number)] * (span // 128), 1)
        top = r.stat_s[s, 0:1, :]
        higher = jnp.maximum(top, jnp.max(r.logit_s[held, :], 0, keepdims=True))
        shrink = jnp.exp(top - higher)
        expo = jnp.exp(r.logit_s[held, :] - higher)
        r.stat_s[s, 0:1, :] = higher
        r.stat_s[s, 1:2, :] = r.stat_s[s, 1:2, :] * shrink + jnp.sum(expo, 0, keepdims=True)
        if kept(n_dp):
            low_expo = lowered(expo)
            r.expo_s[rows, lanes] = low_expo
            r.stat_s[s, 2 + group : 3 + group, :] = higher
            part = dot(r.cand_t[:, rows], low_expo)
        else:
            part = across(r.cands[rows, :], lowered(expo))
        r.acc_s[:, lanes] = r.acc_s[:, lanes] * shrink + part

    def count(s, group):
        first = (0, 2, n_z + 1)[group]
        number = (2, n_z - 1, n_z - 1)[group]
        if number <= 3:
            if number:
                count_in(s, first, number, group)
        else:
            loop(first, first + number, lambda i: count_in(s, i, 1, group))

    count(0, 0)
    fin_near.wait_recv()
    turn_fin(1)
    count(1, 0)
    fin_far.wait_recv()
    fin_relay.start()
    turn_fin(2)
    loop(3, n_z, hand_on)
    count(2, 0)
    fin_relay.wait_recv()
    turn_fin(3)
    count(3, 0)
    loop(2, n_z + 1, prepare)
    count(3, 1)
    count(2, 1)
    count(0, 1)
    count(1, 1)

    def prepare_side(k):
        for copy in offer_side(k):
            copy.wait_recv()
        prepare(slot(k, 1))

    loop(1, n_z, prepare_side)

    a_base = wire.take(6)

    def give(i, who):
        return Group(
            wire.make(r.acc_send.at[i], r.acc_got.at[i], a_base + 2 * i, here.ffn(who)),
            wire.make(r.mid_send.at[i], r.mid_got.at[i], a_base + 2 * i + 1, here.ffn(who)),
        )

    gives = [give(0, 1), give(1, 1), give(2, 2)]
    ended += gives

    def fill(i, s):
        r.acc_send[i] = lowered(r.acc_s[:, s * span : (s + 1) * span])
        r.mid_send[i] = r.stat_s[s]
        gives[i].start()

    def merge(s, i):
        gives[i].wait_recv()
        lanes = slice(s * span, (s + 1) * span)
        top, other = r.stat_s[s, 0:1, :], r.mid_got[i, 0:1, :]
        higher = jnp.maximum(top, other)
        left, right = jnp.exp(top - higher), jnp.exp(other - higher)
        r.acc_s[:, lanes] = r.acc_s[:, lanes] * left + raised(r.acc_got[i]) * right
        r.stat_s[s, 0:1, :] = higher
        r.stat_s[s, 1:2, :] = r.stat_s[s, 1:2, :] * left + r.mid_got[i, 1:2, :] * right

    count(3, 2)
    fill(0, 3)
    count(2, 2)
    merge(2, 0)
    fill(2, 2)
    count(1, 2)
    fill(1, 1)
    count(0, 2)
    merge(0, 1)
    for s in range(4):
        rows = slice(s * span, (s + 1) * span)
        pre = r.pre_s[rows, :]
        inner = jnp.tanh(ROOT * (pre + 0.044715 * pre * pre * pre))
        r.pre_s[rows, :] = 0.5 * (1.0 + inner) + 0.5 * pre * (1.0 - inner * inner) * (
            ROOT * (1.0 + 3.0 * 0.044715 * pre * pre)
        )
    merge(0, 2)
    total = r.stat_s[0, 1:2, :]
    log_total = r.stat_s[0, 0:1, :] + jnp.log(total)
    r.tot_s[0] = jnp.broadcast_to(jnp.where(valid_lane > 0, log_total, -NEG), (8, span))
    for copy in (
        all_passes(0, 0),
        all_passes(0, 1),
        all_passes(2, 2),
        to_far(len(cuts)),
        to_near(len(cuts)),
        relay(len(cuts)),
    ):
        copy.wait_send()

    t_base = wire.take(1)

    def to_members(ref, number):
        three = ref.at[pl.ds(1, 3)]
        return Joined(
            [wire.make(ref.at[0], ref.at[s], number, here.ffn(s)) for s in (1, 2, 3)],
            wire.make(three, three, number, here.side()),
        )

    tell = to_members(r.tot_s, t_base)
    tell.start()
    ended.append(tell)
    if not kept(n_dp):
        r.cand_t[...] = turned(r.cands[0:span, :])
    target_t = raised(r.cand_t[:, 0:span])
    positive = (
        jnp.sum(raised(r.fint_s[:, :span]) * target_t, 0, keepdims=True) - r.bias_s[0:1, :]
    )
    loss = total_of(valid_lane * (log_total - positive))
    grad_final = ((r.acc_s[:, 0:span] / total - target_t) * valid_lane).T

    grad_h2, gain_grad3 = rms_back(r.h2_s[...], gain3, grad_final)
    up = lowered(grad_h2)
    r.h2_s[...] = grad_h2
    for s in (1, 3, 2, 0):
        lanes = slice(s * span, (s + 1) * span)
        r.gf_s[s, 1] = across(r.act_s[:, lanes], up)
        grad_act = against(up, r.weights[s, 1])
        grad_pre = lowered(grad_act * r.pre_s[s * span : (s + 1) * span, :])
        r.gf_s[s, 0] = dot(r.n2t_s[...], grad_pre)
        r.act_s[:, lanes] = grad_pre
    for i, s in enumerate((1, 3)):
        for j in range(2):
            r.fnear_send[i, j * width : (j + 1) * width, :] = lowered(r.gf_s[s, j])
    all_asks = wire.make(r.req.at[others], r.req.at[others], q_base, here.side())
    for copy in (all_asks, all_replies(), all_biases(), w_far, w_near, w_relay):
        copy.wait_send()
    def end_offers(j):
        for h in range(2):
            pl.when(has_up & (here.z >= j))(lambda: send_up(j)[h].wait_send())
            pl.when(has_down & (here.z + j < n_z))(lambda: send_down(j)[h].wait_send())
            offer_side(j)[h].wait_send()

    each(0, n_z, end_offers)
    for copy in ended:
        copy.wait_send()
    ended.clear()
    wire.renew()
    e_base = wire.take(6)
    f_near = wire.make(r.fnear_send, r.fnear_got, e_base, here.ffn(1))
    f_far = wire.make(r.ffar_send, r.ffar_got, e_base + 1, here.ffn(2))
    s_near = wire.make(r.snear_send, r.snear_got, e_base + 2, here.ffn(1))
    s_far = wire.make(r.sfar_send, r.sfar_got, e_base + 3, here.ffn(2))
    e_near = wire.make(r.enear_send, r.enear_got, e_base + 4, here.ffn(1))
    e_far = wire.make(r.efar_send, r.efar_got, e_base + 5, here.ffn(2))
    ended += [f_near, f_far, s_near, s_far, e_near, e_far]
    f_near.start()

    grad_normed2 = against(
        r.act_s[...], jnp.concatenate([r.weights[s, 0] for s in range(4)], 1)
    )
    grad_h1_norm, gain_grad2 = rms_back(r.h1_s[...], gain2, grad_normed2)
    grad_h1 = r.h2_s[...] + grad_h1_norm
    r.h1_s[...] = grad_h1
    tell.wait_recv()
    if kept(n_dp):
        for s in range(4):
            for group in range(3):
                level = r.stat_s[s, 2 + group : 3 + group, :] - r.tot_s[s, 0:1, :]
                r.scale_s[group : group + 1, s * span : (s + 1) * span] = jnp.exp(level)
    side_base, line_base = wire.take(n_z), wire.take(n_z)

    def cand_side(k):
        return wire.make(r.cand_send.at[k], r.side_got.at[k], side_base + k, here.side())

    def cand_line(k):
        return wire.make(r.cand_send.at[k], r.line_got.at[k], line_base + k, here.down(k))

    def cand_grad(i):
        if kept(n_dp):
            group = jnp.where(i < 2, 0, jnp.where(i <= n_z, 1, 2))
            share_of = r.scale_s[pl.ds(group, 1), :]
            weights = raised(r.expo_s[at(i, span), :]) * share_of
            return dot(lowered(weights), r.fin_s[...])
        column = jnp.concatenate([columns(i, 1)] * (4 * span // 128), 1)
        level = jnp.concatenate([r.tot_s[s, 0:1, :] for s in range(4)], 1)
        logits = dot(r.cands[at(i, span), :], r.fint_s[...]) + column
        return dot(lowered(jnp.exp(logits - level)), r.fin_s[...])

    def slot_at(k, ky):
        return jnp.where(k == 0, ky, 1 + k + ky * (n_z - 1))

    def side_step(k):
        r.cand_send[k] = lowered(cand_grad(slot_at(k, 1)))
        cand_side(k).start()

    def line_step(k):
        grad = cand_grad(slot_at(k, 0))
        cand_side(k).wait_send()
        cand_side(k).wait_recv()
        r.cand_send[k] = lowered(grad + raised(r.side_got[k]))
        cand_line(k).start()

    middle = n_z // 2
    side_step(middle)
    loop(1, middle, side_step)
    loop(middle + 1, n_z, side_step)
    if middle:
        side_step(0)

    f_near.wait_recv()
    for j in range(2):
        rows = slice(j * width, (j + 1) * width)
        r.ffar_send[rows, :] = lowered(r.gf_s[2, j] + raised(r.fnear_got[1, rows, :]))
    f_far.start()

    attn_up = lowered(grad_h1)
    r.acc_s[:, 3 * width :] = dot(r.mixt_s[...], attn_up)
    grad_mixed = lowered(against(attn_up, r.wo16[...]))
    grad_mixed_f = raised(grad_mixed)
    r.mixt_s[...] = turned(grad_mixed)
    for h in range(heads):
        r.stack_s[h * span : (h + 1) * span, :] = lowered(
            jnp.where(lane_head == h, grad_mixed_f, 0.0)
        )
    r.kv_s[...] = dot(r.p16_s[...], r.stack_s[...])
    r.logit_s[span : 2 * span, :] = r.kv_s[span:, :]
    r.own_s[...] = r.kv_s[0:span, :]
    k_base = wire.take(2)

    def lend(i):
        rows = at(i, span)
        return wire.make(r.logit_s.at[rows], r.kv_got.at[rows], k_base + i, here.ffn(1))

    lend_k, lend_v = lend(0), lend(1)
    ended += [lend_k, lend_v]
    lend_v.start()

    def backward_head(h):
        rows = at(h, HD)
        mine = jnp.where(row_head == h, raised(r.mixt_s[...]), 0.0)
        grad_probs = dot(r.v_s[...], lowered(mine))
        probs = r.p_s[h]
        inner = jnp.sum(probs * grad_probs, 0, keepdims=True)
        grad_scores = lowered(probs * (grad_probs - inner))
        r.p16_s[:, at(h, span)] = grad_scores
        r.dq_s[rows, :] = dot(r.kt_s[rows, :], grad_scores) * scale

    loop(0, heads // 2, backward_head)
    if middle:
        line_step(middle)
    strip = span // 4
    halves = (jnp.where(half == 0, 1.0, 0.0), jnp.where(half == 1, 1.0, 0.0))

    def strip_at(s):
        return pl.ds(pl.multiple_of(here.member[s] * strip, strip), strip)

    def early_pieces(s):
        yield 0, r.acc_s[strip_at(s), 3 * width :]
        yield strip, r.acc_s[strip_at(s), 2 * width : 3 * width]

    def pieces(s):
        for j in range(2):
            yield j * strip, r.acc_s[strip_at(s), j * width : (j + 1) * width]
        for u in range(2):
            yield (2 + u) * strip, r.h0_s[strip_at(s), :] * halves[u]

    lend_v.wait_recv()
    r.gv_s[...] = lowered(r.own_s[...] + r.kv_got[span:, :])
    r.acc_s[:, 2 * width : 3 * width] = across(r.n1_s[...], r.gv_s[...])
    for i, s in enumerate((1, 3)):
        for first, value in early_pieces(s):
            r.enear_send[i, first : first + strip, :] = lowered(value)
    e_near.start()
    loop(heads // 2, heads, backward_head)
    loop(1, middle, line_step)
    e_near.wait_recv()
    for first, value in early_pieces(2):
        got = raised(r.enear_got[1, first : first + strip, :])
        r.efar_send[first : first + strip, :] = lowered(value + got)
    e_far.start()
    queries = raised(r.q_s[...])
    for h in range(heads):
        r.stack_s[h * span : (h + 1) * span, :] = lowered(jnp.where(lane_head == h, queries, 0.0))
    r.kv_s[...] = dot(r.p16_s[...], r.stack_s[...]) * scale
    r.logit_s[0:span, :] = r.kv_s[span:, :]
    lend_k.start()
    loop(middle + 1, n_z, line_step)
    r.h2_s[...] = cand_grad(0)
    ffn_part, strip_part = parts(n_dp, span, width)
    f_far.wait_recv()
    for j in range(2):
        rows = slice(j * width, (j + 1) * width)
        r.pre_s[rows, :] = (
            r.gf_s[0, j] + raised(r.fnear_got[0, rows, :]) + raised(r.ffar_got[rows, :])
        )
    e_far.wait_recv()
    early_rows = 2 * width + 2 * strip
    for first, value in early_pieces(0):
        rows = slice(first, first + strip)
        r.pre_s[2 * width + first : 2 * width + first + strip, :] = (
            value + raised(r.enear_got[0, rows, :]) + raised(r.efar_got[rows, :])
        )
    if n_dp * ffn_part > early_rows:
        r.pre_s[early_rows : n_dp * ffn_part, :] = jnp.zeros(
            (n_dp * ffn_part - early_rows, width), FULL
        )
    m_base = wire.take(2 + 2 * n_z)

    def sum_dp(source, size, side_send, side_got, line_send, line_got, base):
        def rows_of(k, y):
            return at(y * n_z + lax.rem(here.z + k, n_z), size)

        across_y = wire.make(side_send, side_got, base, here.side())

        def along(k):
            return wire.make(line_send.at[k], line_got.at[k], base + 1 + k, here.up(k))

        def begin_side():
            def fill_side(k):
                side_send[at(k, size), :] = lowered(source[rows_of(k, 1 - here.y), :])

            loop(0, n_z, fill_side)
            across_y.start()

        def begin_line():
            across_y.wait_recv()

            def fill_line(k):
                line_send[k] = lowered(
                    source[rows_of(k, here.y), :] + raised(side_got[at(k, size), :])
                )
                along(k).start()

            loop(1, n_z, fill_line)

        def finish():
            value = source[rows_of(0, here.y), :] + raised(side_got[0:size, :])
            for k in range(1, n_z):
                along(k).wait_recv()
                value = value + raised(line_got[k])
            return value

        def end():
            across_y.wait_send()
            each(1, n_z, lambda k: along(k).wait_send())

        return begin_side, begin_line, finish, end

    ffn_side, ffn_line, ffn_finish, ffn_end = sum_dp(
        r.pre_s,
        ffn_part,
        r.fside_send,
        r.fside_got,
        r.fline_send,
        r.fline_got,
        m_base,
    )
    strip_side, strip_line, strip_finish, strip_end = sum_dp(
        r.strip_s,
        strip_part,
        r.sside_send,
        r.sside_got,
        r.sline_send,
        r.sline_got,
        m_base + 1 + n_z,
    )
    ffn_side()


    grad_q = lowered(r.dq_s[...].T)
    lend_k.wait_recv()
    grad_qk = jnp.concatenate(
        [grad_q, lowered(r.kv_s[0:span, :] + r.kv_got[0:span, :])],
        1,
    )
    grad_united = jnp.concatenate([grad_qk, r.gv_s[...]], 1)
    grad_h0_norm, gain_grad1 = rms_back(r.h0_s[...], gain1, against(grad_united, r.wq16[...]))
    grad_h0 = r.h1_s[...] + grad_h0_norm
    r.h0_s[...] = grad_h0

    r.acc_s[:, : 2 * width] = across(r.n1_s[...], grad_qk)

    for i, s in enumerate((1, 3)):
        for first, value in pieces(s):
            r.snear_send[i, first : first + strip, :] = lowered(value)
    s_near.start()

    o_base = wire.take(6)

    def chunk(s, column):
        return r.found.at[at(2 * s + column, span)]

    def row_copies(column):
        return (
            wire.make(chunk(0, column), chunk(2, column), o_base + 3 * column, here.ffn(2)),
            wire.make(chunk(0, column), chunk(1, column), o_base + 3 * column + 1, here.ffn(1)),
            wire.make(chunk(2, column), chunk(3, column), o_base + 3 * column + 2, here.ffn(1)),
        )

    in_far, in_near, in_relay = row_copies(0)
    out_far, out_near, out_relay = row_copies(1)
    ended += [in_far, in_near, in_relay, out_far, out_near, out_relay]
    r.found[0:span, :] = lowered(grad_h0)
    in_far.start()
    in_near.start()

    lane8 = iota((1, width), 1)
    row8 = iota((8, width), 0)
    stats = jnp.where(lane8 == 0, loss, 0.0)
    for i, number in enumerate((total_of(valid_lane), sum_hid, sum_attn, sum_ffn)):
        stats = jnp.where(lane8 == i + 1, number, stats)
    small = jnp.where(row8 == 0, gain_grad1, 0.0)
    small = jnp.where(row8 == 1, gain_grad2, small)
    small = jnp.where(row8 == 2, gain_grad3, small)
    r.small[0, 0] = jnp.where(row8 == 3, stats, small)
    l_base = wire.take(1)

    tell_small = to_members(r.small.at[0], l_base)
    tell_small.start()
    ended.append(tell_small)

    s_near.wait_recv()
    for first, value in pieces(2):
        got = raised(r.snear_got[1, first : first + strip, :])
        r.sfar_send[first : first + strip, :] = lowered(value + got)
    s_far.start()
    cand_side(0).wait_send()
    cand_side(0).wait_recv()
    r.own_s[...] = (
        r.h2_s[...] + raised(r.side_got[0]) - valid_col * raised(r.fin_s[0:span, :])
    )

    def add_line(k):
        cand_line(k).wait_recv()
        r.own_s[...] = r.own_s[...] + raised(r.line_got[k])

    loop(1, n_z, add_line)
    r.found[span : 2 * span, :] = lowered(r.own_s[...])
    out_far.start()
    out_near.start()

    ffn_line()

    in_far.wait_recv()
    in_relay.start()

    s_far.wait_recv()
    for first, value in pieces(0):
        rows = slice(first, first + strip)
        r.strip_s[rows, :] = (
            value + raised(r.snear_got[0, rows, :]) + raised(r.sfar_got[rows, :])
        )
    late_rows = 4 * strip
    if n_dp * strip_part > late_rows:
        r.strip_s[late_rows:, :] = jnp.zeros((n_dp * strip_part - late_rows, width), FULL)
    strip_side()

    order = here.y * n_z + here.z
    v_base = wire.take(4)

    def gather_dp(ref, size, base):
        own_part = ref.at[at(order, size)]
        own_column = ref.at[at(here.y, n_z * size)]

        def line(k):
            return wire.make(own_part, own_part, base, here.up(k))

        others = ref.at[pl.ds(0, (n_z - 1) * size)]
        lines = Joined(
            [line(k) for k in range(1, n_z)], wire.make(others, others, base, here.side())
        )
        return lines, wire.make(own_column, own_column, base + 1, here.side())

    ffn_all, ffn_all_side = gather_dp(r.whole_f, ffn_part, v_base)
    strip_all, strip_all_side = gather_dp(r.whole_t, strip_part, v_base + 2)
    ended += [ffn_all, strip_all, ffn_all_side, strip_all_side]
    mine = ffn_finish()
    squares = total_of(mine * mine)
    r.whole_f[at(order, ffn_part), :] = lowered(mine)
    ffn_all.start()
    tell_small.wait_recv()
    r.small[1, 0] = (r.small[0, 0] + r.small[0, 1]) + (r.small[0, 2] + r.small[0, 3])
    h_base = wire.take(2)

    def share(row, k, number):
        return wire.make(r.small.at[row, 0], r.small_dp.at[row // 4, d], number, here.ahead(k))

    def all_shares(row, number):
        others = r.small_dp.at[row // 4, pl.ds(0, n_dp - 1)]
        return wire.make(others, others, number, here.side())

    each(1, n_dp, lambda k: share(1, k, h_base).start())
    r.small_dp[0, d] = r.small[1, 0]

    out_far.wait_recv()
    out_relay.start()

    strip_line()

    in_near.wait_recv()
    in_relay.wait_recv()
    out_near.wait_recv()
    out_relay.wait_recv()

    g_base = wire.take(1)

    def outgoing(k):
        return pl.ds(pl.multiple_of(8 * span + k * cap, cap), cap)

    def ship(k):
        return wire.make(
            r.found.at[outgoing(k)], r.incoming.at[at(k, cap)], g_base, here.ahead(k)
        )

    def all_rows():
        rows = pl.ds(8 * span + cap, (n_dp - 1) * cap)
        landed = r.incoming.at[pl.ds(cap, (n_dp - 1) * cap)]
        return wire.make(r.found.at[rows], landed, g_base, here.side())

    places = pl.ds(8 * span, filled)
    if kept(n_dp):
        r.found[places, :] = lowered(dot(r.pick_s[...], r.found[0 : 8 * span, :]))
    else:
        marks_to = build_marks()

        def choose(k):
            chosen = picks(marks_to, k)
            r.found[outgoing(k), :] = lowered(dot(chosen, r.found[0 : 8 * span, :]))

        loop(0, n_dp, choose)
    ship(n_z).start()
    r.incoming[0:cap, :] = r.found[outgoing(0), :]

    mine = strip_finish()
    squares = squares + total_of(mine * mine)
    r.whole_t[at(order, strip_part), :] = lowered(mine)
    strip_all.start()
    each(1, n_z, lambda k: ship(k).start())
    each(n_z + 1, n_dp, lambda k: ship(k).start())

    several = min(n_dp, 8)

    def own_marks(g):
        for k in range(several):
            r.owned[:, k * 128 : (k + 1) * 128] = lowered(
                one_hot_columns(raised(r.asked[g * several + k]), rows_dev)
            )

    if n_dp == several:
        own_marks(0)

    ffn_all.wait_recv()
    ffn_all_side.start()

    strip_all.wait_recv()
    strip_all_side.start()
    for copy in ended:
        copy.wait_send()
    ended.clear()

    def end_line(k):
        cand_line(k).wait_send()

    each(1, n_z, end_line)

    ffn_end()
    strip_end()

    strip_all_side.wait_recv()
    c_base = wire.take(6)

    def spread_strips(first, rows, base):
        part = pl.ds(first, rows)
        mine_at, far_at = r.strips.at[f, part], r.strips.at[far, part]
        copies = (
            wire.make(mine_at, mine_at, base, here.ffn(2)),
            wire.make(mine_at, mine_at, base + 1, here.ffn(1)),
            wire.make(far_at, far_at, base + 2, here.ffn(1)),
        )
        ended.extend(copies)
        return copies

    r.strips[f, 2 * strip :, :] = r.whole_t[0:late_rows, :]
    strip_far, strip_near, strip_relay = spread_strips(2 * strip, late_rows, c_base + 3)
    strip_far.start()
    strip_near.start()
    ffn_all_side.wait_recv()
    outs = [
        pltpu.make_async_copy(src, dst, r.load_sems.at[i])
        for i, (src, dst) in enumerate(
            (
                (r.whole_f.at[pl.ds(0, 2 * width)], r.ffn_out),
                (r.table_grad, r.table_out),
            )
        )
    ]

    def strip_out(s):
        place = here.member[s]
        return pltpu.make_async_copy(
            r.strips.at[place], r.strips_out.at[place], r.load_sems.at[2 + s]
        )

    outs[0].start()
    r.strips[f, 0 : 2 * strip, :] = r.whole_f[2 * width : early_rows, :]
    early_far, early_near, early_relay = spread_strips(0, 2 * strip, c_base)
    early_far.start()
    early_near.start()

    all_rows().wait_recv()

    if n_dp == several:
        for first in range(0, rows_dev, 208):
            rows = slice(first, min(first + 208, rows_dev))
            value = dot(r.owned[rows, :], r.incoming[...])
            r.table_grad[rows, :] = value
            squares = squares + total_of(value * value)
    else:
        r.table_grad[...] = jnp.zeros((rows_dev, width), FULL)
        r.padded_in[...] = jnp.zeros_like(r.padded_in)

        def add_rows(g):
            own_marks(g)
            for k in range(several):
                r.padded_in[k * 128 : k * 128 + cap, :] = r.incoming[
                    at(g * several + k, cap), :
                ]
            r.table_grad[...] = r.table_grad[...] + dot(r.owned[...], r.padded_in[...])

        loop(0, n_dp // several, add_rows)
        table_grad = r.table_grad[...]
        squares = squares + total_of(table_grad * table_grad)
    outs[1].start()

    r.small[3, 0] = jnp.broadcast_to(squares, (8, width))
    tell_norm = to_members(r.small.at[3], wire.take(1))
    tell_norm.start()
    ended.append(tell_norm)
    all_shares(1, h_base).wait_recv()
    tell_norm.wait_recv()
    r.small[4, 0] = (r.small[3, 0] + r.small[3, 1]) + (r.small[3, 2] + r.small[3, 3])

    each(1, n_dp, lambda k: share(4, k, h_base + 1).start())
    r.small_dp[1, d] = r.small[4, 0]
    early_far.wait_recv()
    early_relay.start()
    early_near.wait_recv()
    strip_near.wait_recv()
    strip_out(0).start()
    strip_out(1).start()
    strip_far.wait_recv()
    strip_relay.start()
    strip_out(2).start()
    all_shares(4, h_base + 1).wait_recv()
    totals, squares = r.small_dp[0, 0], r.small_dp[1, 0]
    for k in range(1, n_dp):
        totals = totals + r.small_dp[0, k]
        squares = squares + r.small_dp[1, k]
    gains = jnp.where(row8 < 3, totals, 0.0)
    norm = jnp.sqrt(squares + total_of(gains * gains))
    r.sums[...] = jnp.where(row8 == 4, norm, totals)

    all_rows().wait_send()
    all_shares(1, h_base).wait_send()
    all_shares(4, h_base + 1).wait_send()


    early_relay.wait_recv()
    strip_relay.wait_recv()
    strip_out(3).start()
    for copy in outs + [strip_out(s) for s in range(4)]:
        copy.wait()
    for copy in ended:
        copy.wait_send()
    assert wire.arrived <= r.recv_sems.shape[0]
    assert wire.most <= r.send_sems.shape[0]


def step(n_dp, cap, owner, row, lengths, count, table, wq, wo, w_in, w_back, gains, positions):
    rows_dev, width = table.shape
    span = owner.shape[1] // 4
    heads, n_z = width // HD, n_dp // 2
    shapes = plan(n_dp, cap, rows_dev, span, width, heads)
    names = INPUTS + OUTPUTS + list(shapes) + ["load_sems", "send_sems", "recv_sems"]
    vmem = pl.BlockSpec(memory_space=pltpu.VMEM)
    smem = pl.BlockSpec(memory_space=pltpu.SMEM)
    rest = pl.BlockSpec(memory_space=pl.ANY)
    sends, arrivals = 9 * n_z + 23, 20 * n_z + 48

    def out(kind, *shape):
        return jax.ShapeDtypeStruct(shape, kind)

    return pl.pallas_call(
        functools.partial(step_kernel, n_dp, cap, names),
        out_shape=(
            out(FULL, rows_dev, width),
            out(LOW, 2 * width, width),
            out(LOW, 4, 6 * span // 4, width),
            out(FULL, 8, width),
        ),
        in_specs=[vmem, vmem, smem, vmem, rest, rest, rest, rest, rest, vmem, rest],
        out_specs=(rest, rest, rest, vmem),
        scratch_shapes=[pltpu.VMEM(shape[:-1], shape[-1]) for shape in shapes.values()]
        + [
            pltpu.SemaphoreType.DMA((6,)),
            pltpu.SemaphoreType.DMA((sends,)),
            pltpu.SemaphoreType.DMA((arrivals,)),
        ],
        compiler_params=pltpu.CompilerParams(
            collective_id=0,
            has_side_effects=True,
            vmem_limit_bytes=63 * MIB,
        ),
        name="step",
    )(owner, row, lengths, count, table, wq, wo, w_in, w_back, gains, positions)


STATES = 21
GAINS = 5


def jobs(rows_dev, width):
    quarter = -(-rows_dev // 32) * 8
    result = []
    for first in range(0, rows_dev, quarter):
        result.append((0, first, min(quarter, rows_dev - first)))
    return result + [(3, 0, width), (4, 0, width), (1, 0, width), (6, 0, 2 * width), (2, 0, width)]


def update_kernel(rows_dev, table_grad, ffn_grad, strips, sums, *refs):
    ins, refs = refs[:STATES], refs[STATES:]
    loss_out, rms_out, norm_out = refs[:3]
    outs, refs = refs[3 : 3 + STATES], refs[3 + STATES :]
    held, made, refs = refs[:18], refs[18:36], refs[36:]
    table_s, ffn_s, strips_s, grad_sems, in_sems, out_sems = refs
    width = sums.shape[1]
    work = jobs(rows_dev, width)

    def kept_at(which, i):
        return 3 * (which if which < GAINS else which - 1) + i

    def moves(number):
        which, first, rows = work[number]
        part = pl.ds(first, rows)
        here = [kept_at(which, i) for i in range(3)]
        return (
            [
                pltpu.make_async_copy(
                    ins[3 * which + i].at[part],
                    held[here[i]].at[part],
                    in_sems.at[number, i],
                )
                for i in range(3)
            ],
            [
                pltpu.make_async_copy(
                    made[here[i]].at[part],
                    outs[3 * which + i].at[part],
                    out_sems.at[number, i],
                )
                for i in range(3)
            ],
        )

    grads = [
        pltpu.make_async_copy(table_grad, table_s, grad_sems.at[0]),
        pltpu.make_async_copy(ffn_grad, ffn_s, grad_sems.at[1]),
        pltpu.make_async_copy(strips, strips_s, grad_sems.at[2]),
    ]
    grads[0].start()
    for number in range(len(work)):
        for i, copy in enumerate(moves(number)[0]):
            copy.start(priority=(number + i) % 2)
        if number == 1:
            grads[1].start()
            grads[2].start()
    norm = sums[4:5, 0:1]
    factor = CLIP / jnp.maximum(norm, CLIP)
    corr_one = 1.0 - BETA_ONE**STEP
    corr_two = 1.0 - BETA_TWO**STEP

    def adam(which, rows, lanes, grad, rate):
        if which == GAINS:
            source, target = ins[3 * which : 3 * which + 3], outs[3 * which : 3 * which + 3]
        else:
            first = kept_at(which, 0)
            source, target = held[first : first + 3], made[first : first + 3]
        weight, moment, second = (ref[rows, lanes] for ref in source)
        clipped = raised(grad) * factor
        moment = BETA_ONE * moment + (1.0 - BETA_ONE) * clipped
        second = BETA_TWO * second + (1.0 - BETA_TWO) * clipped * clipped
        target[0][rows, lanes] = weight - rate * (
            moment / corr_one / (jnp.sqrt(second / corr_two) + ADAM_EPS) + DECAY * weight
        )
        target[1][rows, lanes] = moment
        target[2][rows, lanes] = second

    every = slice(None)
    strip = strips_s.shape[1] // 6
    waited = set()

    def need(i):
        if i not in waited:
            waited.add(i)
            grads[i].wait()

    for number, (which, first, rows) in enumerate(work):
        copies_in, copies_out = moves(number)
        need(0 if which == 0 else 1 if which in (3, 4) else 2)
        for copy in copies_in:
            copy.wait()
        if which == 0:
            part = slice(first, first + rows)
            adam(0, part, every, table_s[part, :], LEARN)
        elif which in (3, 4):
            start = (which - 3) * width
            adam(which, every, every, ffn_s[start : start + width, :], LEARN)
        for m in range(4):
            at_rows = slice(m * strip, (m + 1) * strip)
            if which == 1:
                for j, i in enumerate((2, 3, 1)):
                    lanes = slice(j * width, (j + 1) * width)
                    grad = strips_s[m, i * strip : (i + 1) * strip, :]
                    adam(1, at_rows, lanes, grad, LEARN)
            elif which == 2:
                adam(2, at_rows, every, strips_s[m, 0:strip, :], LEARN)
            elif which == 6:
                for u in range(2):
                    at_rows = slice((4 * u + m) * strip, (4 * u + m + 1) * strip)
                    grad = strips_s[m, (4 + u) * strip : (5 + u) * strip, :]
                    adam(6, at_rows, every, grad, LEARN)
        for i, copy in enumerate(copies_out):
            copy.start(priority=(number + i) % 2)
    adam(GAINS, every, every, sums[0:3, :], GAIN_LEARN)
    stats = sums[3:4, :]
    roots = jnp.sqrt(stats / (stats[:, 1:2] * float(width)))

    def one(row, i):
        return jnp.sum(jnp.where(iota(row.shape, 1) == i, row, 0.0))

    loss_out[0] = one(stats, 0)
    loss_out[1] = one(stats, 1)
    for i in range(3):
        rms_out[i] = one(roots, 2 + i)
    norm_out[0] = one(sums[4:5, :], 0)
    for number in range(len(work)):
        for copy in moves(number)[1]:
            copy.wait()


def update(table_grad, ffn_grad, strips, sums, states):
    vmem = pl.BlockSpec(memory_space=pltpu.VMEM)
    smem = pl.BlockSpec(memory_space=pltpu.SMEM)
    rest = pl.BlockSpec(memory_space=pl.ANY)
    places = [vmem if i // 3 == GAINS else rest for i in range(STATES)]
    room = [pltpu.VMEM(a.shape, FULL) for i, a in enumerate(states) if i // 3 != GAINS]
    rows_dev, width = table_grad.shape
    number = len(jobs(rows_dev, width))
    return pl.pallas_call(
        functools.partial(update_kernel, rows_dev),
        out_shape=tuple(jax.ShapeDtypeStruct((n,), FULL) for n in (2, 3, 1))
        + tuple(jax.ShapeDtypeStruct(a.shape, FULL) for a in states),
        in_specs=[rest] * 3 + [vmem] + places,
        out_specs=[smem] * 3 + places,
        scratch_shapes=room
        + room
        + [pltpu.VMEM(a.shape, a.dtype) for a in (table_grad, ffn_grad, strips)]
        + [
            pltpu.SemaphoreType.DMA((3,)),
            pltpu.SemaphoreType.DMA((number, 3)),
            pltpu.SemaphoreType.DMA((number, 3)),
        ],
        compiler_params=pltpu.CompilerParams(vmem_limit_bytes=63 * MIB),
        name="update",
    )(table_grad, ffn_grad, strips, sums, *states)


def shards(
    item_owner,
    item_row,
    lengths,
    log_count,
    item_table,
    table_mom,
    table_sec,
    qkv_weight,
    qkv_mom,
    qkv_sec,
    out_weight,
    out_mom,
    out_sec,
    ffn_in,
    ffn_in_mom,
    ffn_in_sec,
    ffn_back,
    ffn_back_mom,
    ffn_back_sec,
    norm_gains,
    gains_mom,
    gains_sec,
    positions,
    positions_mom,
    positions_sec,
):
    n_dp = lax.axis_size("dp")
    tokens = item_owner.shape[0]
    cap = max(2, 4 * tokens // (n_dp * lax.axis_size("ffn")))
    table_grad, ffn_grad, strips, sums = step(
        n_dp,
        cap,
        item_owner.T,
        item_row.T,
        lengths,
        log_count,
        item_table,
        qkv_weight,
        out_weight,
        ffn_in,
        ffn_back,
        norm_gains,
        positions,
    )
    return update(
        table_grad,
        ffn_grad,
        strips,
        sums,
        (
            item_table,
            table_mom,
            table_sec,
            qkv_weight,
            qkv_mom,
            qkv_sec,
            out_weight,
            out_mom,
            out_sec,
            ffn_in,
            ffn_in_mom,
            ffn_in_sec,
            ffn_back,
            ffn_back_mom,
            ffn_back_sec,
            norm_gains,
            gains_mom,
            gains_sec,
            positions,
            positions_mom,
            positions_sec,
        ),
    )


def solution(mesh):
    whole, rows, table = P(), P("dp", None), P(("dp", "ffn"), None)
    wide, tall = P(None, "ffn"), P("ffn", None)
    states = (table,) * 3 + (whole,) * 6 + (wide,) * 3 + (tall,) * 3 + (whole,) * 6
    return jax.shard_map(
        shards,
        mesh=mesh,
        in_specs=(rows, rows, P("dp"), P(("dp", "ffn"))) + states,
        out_specs=(whole,) * 3 + states,
        check_vma=False,
    )
```
